128 devices in a mesh: member: 8 (over z_hi, x), space: 16 (over z_lo, y, core).
Axes of the slice: x: 4, y: 4, z: 4 (z_hi: 2, z_lo: 2; z = z_hi * 2 + z_lo), core: 2. Of those that a mesh axis runs over, the one named last changes fastest.
Arguments:
- ens: bfloat16 [16, 36, 256, 1440], P('member', None, 'space'), may hold values from -6 to 6
- truth: bfloat16 [36, 256, 1440], P(None, 'space'), may hold values from -6 to 6
- legendre: bfloat16 [256, 128, 721], P('space'), may hold values from -0.375 to 0.375
- orders: int32 [128], replicated, may hold values from 0 to 720, as said below
Outputs:
- grid_score: float32 [36, 16, 16], P(None, 'space', 'member')
- grid_grad: bfloat16 [16, 36, 16, 16, 1440], P(None, None, 'space', 'member')
- spec_score: float32 [128, 36, 721], P('space')
- spec_grad: bfloat16 [16, 36, 256, 1440], P('member', None, 'space')
The draws below stay inside these ranges and needn't reach their ends.
Inputs may be any that keep to these rules, and one draw needn't show every extreme that they name: The 128 listed orders are distinct; 0 and 720 are always among them.
All inputs are finite; a program needn't handle non-finite values.
Results may differ from the reference program's by a relative error of at most 0.024.
Values may be sent and summed in bfloat16 or wider, within the bound.
No kernel may reach another device: no remote copies, remote signals or barrier semaphores. Data moves between devices by JAX's collectives and lax.ppermute only.
A program may use at most 192 MiB of HBM per device.

```python
import math
import jax
import jax.numpy as jnp
from jax import lax

VARS = 36
NLON = 1440
LDEG = 721
MMAX = 721
LAT_DEV = 16
ENS = 16
NLAT = 256
MW = 128
N_SPACE = 16


def draw_orders(key, part):
    key = jax.random.fold_in(key, 7)
    key_pick, key_order = jax.random.split(key)
    inner_orders = jax.random.permutation(key_pick, MMAX - 2)[:MW - 2].astype(jnp.int32) + 1
    listed = jnp.concatenate([jnp.array([0, MMAX - 1], dtype=jnp.int32), inner_orders])
    return listed[jax.random.permutation(key_order, MW)]


def levels(key, shape, shards, smallest, top_value):
    def one(axis_at, blocks):
        draws = jax.random.uniform(jax.random.fold_in(jax.random.fold_in(key, 6), axis_at), (blocks,), jnp.float32, smallest / len(shards), top_value / len(shards))
        return jnp.repeat(jnp.exp(draws), shape[axis_at] // blocks).reshape((-1,) + (1,) * (len(shape) - axis_at - 1))

    loudness = one(*shards[0])
    for cut in shards[1:]:
        loudness = loudness * one(*cut)
    return loudness


def bell_draw(stream_key, extent, scale, most, shards=(), held_as=jnp.bfloat16):
    level = levels(stream_key, extent, shards, -0.22, 0.18) if shards else 1.0
    values = jax.random.normal(stream_key, extent, jnp.float32) * scale * level
    return jnp.minimum(jnp.maximum(values, -most), most).astype(held_as)


def setup_inputs(seed: int = 0) -> dict:
    key_list = jax.random.split(jax.random.key(seed), 5)
    return {
        "ens": bell_draw(key_list[0], (ENS, VARS, NLAT, NLON), 1.0, 6.0, ((0, 8), (2, 16))),
        "truth": bell_draw(key_list[1], (VARS, NLAT, NLON), 1.0, 6.0, ((1, 16),)),
        "legendre": bell_draw(key_list[2], (NLAT, MW, LDEG), NLAT ** -0.5, 0.375, ((0, 16),)),
        "orders": draw_orders(jax.random.fold_in(key_list[4], 71), 0),
    }


FAIR_GAP = 0.05
SOFTEN = 0.1

def fourier_table(orders, lon_count):
    longitude = jnp.arange(lon_count, dtype=jnp.int32)
    phase_index = longitude[:, None] * orders[None, :] % lon_count
    angles = phase_index.astype(jnp.float32) * (2.0 * math.pi / lon_count)
    norm_scale = 1.0 / math.sqrt(lon_count)
    return jnp.stack([jnp.cos(angles) * norm_scale, -jnp.sin(angles) * norm_scale], axis=1).astype(jnp.bfloat16)

def latitude_weights(lat_count):
    row_index = jnp.arange(lat_count, dtype=jnp.float32)
    sine_values = jnp.sin((row_index + 0.5) * (math.pi / lat_count))
    return sine_values * (lat_count / jnp.sum(sine_values))

def grid_reference(members, target, weights, fairness):
    values = members.astype(jnp.float32)
    ens_count = values.shape[0]

    def add_member(index, carried):
        spread, sign_sums = carried
        member_row = lax.dynamic_slice_in_dim(values, index, 1, 0)
        differences = values - member_row
        return (spread + lax.optimization_barrier(jnp.sum(jnp.abs(differences), axis=0)), sign_sums + jnp.sign(differences))
    initial = (jnp.zeros(values.shape[1:], jnp.float32), jnp.zeros(values.shape, jnp.float32))
    spread, sign_sums = lax.fori_loop(0, ens_count, add_member, initial)
    errors = values - target.astype(jnp.float32)[None]
    cell_scores = lax.optimization_barrier(jnp.mean(jnp.abs(errors), axis=0)) - fairness / (2.0 * ens_count * (ens_count - 1)) * spread
    gradient = weights[None, :, None] * (jnp.sign(errors) - fairness / (ens_count - 1) * sign_sums)
    return (lax.optimization_barrier(jnp.mean(cell_scores, axis=-1)), gradient.astype(jnp.bfloat16))

def spectral_reference(values, target, order_weight, fairness):
    ens_count = values.shape[3]

    def add_member(index, carried):
        spread, pulls = carried
        member_row = lax.dynamic_slice_in_dim(values, index, 1, 3)
        differences = values - member_row
        magnitude = jnp.sqrt(differences[:, :, 0] ** 2 + differences[:, :, 1] ** 2 + SOFTEN * SOFTEN)
        return (spread + lax.optimization_barrier(jnp.sum(magnitude - SOFTEN, axis=2)), pulls + differences / magnitude[:, :, None])
    initial = (jnp.zeros(values.shape[:2] + values.shape[4:], jnp.float32), jnp.zeros(values.shape, jnp.float32))
    spread, pulls = lax.fori_loop(0, ens_count, add_member, initial)
    errors = values - target[:, :, :, None]
    error_size = jnp.sqrt(errors[:, :, 0] ** 2 + errors[:, :, 1] ** 2 + SOFTEN * SOFTEN)
    scores = lax.optimization_barrier(jnp.mean(error_size - SOFTEN, axis=2)) - fairness / (2.0 * ens_count * (ens_count - 1)) * spread
    gradient = order_weight[:, None, None, None, None] * (errors / error_size[:, :, None] - fairness / (ens_count - 1) * pulls)
    return (jnp.transpose(scores, (0, 2, 1)), gradient)

def reference(ens, truth, legendre, orders):
    ens_count, var_count, lat_count, lon_count = ens.shape
    order_count = orders.shape[0]
    degree_count = legendre.shape[2]
    fairness = 1.0 - FAIR_GAP / ens_count
    transform = fourier_table(orders, lon_count)
    flat_table = transform.reshape(lon_count, 2 * order_count)

    def forward_field(field):
        product = jnp.dot(field.reshape(-1, lon_count), flat_table, preferred_element_type=jnp.float32)
        return product.astype(jnp.bfloat16).reshape(var_count, lat_count, 2, order_count)
    fields = jnp.concatenate([ens, truth[None]], axis=0)
    fourier = lax.map(forward_field, fields)
    fourier = jnp.transpose(fourier, (2, 4, 3, 0, 1)).reshape(lat_count, order_count, -1)

    def add_band(running, band_index):
        weights = lax.dynamic_slice_in_dim(legendre, band_index * LAT_DEV, LAT_DEV, 0).astype(jnp.float32)
        rows_band = lax.dynamic_slice_in_dim(fourier, band_index * LAT_DEV, LAT_DEV, 0).astype(jnp.float32)
        band_part = jnp.einsum('tkl,tkx->klx', weights, rows_band).astype(jnp.bfloat16)
        return (running + lax.optimization_barrier(band_part).astype(jnp.float32), None)
    initial = jnp.zeros((order_count, degree_count, fourier.shape[2]), jnp.float32)
    summed, _ = lax.scan(add_band, initial, jnp.arange(N_SPACE, dtype=jnp.int32))
    spectra = lax.optimization_barrier(summed.astype(jnp.bfloat16)).astype(jnp.float32)
    spectra = spectra.reshape(order_count, degree_count, 2, ens_count + 1, var_count)
    members_spec = spectra[:, :, :, :ens_count]
    truth_spec = spectra[:, :, :, ens_count]
    order_weight = jnp.where(orders == 0, 1.0, 2.0).astype(jnp.float32)
    spec_score, pulls = spectral_reference(members_spec, truth_spec, order_weight, fairness)
    pulls = pulls.astype(jnp.bfloat16).reshape(order_count, degree_count, -1)
    fourier_grad = jnp.einsum('tkl,klx->tkx', legendre.astype(jnp.float32), pulls.astype(jnp.float32))
    fourier_grad = fourier_grad.astype(jnp.bfloat16).reshape(lat_count, order_count, 2, ens_count, var_count)

    def backward_member(member_grad):
        arranged = jnp.transpose(member_grad, (3, 0, 2, 1)).reshape(var_count * lat_count, 2 * order_count)
        product = jnp.dot(arranged, flat_table.T, preferred_element_type=jnp.float32)
        return product.astype(jnp.bfloat16).reshape(var_count, lat_count, lon_count)
    spec_grad = lax.map(backward_member, jnp.moveaxis(fourier_grad, 3, 0))
    lat_weight = latitude_weights(lat_count)

    def grid_variable(pieces):
        members, target = pieces
        return grid_reference(members, target, lat_weight, fairness)
    grid_rows, grid_grads = lax.map(grid_variable, (jnp.moveaxis(ens, 1, 0), truth))
    grid_score = grid_rows.reshape(var_count, N_SPACE, LAT_DEV)
    grid_grad = jnp.transpose(grid_grads, (1, 0, 2, 3)).reshape(ens_count, var_count, N_SPACE, LAT_DEV, lon_count)
    return (grid_score, grid_grad, spec_score, spec_grad)
```

```python
import functools
import math

import jax
import jax.numpy as jnp
from jax import lax
from jax.experimental import pallas as pl
from jax.experimental.pallas import tpu as pltpu
from jax.sharding import PartitionSpec as P

FAIR_GAP = 0.05
SOFTEN = 0.1
MIB = 1024 * 1024
BAND = 16
LANES = 128
ROW_PAD = 40


def latitude_weights(lat_count):
    row_index = jnp.arange(lat_count, dtype=jnp.float32)
    sine_values = jnp.sin((row_index + 0.5) * (math.pi / lat_count))
    return sine_values * (lat_count / jnp.sum(sine_values))


def write_table(orders_ref, table_ref):
    lon_count = table_ref.shape[0]
    order_count = orders_ref.shape[1]
    chunk = 160
    norm = 1.0 / math.sqrt(lon_count)
    listed = orders_ref[...].astype(jnp.float32)

    def fill(step, _):
        start = pl.multiple_of(step * chunk, chunk)
        rows = lax.broadcasted_iota(jnp.int32, (chunk, order_count), 0) + start
        product = rows.astype(jnp.float32) * listed
        turns = jnp.floor(product * (1.0 / lon_count))
        phase = product - turns * lon_count
        quarter = jnp.floor(phase * (4.0 / lon_count) + 0.5)
        angle = (phase - quarter * (lon_count / 4.0)) * (2.0 * math.pi / lon_count)
        square = angle * angle
        sine = angle * (
            1.0 + square * (-1.0 / 6 + square * (1.0 / 120 + square * (-1.0 / 5040 + square / 362880)))
        )
        cosine = 1.0 + square * (
            -0.5 + square * (1.0 / 24 + square * (-1.0 / 720 + square * (1.0 / 40320)))
        )
        half = jnp.floor(quarter * 0.5)
        odd = quarter - 2.0 * half
        half_odd = half - 2.0 * jnp.floor(half * 0.5)
        flip = 1.0 - 2.0 * half_odd
        swap = odd > 0.5
        cos_value = jnp.where(swap, -sine, cosine) * flip
        sin_value = jnp.where(swap, cosine, sine) * flip
        table_ref[pl.ds(start, chunk), :order_count] = (cos_value * norm).astype(jnp.bfloat16)
        table_ref[pl.ds(start, chunk), order_count:] = (-sin_value * norm).astype(jnp.bfloat16)
        return 0

    lax.fori_loop(0, lon_count // chunk, fill, 0)


def forward_kernel(
    var_count, start_ref, orders_ref, ens_ref, truth_ref, leg_ref, out_ref, table_ref,
    staged, swapped, truth_part, leg_part, sems,
):
    step = pl.program_id(0)
    own_rows = 2 * var_count * BAND
    block = ens_ref.shape[0]
    deg_part = leg_part.shape[0]
    var_part = truth_part.shape[0]
    leg_at = 2 * own_rows
    truth_at = leg_at + deg_part * BAND
    truth_rows = var_part * BAND
    used = truth_at + 2 * truth_rows
    order_count = orders_ref.shape[1]

    @pl.when(step == 0)
    def _():
        truth_copy = pltpu.make_async_copy(
            truth_ref.at[pl.ds(start_ref[0], var_part)], truth_part, sems.at[0]
        )
        leg_copy = pltpu.make_async_copy(
            leg_ref.at[pl.ds(start_ref[1], deg_part)], leg_part, sems.at[1]
        )
        truth_copy.start()
        leg_copy.start()
        write_table(orders_ref, table_ref)
        staged[used:, :] = jnp.zeros((staged.shape[0] - used, order_count), jnp.float32)
        truth_copy.wait()
        rows = jnp.dot(
            truth_part[...].reshape(truth_rows, -1), table_ref[...],
            preferred_element_type=jnp.float32,
        )
        staged[truth_at : truth_at + truth_rows, :] = rows[:, :order_count]
        staged[truth_at + truth_rows : used, :] = rows[:, order_count:]
        leg_copy.wait()
        staged[leg_at:truth_at, :] = (
            leg_part[...].reshape(deg_part * BAND, order_count).astype(jnp.float32)
        )

    rows = jnp.dot(ens_ref[...], table_ref[...], preferred_element_type=jnp.float32)
    at = pl.multiple_of(step * block, block)
    staged[pl.ds(at, block), :] = rows[:, :order_count]
    staged[pl.ds(own_rows + at, block), :] = rows[:, order_count:]

    @pl.when(step == pl.num_programs(0) - 1)
    def _():
        width = staged.shape[0] // BAND
        for row in range(BAND):
            piece = staged[pl.ds(row, width, stride=BAND), :]
            swapped[0, pl.ds(row, order_count, stride=BAND), :] = piece[:LANES].T
            swapped[1, pl.ds(row, order_count, stride=BAND), :] = piece[LANES:].T
        for part in range(2):
            out_ref[:, :, part * LANES : (part + 1) * LANES] = (
                swapped[part].reshape(order_count, BAND, LANES).astype(jnp.bfloat16)
            )


def forward(ens, truth, legendre, orders, member_index, member_count):
    own_count, var_count, band_rows, lon_count = ens.shape
    order_count = orders.shape[0]
    deg_count = legendre.shape[2]
    deg_part = -(-deg_count // member_count)
    var_part = -(-var_count // member_count)
    starts = jnp.stack(
        [
            jnp.minimum(member_index * var_part, var_count - var_part),
            jnp.minimum(member_index * deg_part, deg_count - deg_part),
        ]
    ).astype(jnp.int32)
    rows = own_count * var_count * band_rows
    steps = 4
    width = 2 * LANES
    return pl.pallas_call(
        functools.partial(forward_kernel, var_count),
        grid=(steps,),
        in_specs=[
            pl.BlockSpec(memory_space=pltpu.SMEM),
            pl.BlockSpec((1, order_count), lambda i: (0, 0)),
            pl.BlockSpec((rows // steps, lon_count), lambda i: (i, 0)),
            pl.BlockSpec(memory_space=pl.ANY),
            pl.BlockSpec(memory_space=pl.ANY),
        ],
        out_specs=[
            pl.BlockSpec((order_count, band_rows, width), lambda i: (0, 0, 0)),
            pl.BlockSpec((lon_count, 2 * order_count), lambda i: (0, 0)),
        ],
        out_shape=[
            jax.ShapeDtypeStruct((order_count, band_rows, width), jnp.bfloat16),
            jax.ShapeDtypeStruct((lon_count, 2 * order_count), jnp.bfloat16),
        ],
        scratch_shapes=[
            pltpu.VMEM((width * band_rows, order_count), jnp.float32),
            pltpu.VMEM((2, order_count * band_rows, LANES), jnp.float32),
            pltpu.VMEM((var_part, band_rows, lon_count), jnp.bfloat16),
            pltpu.VMEM((deg_part, band_rows, order_count), jnp.bfloat16),
            pltpu.SemaphoreType.DMA((2,)),
        ],
        compiler_params=pltpu.CompilerParams(vmem_limit_bytes=32 * MIB),
        cost_estimate=pl.CostEstimate(
            flops=2 * rows * lon_count * 2 * order_count, bytes_accessed=6 * MIB, transcendentals=0
        ),
        name="forward",
    )(starts, orders.reshape(1, -1), ens.reshape(rows, lon_count), truth,
      jnp.transpose(legendre, (2, 0, 1)))


def spectral_kernel(
    fairness, member_count, var_count, deg_count, omega_ref, in_ref, grad_ref, score_ref,
    weights, values, spectra, pulls, scores,
):
    ens_count = 2 * member_count
    deg_part = -(-deg_count // member_count)
    var_part = -(-var_count // member_count)
    lat_count = weights.shape[0]
    space_count = lat_count // BAND
    leg_at = 4 * var_count
    truth_at = leg_at + deg_part
    omega = omega_ref[0]
    spread_scale = -fairness / (ens_count * (ens_count - 1))
    pull_scale = -fairness / (ens_count - 1)

    values[...] = jnp.zeros_like(values)
    weights[...] = jnp.zeros_like(weights)
    for member in range(member_count):
        block = in_ref[:, member].reshape(lat_count, 2 * LANES)
        deg_start = min(member * deg_part, deg_count - deg_part)
        weights[:, deg_start : deg_start + deg_part] = block[:, leg_at : leg_at + deg_part].astype(
            jnp.float32
        )
        turned = block.astype(jnp.float32).T
        var_start = min(member * var_part, var_count - var_part)
        for c in range(2):
            for own in range(2):
                at = (c * (ens_count + 1) + 2 * member + own) * ROW_PAD
                source = (2 * c + own) * var_count
                values[at : at + var_count, :] = turned[source : source + var_count]
            at = (c * (ens_count + 1) + ens_count) * ROW_PAD + var_start
            source = truth_at + c * var_part
            values[at : at + var_part, :] = turned[source : source + var_part]
    table = weights[...].astype(jnp.bfloat16)
    spectra[...] = jnp.dot(
        values[...].astype(jnp.bfloat16), table, preferred_element_type=jnp.float32
    )

    def tile(index, _):
        lane_tile = index % (weights.shape[1] // LANES)
        row_tile = index // (weights.shape[1] // LANES)
        lanes = pl.ds(pl.multiple_of(lane_tile * LANES, LANES), LANES)

        def load(c, e):
            at = (c * (ens_count + 1) + e) * ROW_PAD
            return spectra[pl.ds(pl.multiple_of(at + row_tile * 8, 8), 8), lanes]

        def pair(a, b):
            d0 = a[0] - b[0]
            d1 = a[1] - b[1]
            square = d0 * d0 + d1 * d1 + SOFTEN * SOFTEN
            inverse = lax.rsqrt(square)
            return square * inverse, d0 * inverse, d1 * inverse

        z = [(load(0, e), load(1, e)) for e in range(ens_count)]
        y = (load(0, ens_count), load(1, ens_count))
        zero = jnp.zeros((8, LANES), jnp.float32)
        pull = [[zero, zero] for _ in range(ens_count)]
        spread = zero
        for i in range(ens_count):
            for j in range(i + 1, ens_count):
                size, u0, u1 = pair(z[i], z[j])
                spread = spread + size
                pull[i][0] = pull[i][0] + u0
                pull[i][1] = pull[i][1] + u1
                pull[j][0] = pull[j][0] - u0
                pull[j][1] = pull[j][1] - u1
        error = zero
        for e in range(ens_count):
            size, u0, u1 = pair(z[e], y)
            error = error + size
            for c, u in enumerate((u0, u1)):
                at = ((e // 2) * 4 + 2 * c + e % 2) * ROW_PAD
                pulls[pl.ds(pl.multiple_of(at + row_tile * 8, 8), 8), lanes] = omega * (
                    u + pull_scale * pull[e][c]
                )
        pairs = ens_count * (ens_count - 1) // 2
        score = (error - SOFTEN * ens_count) * (1.0 / ens_count) + spread_scale * (
            spread - SOFTEN * pairs
        )
        scores[pl.ds(pl.multiple_of(row_tile * 8, 8), 8), lanes] = score
        return 0

    lax.fori_loop(0, (ROW_PAD // 8) * (weights.shape[1] // LANES), tile, 0)
    score_ref[...] = scores[:var_count, :deg_count].astype(jnp.bfloat16)
    for member in range(member_count):
        part = pulls[member * 4 * ROW_PAD : (member + 1) * 4 * ROW_PAD, :].astype(jnp.bfloat16)
        back = lax.dot_general(
            table, part, (((1,), (1,)), ((), ())), preferred_element_type=jnp.float32
        ).astype(jnp.bfloat16)
        grad_ref[:, member, :, : 4 * ROW_PAD] = back.reshape(space_count, BAND, 4 * ROW_PAD)
        grad_ref[:, member, :, 4 * ROW_PAD :] = jnp.zeros(
            (space_count, BAND, 2 * LANES - 4 * ROW_PAD), jnp.bfloat16
        )


def spectral(received, omega, fairness, member_count, var_count, deg_count):
    senders, band_rows, width = received.shape
    space_count = senders // member_count
    lat_count = space_count * band_rows
    deg_pad = -(-deg_count // LANES) * LANES
    ens_count = 2 * member_count
    grads, score = pl.pallas_call(
        functools.partial(spectral_kernel, fairness, member_count, var_count, deg_count),
        in_specs=[
            pl.BlockSpec(memory_space=pltpu.SMEM),
            pl.BlockSpec(memory_space=pltpu.VMEM),
        ],
        out_specs=[pl.BlockSpec(memory_space=pltpu.VMEM)] * 2,
        out_shape=[
            jax.ShapeDtypeStruct((space_count, member_count, band_rows, width), jnp.bfloat16),
            jax.ShapeDtypeStruct((var_count, deg_count), jnp.bfloat16),
        ],
        scratch_shapes=[
            pltpu.VMEM((lat_count, deg_pad), jnp.float32),
            pltpu.VMEM((2 * (ens_count + 1) * ROW_PAD, lat_count), jnp.float32),
            pltpu.VMEM((2 * (ens_count + 1) * ROW_PAD, deg_pad), jnp.float32),
            pltpu.VMEM((2 * ens_count * ROW_PAD, deg_pad), jnp.float32),
            pltpu.VMEM((ROW_PAD, deg_pad), jnp.float32),
        ],
        compiler_params=pltpu.CompilerParams(vmem_limit_bytes=40 * MIB),
        cost_estimate=pl.CostEstimate(
            flops=60_000_000, bytes_accessed=40 * MIB, transcendentals=0
        ),
        name="spectral",
    )(omega, received.reshape(space_count, member_count, band_rows, width))
    return grads.reshape(received.shape), score


def backward_kernel(var_count, in_ref, table_ref, out_ref, staged, turned):
    step = pl.program_id(0)
    order_count = in_ref.shape[0]
    block = out_ref.shape[0]
    rows = 2 * var_count * BAND

    @pl.when(step == 0)
    def _():
        for part in range(2):
            staged[part] = (
                in_ref[:, :, part * LANES : (part + 1) * LANES]
                .astype(jnp.float32)
                .reshape(order_count * BAND, LANES)
            )
        for row in range(BAND):
            low = staged[0, pl.ds(row, order_count, stride=BAND), :].T
            high = staged[1, pl.ds(row, order_count, stride=BAND), :].T
            whole = jnp.concatenate([low, high], axis=0)
            for c in range(2):
                for own in range(2):
                    source = (2 * c + own) * ROW_PAD
                    at = own * var_count * BAND + row
                    turned[c, pl.ds(at, var_count, stride=BAND), :] = whole[
                        source : source + var_count
                    ]

    at = pl.multiple_of(step * block, block)
    left = jnp.concatenate(
        [turned[0, pl.ds(at, block), :], turned[1, pl.ds(at, block), :]], axis=1
    ).astype(jnp.bfloat16)
    out_ref[...] = lax.dot_general(
        left, table_ref[...], (((1,), (1,)), ((), ())), preferred_element_type=jnp.float32
    ).astype(jnp.bfloat16)


def backward(received, table, own_count, var_count):
    order_count, band_rows, width = received.shape
    lon_count = table.shape[0]
    rows = own_count * var_count * band_rows
    steps = 4
    return pl.pallas_call(
        functools.partial(backward_kernel, var_count),
        grid=(steps,),
        in_specs=[
            pl.BlockSpec((order_count, band_rows, width), lambda i: (0, 0, 0)),
            pl.BlockSpec((lon_count, 2 * order_count), lambda i: (0, 0)),
        ],
        out_specs=pl.BlockSpec((rows // steps, lon_count), lambda i: (i, 0)),
        out_shape=jax.ShapeDtypeStruct((rows, lon_count), jnp.bfloat16),
        scratch_shapes=[
            pltpu.VMEM((2, order_count * band_rows, LANES), jnp.float32),
            pltpu.VMEM((2, rows, order_count), jnp.float32),
        ],
        compiler_params=pltpu.CompilerParams(vmem_limit_bytes=32 * MIB),
        cost_estimate=pl.CostEstimate(
            flops=2 * rows * lon_count * 2 * order_count, bytes_accessed=6 * MIB, transcendentals=0
        ),
        name="backward",
    )(received, table)


def grid_kernel(fairness, lon_count, ens_ref, truth_ref, weight_ref, grad_ref, score_ref, total):
    step = pl.program_id(0)
    ens_count, row_count, width = ens_ref.shape
    one = jnp.ones((1, 1), jnp.bfloat16)
    spread_scale = -fairness / (ens_count * (ens_count - 1))
    pull_scale = -fairness / (ens_count - 1)

    @pl.when(step == 0)
    def _():
        total[...] = jnp.zeros_like(total)

    def sign(a, b):
        zero = jnp.zeros(a.shape, jnp.bfloat16)
        return jnp.where(a > b, zero + one, jnp.where(b > a, zero - one, zero))

    def tile(at, rows, lane_at):
        span = pl.ds(at, rows)
        lanes = slice(lane_at, lane_at + LANES)
        x = [ens_ref[e, span, lanes] for e in range(ens_count)]
        y = truth_ref[span, lanes]
        sums = [jnp.zeros((rows, LANES), jnp.bfloat16) for _ in range(ens_count)]
        for i in range(ens_count):
            for j in range(i + 1, ens_count):
                s = sign(x[i], x[j])
                sums[i] = sums[i] + s
                sums[j] = sums[j] - s
        goal = y.astype(jnp.float32)
        weight = weight_ref[span, :]
        error = jnp.zeros((rows, LANES), jnp.float32)
        spread = jnp.zeros((rows, LANES), jnp.float32)
        for e in range(ens_count):
            value = x[e].astype(jnp.float32)
            toward = sums[e].astype(jnp.float32)
            error = error + jnp.abs(value - goal)
            spread = spread + value * toward
            grad_ref[e, span, lanes] = (
                weight * (sign(x[e], y).astype(jnp.float32) + pull_scale * toward)
            ).astype(jnp.bfloat16)
        score = error * (1.0 / ens_count) + spread_scale * spread
        lane = lax.broadcasted_iota(jnp.int32, (rows, LANES), 1) + (step * width + lane_at)
        total[span, :] += jnp.where(lane < lon_count, score, 0.0)

    whole = row_count // 16
    for lane_at in range(0, width, LANES):
        def body(index, _, lane_at=lane_at):
            tile(pl.multiple_of(index * 16, 16), 16, lane_at)
            return 0

        lax.fori_loop(0, whole, body, 0)
        if row_count % 16:
            tile(whole * 16, row_count % 16, lane_at)

    @pl.when(step == pl.num_programs(0) - 1)
    def _():
        score_ref[...] = jnp.sum(total[...], axis=1, keepdims=True) * (1.0 / lon_count)


def grid_scores(members, target, weights, fairness):
    ens_count, row_count, lon_count = members.shape
    width = 2 * LANES
    return pl.pallas_call(
        functools.partial(grid_kernel, fairness, lon_count),
        grid=(-(-lon_count // width),),
        in_specs=[
            pl.BlockSpec((ens_count, row_count, width), lambda i: (0, 0, i)),
            pl.BlockSpec((row_count, width), lambda i: (0, i)),
            pl.BlockSpec((row_count, 1), lambda i: (0, 0)),
        ],
        out_specs=[
            pl.BlockSpec((ens_count, row_count, width), lambda i: (0, 0, i)),
            pl.BlockSpec((row_count, 1), lambda i: (0, 0)),
        ],
        out_shape=[
            jax.ShapeDtypeStruct((ens_count, row_count, lon_count), jnp.bfloat16),
            jax.ShapeDtypeStruct((row_count, 1), jnp.float32),
        ],
        scratch_shapes=[pltpu.VMEM((row_count, LANES), jnp.float32)],
        compiler_params=pltpu.CompilerParams(vmem_limit_bytes=32 * MIB),
        cost_estimate=pl.CostEstimate(
            flops=60_000_000, bytes_accessed=40 * MIB, transcendentals=0
        ),
        name="grid",
    )(members, target, weights)


def local(ens, truth, legendre, orders):
    own_count, var_count, band_rows, lon_count = ens.shape
    order_count = orders.shape[0]
    deg_count = legendre.shape[2]
    space_count = lax.axis_size("space")
    member_count = lax.axis_size("member")
    space_index = lax.axis_index("space")
    member_index = lax.axis_index("member")
    lat_count = band_rows * space_count
    ens_count = own_count * member_count
    sub_rows = band_rows // member_count
    fairness = 1.0 - FAIR_GAP / ens_count

    owners = ("space", "member")
    sent, table = forward(ens, truth, legendre, orders, member_index, member_count)
    received = lax.all_to_all(sent, owners, split_axis=0, concat_axis=0, tiled=True)
    own_order = lax.dynamic_slice_in_dim(orders, space_index * member_count + member_index, 1, 0)
    omega = jnp.where(own_order == 0, 1.0, 2.0).astype(jnp.float32)
    grads, score = spectral(received, omega, fairness, member_count, var_count, deg_count)
    returned = lax.all_to_all(grads, owners, split_axis=0, concat_axis=0, tiled=True)
    spec_grad = backward(returned, table, own_count, var_count).reshape(ens.shape)
    spec_score = lax.all_gather(score, "member", axis=0, tiled=False).astype(jnp.float32)

    parted = ens.reshape(own_count, var_count, member_count, sub_rows, lon_count)
    parted = parted.transpose(2, 0, 3, 1, 4).reshape(
        member_count, own_count * sub_rows * var_count, lon_count
    )
    gathered = lax.all_to_all(parted, "member", split_axis=0, concat_axis=0, tiled=True)
    members = gathered.reshape(ens_count, sub_rows * var_count, lon_count)
    target = lax.dynamic_slice_in_dim(truth, member_index * sub_rows, sub_rows, 1)
    target = target.transpose(1, 0, 2).reshape(sub_rows * var_count, lon_count)
    row_weights = lax.dynamic_slice_in_dim(
        latitude_weights(lat_count), space_index * band_rows + member_index * sub_rows, sub_rows, 0
    )
    row_weights = jnp.broadcast_to(row_weights[:, None], (sub_rows, var_count)).reshape(-1, 1)
    grid_grad, grid_rows = grid_scores(members, target, row_weights, fairness)
    grid_grad = grid_grad.reshape(ens_count, sub_rows, var_count, lon_count).swapaxes(1, 2)
    grid_grad = grid_grad.reshape(ens_count, var_count, 1, sub_rows, lon_count)
    grid_score = grid_rows.reshape(sub_rows, var_count).T.reshape(var_count, 1, sub_rows)
    return (grid_score, grid_grad, spec_score, spec_grad)


def solution(mesh):
    in_specs = (
        P("member", None, "space", None),
        P(None, "space", None),
        P("space", None, None),
        P(),
    )
    out_specs = (
        P(None, "space", "member"),
        P(None, None, "space", "member", None),
        P("space", None, None),
        P("member", None, "space", None),
    )
    return jax.shard_map(local, mesh=mesh, in_specs=in_specs, out_specs=out_specs, check_vma=False)
```

```python
import functools
import math

import jax
import jax.numpy as jnp
import numpy as np
from jax import lax
from jax.experimental import pallas as pl
from jax.experimental.pallas import tpu as pltpu
from jax.sharding import PartitionSpec as P

FAIR_GAP = 0.05
SOFTEN = 0.1
MIB = 1024 * 1024
COST = 1024
BAND = 16
LANES = 128
HALF = 6 * LANES
ROW_PAD = 40


def latitude_weights(lat_count):
    sine_values = np.sin((np.arange(lat_count) + 0.5) * (math.pi / lat_count))
    return (sine_values * (lat_count / sine_values.sum())).astype(np.float32)


def write_table(orders_ref, table_ref):
    lon_count = table_ref.shape[0]
    order_count = orders_ref.shape[1]
    chunk = 160
    norm = 1.0 / math.sqrt(lon_count)
    listed = orders_ref[...].astype(jnp.float32)

    def fill(step, _):
        start = pl.multiple_of(step * chunk, chunk)
        rows = lax.broadcasted_iota(jnp.int32, (chunk, order_count), 0) + start
        product = rows.astype(jnp.float32) * listed
        turns = jnp.floor(product * (1.0 / lon_count))
        phase = product - turns * lon_count
        quarter = jnp.floor(phase * (4.0 / lon_count) + 0.5)
        angle = (phase - quarter * (lon_count / 4.0)) * (2.0 * math.pi / lon_count)
        square = angle * angle
        sine = angle * (
            1.0 + square * (-1.0 / 6 + square * (1.0 / 120 + square * (-1.0 / 5040 + square / 362880)))
        )
        cosine = 1.0 + square * (
            -0.5 + square * (1.0 / 24 + square * (-1.0 / 720 + square * (1.0 / 40320)))
        )
        half = jnp.floor(quarter * 0.5)
        odd = quarter - 2.0 * half
        half_odd = half - 2.0 * jnp.floor(half * 0.5)
        flip = 1.0 - 2.0 * half_odd
        swap = odd > 0.5
        cos_value = jnp.where(swap, -sine, cosine) * flip
        sin_value = jnp.where(swap, cosine, sine) * flip
        table_ref[pl.ds(start, chunk), :order_count] = (cos_value * norm).astype(jnp.bfloat16)
        table_ref[pl.ds(start, chunk), order_count:] = (-sin_value * norm).astype(jnp.bfloat16)
        return 0

    lax.fori_loop(0, lon_count // chunk, fill, 0)


def forward_kernel(
    var_count, start_ref, orders_ref, ens_ref, truth_ref, leg_ref, out_ref, table_ref,
    staged, swapped, truth_part, leg_part, sems,
):
    step = pl.program_id(0)
    own_rows = 2 * var_count * BAND
    block = ens_ref.shape[0]
    deg_part = leg_part.shape[0]
    var_part = truth_part.shape[0]
    leg_at = 2 * own_rows
    truth_at = leg_at + deg_part * BAND
    truth_rows = var_part * BAND
    used = truth_at + 2 * truth_rows
    order_count = orders_ref.shape[1]

    @pl.when(step == 0)
    def _():
        truth_copy = pltpu.make_async_copy(
            truth_ref.at[pl.ds(start_ref[0], var_part)], truth_part, sems.at[0]
        )
        leg_copy = pltpu.make_async_copy(
            leg_ref.at[pl.ds(start_ref[1], deg_part)], leg_part, sems.at[1]
        )
        truth_copy.start()
        leg_copy.start()
        write_table(orders_ref, table_ref)
        staged[used:, :] = jnp.zeros((staged.shape[0] - used, order_count), jnp.float32)
        truth_copy.wait()
        rows = jnp.dot(
            truth_part[...].reshape(truth_rows, -1), table_ref[...],
            preferred_element_type=jnp.float32,
        )
        staged[truth_at : truth_at + truth_rows, :] = rows[:, :order_count]
        staged[truth_at + truth_rows : used, :] = rows[:, order_count:]
        leg_copy.wait()
        staged[leg_at:truth_at, :] = (
            leg_part[...].reshape(deg_part * BAND, order_count).astype(jnp.float32)
        )

    rows = jnp.dot(ens_ref[...], table_ref[...], preferred_element_type=jnp.float32)
    at = pl.multiple_of(step * block, block)
    staged[pl.ds(at, block), :] = rows[:, :order_count]
    staged[pl.ds(own_rows + at, block), :] = rows[:, order_count:]

    @pl.when(step == pl.num_programs(0) - 1)
    def _():
        width = staged.shape[0] // BAND
        for row in range(BAND):
            piece = staged[pl.ds(row, width, stride=BAND), :]
            swapped[0, pl.ds(row, order_count, stride=BAND), :] = piece[:LANES].T
            swapped[1, pl.ds(row, order_count, stride=BAND), :] = piece[LANES:].T
        for part in range(2):
            out_ref[:, :, part * LANES : (part + 1) * LANES] = (
                swapped[part].reshape(order_count, BAND, LANES).astype(jnp.bfloat16)
            )


def forward(ens, truth, legendre, orders, member_index, member_count):
    own_count, var_count, band_rows, lon_count = ens.shape
    order_count = orders.shape[0]
    deg_count = legendre.shape[2]
    deg_part = -(-deg_count // member_count)
    var_part = -(-var_count // member_count)
    starts = jnp.stack(
        [
            jnp.minimum(member_index * var_part, var_count - var_part),
            jnp.minimum(member_index * deg_part, deg_count - deg_part),
        ]
    ).astype(jnp.int32)
    rows = own_count * var_count * band_rows
    steps = 4
    width = 2 * LANES
    return pl.pallas_call(
        functools.partial(forward_kernel, var_count),
        grid=(steps,),
        in_specs=[
            pl.BlockSpec(memory_space=pltpu.SMEM),
            pl.BlockSpec((1, order_count), lambda i: (0, 0)),
            pl.BlockSpec((rows // steps, lon_count), lambda i: (i, 0)),
            pl.BlockSpec(memory_space=pl.ANY),
            pl.BlockSpec(memory_space=pl.ANY),
        ],
        out_specs=[
            pl.BlockSpec((order_count, band_rows, width), lambda i: (0, 0, 0)),
            pl.BlockSpec((lon_count, 2 * order_count), lambda i: (0, 0)),
        ],
        out_shape=[
            jax.ShapeDtypeStruct((order_count, band_rows, width), jnp.bfloat16),
            jax.ShapeDtypeStruct((lon_count, 2 * order_count), jnp.bfloat16),
        ],
        scratch_shapes=[
            pltpu.VMEM((width * band_rows, order_count), jnp.float32),
            pltpu.VMEM((2, order_count * band_rows, LANES), jnp.float32),
            pltpu.VMEM((var_part, band_rows, lon_count), jnp.bfloat16),
            pltpu.VMEM((deg_part, band_rows, order_count), jnp.bfloat16),
            pltpu.SemaphoreType.DMA((2,)),
        ],
        compiler_params=pltpu.CompilerParams(vmem_limit_bytes=56 * MIB),
        cost_estimate=pl.CostEstimate(flops=COST, bytes_accessed=COST, transcendentals=0),
        name="forward",
    )(starts, orders.reshape(1, -1), ens.reshape(rows, lon_count), truth,
      jnp.transpose(legendre, (2, 0, 1)))


def spectral_kernel(
    fairness, member_count, var_count, deg_count, omega_ref, in_ref, grad_ref, score_ref,
    weights, values, spectra, pulls, scores,
):
    ens_count = 2 * member_count
    deg_part = -(-deg_count // member_count)
    var_part = -(-var_count // member_count)
    lat_count = weights.shape[0]
    space_count = lat_count // BAND
    leg_at = 4 * var_count
    truth_at = leg_at + deg_part
    omega = omega_ref[0]
    spread_scale = -fairness / (ens_count * (ens_count - 1))
    pull_scale = -fairness / (ens_count - 1)

    values[...] = jnp.zeros_like(values)
    weights[...] = jnp.zeros_like(weights)
    for member in range(member_count):
        block = in_ref[:, member].reshape(lat_count, 2 * LANES)
        deg_start = min(member * deg_part, deg_count - deg_part)
        weights[:, deg_start : deg_start + deg_part] = block[:, leg_at : leg_at + deg_part].astype(
            jnp.float32
        )
        turned = block.astype(jnp.float32).T
        var_start = min(member * var_part, var_count - var_part)
        for c in range(2):
            for own in range(2):
                at = (c * (ens_count + 1) + 2 * member + own) * ROW_PAD
                source = (2 * c + own) * var_count
                values[at : at + var_count, :] = turned[source : source + var_count]
            at = (c * (ens_count + 1) + ens_count) * ROW_PAD + var_start
            source = truth_at + c * var_part
            values[at : at + var_part, :] = turned[source : source + var_part]
    table = weights[...].astype(jnp.bfloat16)
    spectra[...] = jnp.dot(
        values[...].astype(jnp.bfloat16), table, preferred_element_type=jnp.float32
    )

    def tile(index, _):
        lane_tile = index % (weights.shape[1] // LANES)
        row_tile = index // (weights.shape[1] // LANES)
        lanes = pl.ds(pl.multiple_of(lane_tile * LANES, LANES), LANES)

        def load(c, e):
            at = (c * (ens_count + 1) + e) * ROW_PAD
            return spectra[pl.ds(pl.multiple_of(at + row_tile * 8, 8), 8), lanes]

        def pair(a, b):
            d0 = a[0] - b[0]
            d1 = a[1] - b[1]
            square = d0 * d0 + d1 * d1 + SOFTEN * SOFTEN
            inverse = lax.rsqrt(square)
            return square * inverse, d0 * inverse, d1 * inverse

        z = [(load(0, e), load(1, e)) for e in range(ens_count)]
        y = (load(0, ens_count), load(1, ens_count))
        zero = jnp.zeros((8, LANES), jnp.float32)
        pull = [[zero, zero] for _ in range(ens_count)]
        spread = zero
        for i in range(ens_count):
            for j in range(i + 1, ens_count):
                size, u0, u1 = pair(z[i], z[j])
                spread = spread + size
                pull[i][0] = pull[i][0] + u0
                pull[i][1] = pull[i][1] + u1
                pull[j][0] = pull[j][0] - u0
                pull[j][1] = pull[j][1] - u1
        error = zero
        for e in range(ens_count):
            size, u0, u1 = pair(z[e], y)
            error = error + size
            for c, u in enumerate((u0, u1)):
                at = ((e // 2) * 4 + 2 * c + e % 2) * ROW_PAD
                pulls[pl.ds(pl.multiple_of(at + row_tile * 8, 8), 8), lanes] = omega * (
                    u + pull_scale * pull[e][c]
                )
        pairs = ens_count * (ens_count - 1) // 2
        score = (error - SOFTEN * ens_count) * (1.0 / ens_count) + spread_scale * (
            spread - SOFTEN * pairs
        )
        scores[pl.ds(pl.multiple_of(row_tile * 8, 8), 8), lanes] = score
        return 0

    lax.fori_loop(0, (ROW_PAD // 8) * (weights.shape[1] // LANES), tile, 0)
    score_ref[...] = scores[:var_count, :deg_count].astype(jnp.bfloat16)
    for member in range(member_count):
        part = pulls[member * 4 * ROW_PAD : (member + 1) * 4 * ROW_PAD, :].astype(jnp.bfloat16)
        back = lax.dot_general(
            table, part, (((1,), (1,)), ((), ())), preferred_element_type=jnp.float32
        )
        halves = back.reshape(space_count, 2, BAND // 2, 4 * ROW_PAD)
        packed = jnp.concatenate(
            [
                halves[:, 0],
                halves[:, 1],
                jnp.zeros((space_count, BAND // 2, 3 * LANES - 8 * ROW_PAD), jnp.float32),
            ],
            axis=2,
        )
        grad_ref[:, member] = packed.astype(jnp.bfloat16)


def spectral(received, omega, fairness, member_count, var_count, deg_count):
    senders, band_rows, width = received.shape
    space_count = senders // member_count
    lat_count = space_count * band_rows
    deg_pad = -(-deg_count // LANES) * LANES
    ens_count = 2 * member_count
    grads, score = pl.pallas_call(
        functools.partial(spectral_kernel, fairness, member_count, var_count, deg_count),
        in_specs=[
            pl.BlockSpec(memory_space=pltpu.SMEM),
            pl.BlockSpec(memory_space=pltpu.VMEM),
        ],
        out_specs=[pl.BlockSpec(memory_space=pltpu.VMEM)] * 2,
        out_shape=[
            jax.ShapeDtypeStruct(
                (space_count, member_count, band_rows // 2, 3 * LANES), jnp.bfloat16
            ),
            jax.ShapeDtypeStruct((var_count, deg_count), jnp.bfloat16),
        ],
        scratch_shapes=[
            pltpu.VMEM((lat_count, deg_pad), jnp.float32),
            pltpu.VMEM((2 * (ens_count + 1) * ROW_PAD, lat_count), jnp.float32),
            pltpu.VMEM((2 * (ens_count + 1) * ROW_PAD, deg_pad), jnp.float32),
            pltpu.VMEM((2 * ens_count * ROW_PAD, deg_pad), jnp.float32),
            pltpu.VMEM((ROW_PAD, deg_pad), jnp.float32),
        ],
        compiler_params=pltpu.CompilerParams(vmem_limit_bytes=56 * MIB),
        cost_estimate=pl.CostEstimate(flops=COST, bytes_accessed=COST, transcendentals=0),
        name="spectral",
    )(omega, received.reshape(space_count, member_count, band_rows, width))
    return grads.reshape(senders, band_rows // 2, 3 * LANES), score


def backward_kernel(var_count, in_ref, table_ref, out_ref, staged, turned):
    step = pl.program_id(0)
    order_count = in_ref.shape[0]
    block = out_ref.shape[0]
    rows = 2 * var_count * BAND

    @pl.when(step == 0)
    def _():
        half = BAND // 2
        for part in range(3):
            staged[part] = (
                in_ref[:, :, part * LANES : (part + 1) * LANES]
                .astype(jnp.float32)
                .reshape(order_count * half, LANES)
            )
        for row in range(half):
            whole = jnp.concatenate(
                [staged[part, pl.ds(row, order_count, stride=half), :].T for part in range(3)],
                axis=0,
            )
            for high in range(2):
                for c in range(2):
                    for own in range(2):
                        source = (4 * high + 2 * c + own) * ROW_PAD
                        at = own * var_count * BAND + high * half + row
                        turned[c, pl.ds(at, var_count, stride=BAND), :] = whole[
                            source : source + var_count
                        ]

    at = pl.multiple_of(step * block, block)
    left = jnp.concatenate(
        [turned[0, pl.ds(at, block), :], turned[1, pl.ds(at, block), :]], axis=1
    ).astype(jnp.bfloat16)
    out_ref[...] = lax.dot_general(
        left, table_ref[...], (((1,), (1,)), ((), ())), preferred_element_type=jnp.float32
    ).astype(jnp.bfloat16)


def backward(received, table, own_count, var_count):
    order_count, half_rows, width = received.shape
    band_rows = 2 * half_rows
    lon_count = table.shape[0]
    rows = own_count * var_count * band_rows
    steps = 4
    return pl.pallas_call(
        functools.partial(backward_kernel, var_count),
        grid=(steps,),
        in_specs=[
            pl.BlockSpec((order_count, half_rows, width), lambda i: (0, 0, 0)),
            pl.BlockSpec((lon_count, 2 * order_count), lambda i: (0, 0)),
        ],
        out_specs=pl.BlockSpec((rows // steps, lon_count), lambda i: (i, 0)),
        out_shape=jax.ShapeDtypeStruct((rows, lon_count), jnp.bfloat16),
        scratch_shapes=[
            pltpu.VMEM((3, order_count * half_rows, LANES), jnp.float32),
            pltpu.VMEM((2, rows, order_count), jnp.float32),
        ],
        compiler_params=pltpu.CompilerParams(vmem_limit_bytes=56 * MIB),
        cost_estimate=pl.CostEstimate(flops=COST, bytes_accessed=COST, transcendentals=0),
        name="backward",
    )(received, table)


def regroup_kernel(var_count, sub_rows, member_ref, ens_ref, truth_ref, out_ref, target_ref,
                   wide, paired):
    member_count = out_ref.shape[0]

    def move(rows_ref, lanes, tile, member, keep):
        for row in range(sub_rows):
            paired[tile, keep, pl.ds(row, var_count, stride=sub_rows), :] = wide[
                tile, pl.ds(member * sub_rows + row, var_count, stride=BAND), :
            ]
        return paired[tile, keep].astype(jnp.bfloat16)

    for tile in range(wide.shape[0]):
        lanes = slice(tile * LANES, (tile + 1) * LANES)

        @pl.when(pl.program_id(1) == 0)
        def _(tile=tile, lanes=lanes):
            wide[tile] = truth_ref[:, lanes].astype(jnp.float32)
            target_ref[:, lanes] = move(truth_ref, lanes, tile, member_ref[0], 0)

        wide[tile] = ens_ref[:, lanes].astype(jnp.float32)
        for member in range(member_count):
            out_ref[member, 0, :, lanes] = move(ens_ref, lanes, tile, member, member)


def regroup(ens, truth, member_index, member_count, span):
    own_count, var_count, band_rows, lon_count = ens.shape
    sub_rows = band_rows // member_count
    width = 3 * LANES
    rows = var_count * sub_rows
    first, last = span
    begin = first // width
    return pl.pallas_call(
        functools.partial(regroup_kernel, var_count, sub_rows),
        grid=(-(-(last - first) // width), own_count),
        in_specs=[
            pl.BlockSpec(memory_space=pltpu.SMEM),
            pl.BlockSpec((var_count * band_rows, width), lambda i, e: (e, i + begin)),
            pl.BlockSpec((var_count * band_rows, width), lambda i, e: (0, i + begin)),
        ],
        out_specs=[
            pl.BlockSpec((member_count, 1, rows, width), lambda i, e: (0, e, 0, i)),
            pl.BlockSpec((rows, width), lambda i, e: (0, i)),
        ],
        out_shape=[
            jax.ShapeDtypeStruct((member_count, own_count, rows, last - first), jnp.bfloat16),
            jax.ShapeDtypeStruct((rows, last - first), jnp.bfloat16),
        ],
        scratch_shapes=[
            pltpu.VMEM((width // LANES, var_count * band_rows, LANES), jnp.float32),
            pltpu.VMEM((width // LANES, member_count, rows, LANES), jnp.float32),
        ],
        compiler_params=pltpu.CompilerParams(vmem_limit_bytes=56 * MIB),
        cost_estimate=pl.CostEstimate(flops=COST, bytes_accessed=COST, transcendentals=0),
        name="regroup",
    )(member_index.reshape(1).astype(jnp.int32), ens.reshape(-1, lon_count),
      truth.reshape(-1, lon_count))


def grid_kernel(fairness, lon_count, first, weight_ref, ens_ref, truth_ref, *rest):
    grad_ref, score_ref, total = rest[-3:]
    step = pl.program_id(0)
    ens_count, row_count, width = ens_ref.shape
    sub_rows = grad_ref.shape[2]
    spread_scale = -fairness / (ens_count * (ens_count - 1))
    pull_scale = -fairness / (ens_count - 1)

    @pl.when(step == 0)
    def _():
        total[...] = jnp.zeros_like(total)

    which = lax.broadcasted_iota(jnp.int32, (16, LANES), 0) % sub_rows
    row_weight = jnp.full((16, LANES), weight_ref[0], jnp.float32)
    for row in range(1, sub_rows):
        row_weight = jnp.where(which == row, weight_ref[row], row_weight)

    def sign(a, b):
        zero = jnp.zeros(a.shape, jnp.bfloat16)
        one = jnp.ones(a.shape, jnp.bfloat16)
        return jnp.where(a > b, one, jnp.where(b > a, -one, zero))

    def tile(at, rows, lane_at):
        span = pl.ds(at, rows)
        lanes = slice(lane_at, lane_at + LANES)
        x = [ens_ref[e, span, lanes] for e in range(ens_count)]
        y = truth_ref[span, lanes]
        sums = [jnp.zeros((rows, LANES), jnp.bfloat16) for _ in range(ens_count)]
        for i in range(ens_count):
            for j in range(i + 1, ens_count):
                s = sign(x[i], x[j])
                sums[i] = sums[i] + s
                sums[j] = sums[j] - s
        goal = y.astype(jnp.float32)
        weight = row_weight[:rows]
        error = jnp.zeros((rows, LANES), jnp.float32)
        spread = jnp.zeros((rows, LANES), jnp.float32)
        for e in range(ens_count):
            value = x[e].astype(jnp.float32)
            toward = sums[e].astype(jnp.float32)
            error = error + jnp.abs(value - goal)
            spread = spread + value * toward
            grad = (
                weight * (sign(x[e], y).astype(jnp.float32) + pull_scale * toward)
            ).astype(jnp.bfloat16)
            grad_ref[e, pl.ds(at // sub_rows, rows // sub_rows), :, lanes] = grad.reshape(rows // sub_rows, sub_rows, LANES)
        score = error * (1.0 / ens_count) + spread_scale * spread
        lane = lax.broadcasted_iota(jnp.int32, (rows, LANES), 1) + ((step + first) * width + lane_at)
        total[span, :] += jnp.where(lane < lon_count, score, 0.0)

    whole = row_count // 16
    for lane_at in range(0, width, LANES):
        def body(index, _, lane_at=lane_at):
            tile(pl.multiple_of(index * 16, 16), 16, lane_at)
            return 0

        lax.fori_loop(0, whole, body, 0)
        if row_count % 16:
            tile(whole * 16, row_count % 16, lane_at)

    @pl.when(step == pl.num_programs(0) - 1)
    def _():
        score_ref[...] = jnp.sum(total[...], axis=1, keepdims=True) * (1.0 / lon_count)


def grid_scores(members, target, weights, fairness, lon_count, sub_rows, at, earlier=None):
    ens_count, row_count, span = members.shape
    var_count = row_count // sub_rows
    width = 2 * LANES
    first = at // width
    carried = () if earlier is None else (earlier,)
    return pl.pallas_call(
        functools.partial(grid_kernel, fairness, lon_count, first),
        grid=(-(-span // width),),
        in_specs=[
            pl.BlockSpec(memory_space=pltpu.SMEM),
            pl.BlockSpec((ens_count, row_count, width), lambda i: (0, 0, i)),
            pl.BlockSpec((row_count, width), lambda i: (0, i)),
        ]
        + [pl.BlockSpec(memory_space=pl.ANY)] * len(carried),
        out_specs=[
            pl.BlockSpec((ens_count, var_count, sub_rows, width), lambda i: (0, 0, 0, i + first)),
            pl.BlockSpec((row_count, 1), lambda i: (0, 0)),
        ],
        out_shape=[
            jax.ShapeDtypeStruct((ens_count, var_count, sub_rows, lon_count), jnp.bfloat16),
            jax.ShapeDtypeStruct((row_count, 1), jnp.float32),
        ],
        scratch_shapes=[pltpu.VMEM((row_count, LANES), jnp.float32)],
        input_output_aliases={3: 0} if carried else {},
        compiler_params=pltpu.CompilerParams(vmem_limit_bytes=56 * MIB),
        cost_estimate=pl.CostEstimate(flops=COST, bytes_accessed=COST, transcendentals=0),
        name="grid",
    )(weights, members, target, *carried)


def local(ens, truth, legendre, orders):
    own_count, var_count, band_rows, lon_count = ens.shape
    order_count = orders.shape[0]
    deg_count = legendre.shape[2]
    space_count = lax.axis_size("space")
    member_count = lax.axis_size("member")
    space_index = lax.axis_index("space")
    member_index = lax.axis_index("member")
    lat_count = band_rows * space_count
    ens_count = own_count * member_count
    sub_rows = band_rows // member_count
    fairness = 1.0 - FAIR_GAP / ens_count

    owners = ("space", "member")
    sent, table = forward(ens, truth, legendre, orders, member_index, member_count)
    received = lax.all_to_all(sent, owners, split_axis=0, concat_axis=0, tiled=True)

    spans = ((0, HALF), (HALF, lon_count))
    halves = [regroup(ens, truth, member_index, member_count, span) for span in spans]
    early, late = (half[0] for half in halves)
    received, early, late = lax.optimization_barrier((received, early, late))

    def exchange(half):
        return lax.all_to_all(half, "member", split_axis=0, concat_axis=0, tiled=True).reshape(
            ens_count, var_count * sub_rows, -1
        )

    early = exchange(early)
    own_order = lax.dynamic_slice_in_dim(orders, space_index * member_count + member_index, 1, 0)
    omega = jnp.where(own_order == 0, 1.0, 2.0).astype(jnp.float32)
    grads, score = spectral(received, omega, fairness, member_count, var_count, deg_count)
    grads, early, late = lax.optimization_barrier((grads, early, late))
    late = exchange(late)
    row_weights = lax.dynamic_slice_in_dim(
        jnp.asarray(latitude_weights(lat_count)),
        space_index * band_rows + member_index * sub_rows, sub_rows, 0,
    )
    grid_args = (row_weights, fairness, lon_count, sub_rows)
    grid_grad, early_rows = grid_scores(early, halves[0][1], *grid_args, 0)
    grads, grid_grad, late = lax.optimization_barrier((grads, grid_grad, late))
    returned = lax.all_to_all(grads, owners, split_axis=0, concat_axis=0, tiled=True)
    grid_grad, late_rows = grid_scores(late, halves[1][1], *grid_args, HALF, grid_grad)
    grid_grad = grid_grad.reshape(ens_count, var_count, 1, sub_rows, lon_count)
    grid_score = (early_rows + late_rows).reshape(var_count, 1, sub_rows)

    returned, score, grid_grad = lax.optimization_barrier((returned, score, grid_grad))
    copies = jnp.broadcast_to(score[None], (member_count,) + score.shape)
    spec_score = lax.all_to_all(copies, "member", split_axis=0, concat_axis=0, tiled=True)
    spec_score = spec_score.astype(jnp.float32)
    spec_grad = backward(returned, table, own_count, var_count).reshape(ens.shape)
    return (grid_score, grid_grad, spec_score, spec_grad)


def solution(mesh):
    in_specs = (
        P("member", None, "space", None),
        P(None, "space", None),
        P("space", None, None),
        P(),
    )
    out_specs = (
        P(None, "space", "member"),
        P(None, None, "space", "member", None),
        P("space", None, None),
        P("member", None, "space", None),
    )
    return jax.shard_map(local, mesh=mesh, in_specs=in_specs, out_specs=out_specs, check_vma=False)
```

```python
import functools
import math

import jax
import jax.numpy as jnp
import numpy as np
from jax import lax
from jax.experimental import pallas as pl
from jax.experimental.pallas import tpu as pltpu
from jax.sharding import PartitionSpec as P

FAIR_GAP = 0.05
SOFTEN = 0.1
MIB = 1024 * 1024
COST = 1024
BAND = 16
LANES = 128
GRID_WIDTH = 2 * LANES
EARLY_BLOCKS = 3
ROW_PAD = 40


def latitude_weights(lat_count):
    sine_values = np.sin((np.arange(lat_count) + 0.5) * (math.pi / lat_count))
    return (sine_values * (lat_count / sine_values.sum())).astype(np.float32)


def write_table(orders_ref, table_ref):
    lon_count = table_ref.shape[0]
    order_count = orders_ref.shape[1]
    chunk = 160
    norm = 1.0 / math.sqrt(lon_count)
    listed = orders_ref[...].astype(jnp.float32)

    def fill(step, _):
        start = pl.multiple_of(step * chunk, chunk)
        rows = lax.broadcasted_iota(jnp.int32, (chunk, order_count), 0) + start
        product = rows.astype(jnp.float32) * listed
        turns = jnp.floor(product * (1.0 / lon_count))
        phase = product - turns * lon_count
        quarter = jnp.floor(phase * (4.0 / lon_count) + 0.5)
        angle = (phase - quarter * (lon_count / 4.0)) * (2.0 * math.pi / lon_count)
        square = angle * angle
        sine = angle * (
            1.0 + square * (-1.0 / 6 + square * (1.0 / 120 + square * (-1.0 / 5040 + square / 362880)))
        )
        cosine = 1.0 + square * (
            -0.5 + square * (1.0 / 24 + square * (-1.0 / 720 + square * (1.0 / 40320)))
        )
        half = jnp.floor(quarter * 0.5)
        odd = quarter - 2.0 * half
        half_odd = half - 2.0 * jnp.floor(half * 0.5)
        flip = 1.0 - 2.0 * half_odd
        swap = odd > 0.5
        cos_value = jnp.where(swap, -sine, cosine) * flip
        sin_value = jnp.where(swap, cosine, sine) * flip
        table_ref[pl.ds(start, chunk), :order_count] = (cos_value * norm).astype(jnp.bfloat16)
        table_ref[pl.ds(start, chunk), order_count:] = (-sin_value * norm).astype(jnp.bfloat16)
        return 0

    lax.fori_loop(0, lon_count // chunk, fill, 0)


def forward_kernel(
    var_count, deg_count, orders_ref, ens_ref, truth_ref, leg_ref, out_ref, table_ref,
    staged, swapped, truth_part, leg_part, sems,
):
    step = pl.program_id(0)
    own_rows = 2 * var_count * BAND
    block = ens_ref.shape[0]
    deg_part = leg_part.shape[0]
    var_part = truth_part.shape[0]
    leg_at = 2 * own_rows
    truth_at = leg_at + deg_part * BAND
    truth_rows = var_part * BAND
    used = truth_at + 2 * truth_rows
    order_count = orders_ref.shape[1]

    @pl.when(step == 0)
    def _():
        member = lax.axis_index("member")
        var_start = jnp.minimum(member * var_part, var_count - var_part)
        deg_start = jnp.minimum(member * deg_part, deg_count - deg_part)
        truth_copy = pltpu.make_async_copy(
            truth_ref.at[pl.ds(var_start, var_part)], truth_part, sems.at[0]
        )
        leg_copy = pltpu.make_async_copy(
            leg_ref.at[pl.ds(deg_start, deg_part)], leg_part, sems.at[1]
        )
        truth_copy.start()
        leg_copy.start()
        write_table(orders_ref, table_ref)
        staged[used:, :] = jnp.zeros((staged.shape[0] - used, order_count), jnp.float32)
        truth_copy.wait()
        rows = jnp.dot(
            truth_part[...].reshape(truth_rows, -1), table_ref[...],
            preferred_element_type=jnp.float32,
        )
        staged[truth_at : truth_at + truth_rows, :] = rows[:, :order_count]
        staged[truth_at + truth_rows : used, :] = rows[:, order_count:]
        leg_copy.wait()
        staged[leg_at:truth_at, :] = (
            leg_part[...].reshape(deg_part * BAND, order_count).astype(jnp.float32)
        )

    rows = jnp.dot(ens_ref[...], table_ref[...], preferred_element_type=jnp.float32)
    at = pl.multiple_of(step * block, block)
    staged[pl.ds(at, block), :] = rows[:, :order_count]
    staged[pl.ds(own_rows + at, block), :] = rows[:, order_count:]

    @pl.when(step == pl.num_programs(0) - 1)
    def _():
        width = staged.shape[0] // BAND
        for row in range(BAND):
            piece = staged[pl.ds(row, width, stride=BAND), :]
            swapped[0, pl.ds(row, order_count, stride=BAND), :] = piece[:LANES].T
            swapped[1, pl.ds(row, order_count, stride=BAND), :] = piece[LANES:].T
        for part in range(2):
            out_ref[:, :, part * LANES : (part + 1) * LANES] = (
                swapped[part].reshape(order_count, BAND, LANES).astype(jnp.bfloat16)
            )


def forward(ens, truth, legendre, orders, member_count):
    own_count, var_count, band_rows, lon_count = ens.shape
    order_count = orders.shape[0]
    deg_count = legendre.shape[2]
    deg_part = -(-deg_count // member_count)
    var_part = -(-var_count // member_count)
    rows = own_count * var_count * band_rows
    steps = 4
    width = 2 * LANES
    return pl.pallas_call(
        functools.partial(forward_kernel, var_count, deg_count),
        grid=(steps,),
        in_specs=[
            pl.BlockSpec((1, order_count), lambda i: (0, 0)),
            pl.BlockSpec((rows // steps, lon_count), lambda i: (i, 0)),
            pl.BlockSpec(memory_space=pl.ANY),
            pl.BlockSpec(memory_space=pl.ANY),
        ],
        out_specs=[
            pl.BlockSpec((order_count, band_rows, width), lambda i: (0, 0, 0)),
            pl.BlockSpec((lon_count, 2 * order_count), lambda i: (0, 0)),
        ],
        out_shape=[
            jax.ShapeDtypeStruct((order_count, band_rows, width), jnp.bfloat16),
            jax.ShapeDtypeStruct((lon_count, 2 * order_count), jnp.bfloat16),
        ],
        scratch_shapes=[
            pltpu.VMEM((width * band_rows, order_count), jnp.float32),
            pltpu.VMEM((2, order_count * band_rows, LANES), jnp.float32),
            pltpu.VMEM((var_part, band_rows, lon_count), jnp.bfloat16),
            pltpu.VMEM((deg_part, band_rows, order_count), jnp.bfloat16),
            pltpu.SemaphoreType.DMA((2,)),
        ],
        compiler_params=pltpu.CompilerParams(vmem_limit_bytes=56 * MIB),
        cost_estimate=pl.CostEstimate(flops=COST, bytes_accessed=COST, transcendentals=0),
        name="forward",
    )(orders.reshape(1, -1), ens.reshape(rows, lon_count), truth,
      jnp.transpose(legendre, (2, 0, 1)))


def spectral_kernel(
    fairness, member_count, var_count, deg_count, orders_ref, in_ref, grad_ref, score_ref,
    weights, values, spectra, pulls, scores,
):
    ens_count = 2 * member_count
    deg_part = -(-deg_count // member_count)
    var_part = -(-var_count // member_count)
    lat_count = weights.shape[0]
    space_count = lat_count // BAND
    leg_at = 4 * var_count
    truth_at = leg_at + deg_part
    own_order = orders_ref[lax.axis_index("space") * member_count + lax.axis_index("member")]
    omega = jnp.where(own_order == 0, 1.0, 2.0).astype(jnp.float32)
    spread_scale = -fairness / (ens_count * (ens_count - 1))
    pull_scale = -fairness / (ens_count - 1)

    values[...] = jnp.zeros_like(values)
    weights[...] = jnp.zeros_like(weights)
    for member in range(member_count):
        block = in_ref[:, member].reshape(lat_count, 2 * LANES)
        deg_start = min(member * deg_part, deg_count - deg_part)
        weights[:, deg_start : deg_start + deg_part] = block[:, leg_at : leg_at + deg_part].astype(
            jnp.float32
        )
        turned = block.astype(jnp.float32).T
        var_start = min(member * var_part, var_count - var_part)
        for c in range(2):
            for own in range(2):
                at = (c * (ens_count + 1) + 2 * member + own) * ROW_PAD
                source = (2 * c + own) * var_count
                values[at : at + var_count, :] = turned[source : source + var_count]
            at = (c * (ens_count + 1) + ens_count) * ROW_PAD + var_start
            source = truth_at + c * var_part
            values[at : at + var_part, :] = turned[source : source + var_part]
    table = weights[...].astype(jnp.bfloat16)
    spectra[...] = jnp.dot(
        values[...].astype(jnp.bfloat16), table, preferred_element_type=jnp.float32
    )

    def tile(index, _):
        lane_tile = index % (weights.shape[1] // LANES)
        row_tile = index // (weights.shape[1] // LANES)
        lanes = pl.ds(pl.multiple_of(lane_tile * LANES, LANES), LANES)

        def load(c, e):
            at = (c * (ens_count + 1) + e) * ROW_PAD
            return spectra[pl.ds(pl.multiple_of(at + row_tile * 8, 8), 8), lanes]

        def pair(a, b):
            d0 = a[0] - b[0]
            d1 = a[1] - b[1]
            square = d0 * d0 + d1 * d1 + SOFTEN * SOFTEN
            inverse = lax.rsqrt(square)
            return square * inverse, d0 * inverse, d1 * inverse

        z = [(load(0, e), load(1, e)) for e in range(ens_count)]
        y = (load(0, ens_count), load(1, ens_count))
        zero = jnp.zeros((8, LANES), jnp.float32)
        pull = [[zero, zero] for _ in range(ens_count)]
        spread = zero
        for i in range(ens_count):
            for j in range(i + 1, ens_count):
                size, u0, u1 = pair(z[i], z[j])
                spread = spread + size
                pull[i][0] = pull[i][0] + u0
                pull[i][1] = pull[i][1] + u1
                pull[j][0] = pull[j][0] - u0
                pull[j][1] = pull[j][1] - u1
        error = zero
        for e in range(ens_count):
            size, u0, u1 = pair(z[e], y)
            error = error + size
            for c, u in enumerate((u0, u1)):
                at = ((e // 2) * 4 + 2 * c + e % 2) * ROW_PAD
                pulls[pl.ds(pl.multiple_of(at + row_tile * 8, 8), 8), lanes] = omega * (
                    u + pull_scale * pull[e][c]
                )
        pairs = ens_count * (ens_count - 1) // 2
        score = (error - SOFTEN * ens_count) * (1.0 / ens_count) + spread_scale * (
            spread - SOFTEN * pairs
        )
        scores[pl.ds(pl.multiple_of(row_tile * 8, 8), 8), lanes] = score
        return 0

    lax.fori_loop(0, (ROW_PAD // 8) * (weights.shape[1] // LANES), tile, 0)
    rounded = scores[:var_count, :deg_count].astype(jnp.bfloat16)
    for member in range(member_count):
        score_ref[member] = rounded
    for member in range(member_count):
        part = pulls[member * 4 * ROW_PAD : (member + 1) * 4 * ROW_PAD, :].astype(jnp.bfloat16)
        back = lax.dot_general(
            table, part, (((1,), (1,)), ((), ())), preferred_element_type=jnp.float32
        )
        halves = back.reshape(space_count, 2, BAND // 2, 4 * ROW_PAD)
        packed = jnp.concatenate(
            [
                halves[:, 0],
                halves[:, 1],
                jnp.zeros((space_count, BAND // 2, 3 * LANES - 8 * ROW_PAD), jnp.float32),
            ],
            axis=2,
        )
        grad_ref[:, member] = packed.astype(jnp.bfloat16)


def spectral(received, orders, fairness, member_count, var_count, deg_count):
    senders, band_rows, width = received.shape
    space_count = senders // member_count
    lat_count = space_count * band_rows
    deg_pad = -(-deg_count // LANES) * LANES
    ens_count = 2 * member_count
    grads, score = pl.pallas_call(
        functools.partial(spectral_kernel, fairness, member_count, var_count, deg_count),
        in_specs=[
            pl.BlockSpec(memory_space=pltpu.SMEM),
            pl.BlockSpec(memory_space=pltpu.VMEM),
        ],
        out_specs=[pl.BlockSpec(memory_space=pltpu.VMEM)] * 2,
        out_shape=[
            jax.ShapeDtypeStruct(
                (space_count, member_count, band_rows // 2, 3 * LANES), jnp.bfloat16
            ),
            jax.ShapeDtypeStruct((member_count, var_count, deg_count), jnp.bfloat16),
        ],
        scratch_shapes=[
            pltpu.VMEM((lat_count, deg_pad), jnp.float32),
            pltpu.VMEM((2 * (ens_count + 1) * ROW_PAD, lat_count), jnp.float32),
            pltpu.VMEM((2 * (ens_count + 1) * ROW_PAD, deg_pad), jnp.float32),
            pltpu.VMEM((2 * ens_count * ROW_PAD, deg_pad), jnp.float32),
            pltpu.VMEM((ROW_PAD, deg_pad), jnp.float32),
        ],
        compiler_params=pltpu.CompilerParams(vmem_limit_bytes=56 * MIB),
        cost_estimate=pl.CostEstimate(flops=COST, bytes_accessed=COST, transcendentals=0),
        name="spectral",
    )(orders, received.reshape(space_count, member_count, band_rows, width))
    return grads.reshape(senders, band_rows // 2, 3 * LANES), score


def backward_kernel(var_count, in_ref, table_ref, out_ref, staged, turned):
    step = pl.program_id(0)
    order_count = in_ref.shape[0]
    block = out_ref.shape[0]
    rows = 2 * var_count * BAND

    @pl.when(step == 0)
    def _():
        half = BAND // 2
        for part in range(3):
            staged[part] = (
                in_ref[:, :, part * LANES : (part + 1) * LANES]
                .astype(jnp.float32)
                .reshape(order_count * half, LANES)
            )
        for row in range(half):
            whole = jnp.concatenate(
                [staged[part, pl.ds(row, order_count, stride=half), :].T for part in range(3)],
                axis=0,
            )
            for high in range(2):
                for c in range(2):
                    for own in range(2):
                        source = (4 * high + 2 * c + own) * ROW_PAD
                        at = own * var_count * BAND + high * half + row
                        turned[c, pl.ds(at, var_count, stride=BAND), :] = whole[
                            source : source + var_count
                        ]

    at = pl.multiple_of(step * block, block)
    left = jnp.concatenate(
        [turned[0, pl.ds(at, block), :], turned[1, pl.ds(at, block), :]], axis=1
    ).astype(jnp.bfloat16)
    out_ref[...] = lax.dot_general(
        left, table_ref[...], (((1,), (1,)), ((), ())), preferred_element_type=jnp.float32
    ).astype(jnp.bfloat16)


def backward(received, table, own_count, var_count):
    order_count, half_rows, width = received.shape
    band_rows = 2 * half_rows
    lon_count = table.shape[0]
    rows = own_count * var_count * band_rows
    steps = 4
    return pl.pallas_call(
        functools.partial(backward_kernel, var_count),
        grid=(steps,),
        in_specs=[
            pl.BlockSpec((order_count, half_rows, width), lambda i: (0, 0, 0)),
            pl.BlockSpec((lon_count, 2 * order_count), lambda i: (0, 0)),
        ],
        out_specs=pl.BlockSpec((rows // steps, lon_count), lambda i: (i, 0)),
        out_shape=jax.ShapeDtypeStruct((rows, lon_count), jnp.bfloat16),
        scratch_shapes=[
            pltpu.VMEM((3, order_count * half_rows, LANES), jnp.float32),
            pltpu.VMEM((2, rows, order_count), jnp.float32),
        ],
        compiler_params=pltpu.CompilerParams(vmem_limit_bytes=56 * MIB),
        cost_estimate=pl.CostEstimate(flops=COST, bytes_accessed=COST, transcendentals=0),
        name="backward",
    )(received, table)


HOPS = ((0, 0), (0, 1), (0, 3), (1, 0), (0, 2), (1, 1), (1, 3), (1, 2))
RING = 4


def partner(member, hop, sign):
    half, spot = member // RING, member % RING
    return (half + hop[0]) % 2 * RING + (spot + sign * hop[1] + RING) % RING


def hop_pairs(hop, member_count):
    return [(i, partner(i, hop, 1)) for i in range(member_count)]


def regroup_kernel(var_count, sub_rows, ens_ref, truth_ref, *rest):
    outs, (target_ref, wide, paired) = rest[:-3], rest[-3:]
    member = lax.axis_index("member")

    def move(tile, goal, keep):
        for row in range(sub_rows):
            paired[tile, keep, pl.ds(row, var_count, stride=sub_rows), :] = wide[
                tile, pl.ds(goal * sub_rows + row, var_count, stride=BAND), :
            ]
        return paired[tile, keep].astype(jnp.bfloat16)

    for tile in range(wide.shape[0]):
        lanes = slice(tile * LANES, (tile + 1) * LANES)

        @pl.when(pl.program_id(1) == 0)
        def _(tile=tile, lanes=lanes):
            wide[tile] = truth_ref[:, lanes].astype(jnp.float32)
            target_ref[:, lanes] = move(tile, member, 0)

        wide[tile] = ens_ref[:, lanes].astype(jnp.float32)
        for place, hop in enumerate(HOPS):
            outs[place][0, :, lanes] = move(tile, partner(member, hop, 1), place)


def regroup(ens, truth, member_count):
    own_count, var_count, band_rows, lon_count = ens.shape
    sub_rows = band_rows // member_count
    width = 3 * LANES
    rows = var_count * sub_rows
    return pl.pallas_call(
        functools.partial(regroup_kernel, var_count, sub_rows),
        grid=(-(-lon_count // width), own_count),
        in_specs=[
            pl.BlockSpec((var_count * band_rows, width), lambda i, e: (e, i)),
            pl.BlockSpec((var_count * band_rows, width), lambda i, e: (0, i)),
        ],
        out_specs=[pl.BlockSpec((1, rows, width), lambda i, e: (e, 0, i))] * member_count
        + [pl.BlockSpec((rows, width), lambda i, e: (0, i))],
        out_shape=[
            jax.ShapeDtypeStruct((own_count, rows, lon_count), jnp.bfloat16)
            for _ in range(member_count)
        ]
        + [jax.ShapeDtypeStruct((rows, lon_count), jnp.bfloat16)],
        scratch_shapes=[
            pltpu.VMEM((width // LANES, var_count * band_rows, LANES), jnp.float32),
            pltpu.VMEM((width // LANES, member_count, rows, LANES), jnp.float32),
        ],
        compiler_params=pltpu.CompilerParams(vmem_limit_bytes=56 * MIB),
        cost_estimate=pl.CostEstimate(flops=COST, bytes_accessed=COST, transcendentals=0),
        name="regroup",
    )(ens.reshape(-1, lon_count), truth.reshape(-1, lon_count))


def grid_kernel(fairness, lon_count, first, part_count, weight_ref, truth_ref, *rest):
    parts, carried = rest[:part_count], rest[part_count:-3]
    grad_ref, score_ref, total = rest[-3:]
    step = pl.program_id(0)
    per_part, row_count, width = parts[0].shape
    ens_count = per_part * part_count
    sub_rows = grad_ref.shape[2]
    pull_scale = -fairness / (ens_count - 1)
    member = lax.axis_index("member")
    senders = [partner(member, hop, -1) for hop in HOPS]
    lat_start = (lax.axis_index("space") * part_count + member) * sub_rows
    which = lax.broadcasted_iota(jnp.int32, (8, LANES), 0) % sub_rows
    weight = jnp.full((8, LANES), weight_ref[lat_start], jnp.float32)
    for row in range(1, sub_rows):
        weight = jnp.where(which == row, weight_ref[lat_start + row], weight)

    @pl.when(step == 0)
    def _():
        total[...] = jnp.zeros_like(total)

    def sign(a, b):
        return jnp.minimum(jnp.maximum((a - b) * 2.0**70, -1.0), 1.0)

    def tile(at, rows, lane_at):
        lanes = slice(lane_at, lane_at + LANES)
        span = pl.ds(at, rows)
        wide = [
            parts[e // per_part][e % per_part, span, lanes].astype(jnp.float32)
            for e in range(ens_count)
        ]
        goals = truth_ref[span, lanes].astype(jnp.float32)
        pieces = []
        for half in range(rows // 8):
            piece = slice(8 * half, 8 * half + 8)
            x = [value[piece] * 2.0**64 for value in wide]
            goal = goals[piece]
            y = goal * 2.0**64
            zero = jnp.zeros((8, LANES), jnp.float32)
            sums = [zero] * ens_count
            for i in range(ens_count):
                for j in range(i + 1, ens_count):
                    s = sign(x[i], x[j])
                    sums[i] = sums[i] + s
                    sums[j] = sums[j] - s
            score = zero
            toward_sum = zero
            grads = []
            for e in range(ens_count):
                toward = sign(x[e], y)
                toward_sum = toward_sum + toward
                pull = toward + pull_scale * sums[e]
                score = score + wide[e][piece] * pull
                grads.append(weight * pull)
            pieces.append(grads)
            score = (score - goal * toward_sum) * (1.0 / ens_count)
            lane = lax.broadcasted_iota(jnp.int32, (8, LANES), 1) + (
                (step + first) * width + lane_at
            )
            total[pl.ds(at + 8 * half, 8), :] += jnp.where(lane < lon_count, score, 0.0)
        for e in range(ens_count):
            whole_grad = jnp.concatenate([grads[e] for grads in pieces], axis=0)
            grad_ref[
                senders[e // per_part] * per_part + e % per_part,
                pl.ds(at // sub_rows, rows // sub_rows), :, lanes,
            ] = whole_grad.astype(jnp.bfloat16).reshape(rows // sub_rows, sub_rows, LANES)

    whole = row_count // 16
    for lane_at in range(0, width, LANES):
        def body(index, _, lane_at=lane_at):
            tile(pl.multiple_of(index * 16, 16), 16, lane_at)
            return 0

        lax.fori_loop(0, whole, body, 0)
        if row_count % 16:
            tile(whole * 16, row_count % 16, lane_at)

    @pl.when(step == pl.num_programs(0) - 1)
    def _():
        result = jnp.sum(total[...], axis=1, keepdims=True) * (1.0 / lon_count)
        score_ref[...] = result + carried[1][...] if carried else result


def grid_scores(parts, target, weights, fairness, sub_rows, blocks, earlier=()):
    per_part, row_count, lon_count = parts[0].shape
    ens_count = per_part * len(parts)
    var_count = row_count // sub_rows
    width = GRID_WIDTH
    first, last = blocks
    return pl.pallas_call(
        functools.partial(grid_kernel, fairness, lon_count, first, len(parts)),
        grid=(last - first,),
        in_specs=[
            pl.BlockSpec(memory_space=pltpu.SMEM),
            pl.BlockSpec((row_count, width), lambda i: (0, i + first)),
        ]
        + [pl.BlockSpec((per_part, row_count, width), lambda i: (0, 0, i + first))] * len(parts)
        + [
            pl.BlockSpec(memory_space=pl.ANY),
            pl.BlockSpec((row_count, 1), lambda i: (0, 0)),
        ][: len(earlier)],
        out_specs=[
            pl.BlockSpec((ens_count, var_count, sub_rows, width), lambda i: (0, 0, 0, i + first)),
            pl.BlockSpec((row_count, 1), lambda i: (0, 0)),
        ],
        out_shape=[
            jax.ShapeDtypeStruct((ens_count, var_count, sub_rows, lon_count), jnp.bfloat16),
            jax.ShapeDtypeStruct((row_count, 1), jnp.float32),
        ],
        scratch_shapes=[pltpu.VMEM((row_count, LANES), jnp.float32)],
        input_output_aliases={2 + len(parts): 0} if earlier else {},
        compiler_params=pltpu.CompilerParams(vmem_limit_bytes=56 * MIB),
        cost_estimate=pl.CostEstimate(flops=COST, bytes_accessed=COST, transcendentals=0),
        name="grid",
    )(weights, target, *parts, *earlier)


def local(ens, truth, legendre, orders):
    own_count, var_count, band_rows, lon_count = ens.shape
    order_count = orders.shape[0]
    deg_count = legendre.shape[2]
    space_count = lax.axis_size("space")
    member_count = lax.axis_size("member")
    lat_count = band_rows * space_count
    ens_count = own_count * member_count
    sub_rows = band_rows // member_count
    fairness = 1.0 - FAIR_GAP / ens_count

    owners = ("space", "member")
    sent, table = forward(ens, truth, legendre, orders, member_count)
    received = lax.all_to_all(sent, owners, split_axis=0, concat_axis=0, tiled=True)

    *parts, target = regroup(ens, truth, member_count)
    for place, hop in enumerate(HOPS):
        if place:
            parts[place] = lax.ppermute(parts[place], "member", hop_pairs(hop, member_count))

    received, *parts[1:3] = lax.optimization_barrier((received, *parts[1:3]))
    grads, score = spectral(received, orders, fairness, member_count, var_count, deg_count)
    grads, *parts[3:] = lax.optimization_barrier((grads, *parts[3:]))
    returned = lax.all_to_all(grads, owners, split_axis=0, concat_axis=0, tiled=True)
    weights = jnp.asarray(latitude_weights(lat_count))
    grid_args = (parts, target, weights, fairness, sub_rows)
    early = grid_scores(*grid_args, (0, EARLY_BLOCKS))

    returned, score, *early = lax.optimization_barrier((returned, score, *early))
    spec_score = lax.all_to_all(score, "member", split_axis=0, concat_axis=0, tiled=True)
    spec_score = spec_score.astype(jnp.float32)
    grid_grad, grid_rows = grid_scores(
        *grid_args, (EARLY_BLOCKS, -(-lon_count // GRID_WIDTH)), early
    )
    grid_grad = grid_grad.reshape(ens_count, var_count, 1, sub_rows, lon_count)
    grid_score = grid_rows.reshape(var_count, 1, sub_rows)
    spec_grad = backward(returned, table, own_count, var_count).reshape(ens.shape)
    return (grid_score, grid_grad, spec_score, spec_grad)


def solution(mesh):
    in_specs = (
        P("member", None, "space", None),
        P(None, "space", None),
        P("space", None, None),
        P(),
    )
    out_specs = (
        P(None, "space", "member"),
        P(None, None, "space", "member", None),
        P("space", None, None),
        P("member", None, "space", None),
    )
    return jax.shard_map(local, mesh=mesh, in_specs=in_specs, out_specs=out_specs, check_vma=False)
```

```python
import functools
import math

import jax
import jax.numpy as jnp
import numpy as np
from jax import lax
from jax.experimental import pallas as pl
from jax.experimental.pallas import tpu as pltpu
from jax.sharding import PartitionSpec as P

FAIR_GAP = 0.05
SOFTEN = 0.1
MIB = 1024 * 1024
COST = 1024
BAND = 16
LANES = 128
GRID_WIDTH = 2 * LANES
EARLY_PARTS = 5
FIELD_COPIES = 2
ROW_PAD = 40


def latitude_weights(lat_count):
    sine_values = np.sin((np.arange(lat_count) + 0.5) * (math.pi / lat_count))
    return (sine_values * (lat_count / sine_values.sum())).astype(np.float32)


def write_table(orders_ref, table_ref):
    lon_count = table_ref.shape[0]
    order_count = orders_ref.shape[1]
    chunk = 160
    norm = 1.0 / math.sqrt(lon_count)
    listed = orders_ref[...].astype(jnp.float32)

    def fill(step, _):
        start = pl.multiple_of(step * chunk, chunk)
        rows = lax.broadcasted_iota(jnp.int32, (chunk, order_count), 0) + start
        product = rows.astype(jnp.float32) * listed
        turns = jnp.floor(product * (1.0 / lon_count))
        phase = product - turns * lon_count
        quarter = jnp.floor(phase * (4.0 / lon_count) + 0.5)
        angle = (phase - quarter * (lon_count / 4.0)) * (2.0 * math.pi / lon_count)
        square = angle * angle
        sine = angle * (
            1.0 + square * (-1.0 / 6 + square * (1.0 / 120 + square * (-1.0 / 5040 + square / 362880)))
        )
        cosine = 1.0 + square * (
            -0.5 + square * (1.0 / 24 + square * (-1.0 / 720 + square * (1.0 / 40320)))
        )
        half = jnp.floor(quarter * 0.5)
        odd = quarter - 2.0 * half
        half_odd = half - 2.0 * jnp.floor(half * 0.5)
        flip = 1.0 - 2.0 * half_odd
        swap = odd > 0.5
        cos_value = jnp.where(swap, -sine, cosine) * flip
        sin_value = jnp.where(swap, cosine, sine) * flip
        table_ref[pl.ds(start, chunk), :order_count] = (cos_value * norm).astype(jnp.bfloat16)
        table_ref[pl.ds(start, chunk), order_count:] = (-sin_value * norm).astype(jnp.bfloat16)
        return 0

    lax.fori_loop(0, lon_count // chunk, fill, 0)


def forward_kernel(
    var_count, deg_count, orders_ref, ens_ref, truth_ref, leg_ref, out_ref, table_ref,
    staged, swapped, fields, truth_part, leg_part, sems,
):
    own_rows = 2 * var_count * BAND
    block = own_rows // FIELD_COPIES
    deg_part = leg_part.shape[0]
    var_part = truth_part.shape[0]
    leg_at = 2 * own_rows
    truth_at = leg_at + deg_part * BAND
    truth_rows = var_part * BAND
    used = truth_at + 2 * truth_rows
    order_count = orders_ref.shape[1]

    member = lax.axis_index("member")
    var_start = jnp.minimum(member * var_part, var_count - var_part)
    deg_start = jnp.minimum(member * deg_part, deg_count - deg_part)
    truth_copy = pltpu.make_async_copy(
        truth_ref.at[pl.ds(var_start, var_part)], truth_part, sems.at[0]
    )
    leg_copy = pltpu.make_async_copy(
        leg_ref.at[pl.ds(deg_start, deg_part)], leg_part, sems.at[1]
    )
    copies = [
        pltpu.make_async_copy(
            ens_ref.at[pl.ds(part * block, block)], fields.at[pl.ds(part * block, block)],
            sems.at[2 + part],
        )
        for part in range(FIELD_COPIES)
    ]
    truth_copy.start()
    for copy in copies:
        copy.start()
    leg_copy.start()
    write_table(orders_ref, table_ref)
    staged[used:, :] = jnp.zeros((staged.shape[0] - used, order_count), jnp.float32)
    truth_copy.wait()
    rows = jnp.dot(
        truth_part[...].reshape(truth_rows, -1), table_ref[...],
        preferred_element_type=jnp.float32,
    )
    staged[truth_at : truth_at + truth_rows, :] = rows[:, :order_count]
    staged[truth_at + truth_rows : used, :] = rows[:, order_count:]
    for part, copy in enumerate(copies):
        copy.wait()
        at = part * block
        rows = jnp.dot(
            fields[at : at + block, :], table_ref[...], preferred_element_type=jnp.float32
        )
        staged[at : at + block, :] = rows[:, :order_count]
        staged[own_rows + at : own_rows + at + block, :] = rows[:, order_count:]
    leg_copy.wait()
    staged[leg_at:truth_at, :] = (
        leg_part[...].reshape(deg_part * BAND, order_count).astype(jnp.float32)
    )

    width = staged.shape[0] // BAND
    for row in range(BAND):
        piece = staged[pl.ds(row, width, stride=BAND), :]
        swapped[0, pl.ds(row, order_count, stride=BAND), :] = piece[:LANES].T
        swapped[1, pl.ds(row, order_count, stride=BAND), :] = piece[LANES:].T
    for part in range(2):
        out_ref[:, :, part * LANES : (part + 1) * LANES] = (
            swapped[part].reshape(order_count, BAND, LANES).astype(jnp.bfloat16)
        )


def forward(ens, truth, legendre, orders, member_count):
    own_count, var_count, band_rows, lon_count = ens.shape
    order_count = orders.shape[0]
    deg_count = legendre.shape[2]
    deg_part = -(-deg_count // member_count)
    var_part = -(-var_count // member_count)
    rows = own_count * var_count * band_rows
    width = 2 * LANES
    return pl.pallas_call(
        functools.partial(forward_kernel, var_count, deg_count),
        in_specs=[pl.BlockSpec(memory_space=pltpu.VMEM)] + [pl.BlockSpec(memory_space=pl.ANY)] * 3,
        out_specs=[pl.BlockSpec(memory_space=pltpu.VMEM)] * 2,
        out_shape=[
            jax.ShapeDtypeStruct((order_count, band_rows, width), jnp.bfloat16),
            jax.ShapeDtypeStruct((lon_count, 2 * order_count), jnp.bfloat16),
        ],
        scratch_shapes=[
            pltpu.VMEM((width * band_rows, order_count), jnp.float32),
            pltpu.VMEM((2, order_count * band_rows, LANES), jnp.float32),
            pltpu.VMEM((rows, lon_count), jnp.bfloat16),
            pltpu.VMEM((var_part, band_rows, lon_count), jnp.bfloat16),
            pltpu.VMEM((deg_part, band_rows, order_count), jnp.bfloat16),
            pltpu.SemaphoreType.DMA((2 + FIELD_COPIES,)),
        ],
        compiler_params=pltpu.CompilerParams(vmem_limit_bytes=56 * MIB),
        cost_estimate=pl.CostEstimate(flops=COST, bytes_accessed=COST, transcendentals=0),
        name="forward",
    )(orders.reshape(1, -1), ens.reshape(rows, lon_count), truth,
      jnp.transpose(legendre, (2, 0, 1)))


def spectral_kernel(
    fairness, member_count, var_count, deg_count, orders_ref, in_ref, grad_ref, score_ref,
    weights, values, spectra, pulls, scores,
):
    ens_count = 2 * member_count
    deg_part = -(-deg_count // member_count)
    var_part = -(-var_count // member_count)
    lat_count = weights.shape[0]
    space_count = lat_count // BAND
    leg_at = 4 * var_count
    truth_at = leg_at + deg_part
    own_order = orders_ref[lax.axis_index("space") * member_count + lax.axis_index("member")]
    omega = jnp.where(own_order == 0, 1.0, 2.0).astype(jnp.float32)
    spread_scale = -fairness / (ens_count * (ens_count - 1))
    pull_scale = -fairness / (ens_count - 1)

    values[...] = jnp.zeros_like(values)
    weights[...] = jnp.zeros_like(weights)
    for member in range(member_count):
        block = in_ref[:, member].reshape(lat_count, 2 * LANES)
        deg_start = min(member * deg_part, deg_count - deg_part)
        weights[:, deg_start : deg_start + deg_part] = block[:, leg_at : leg_at + deg_part].astype(
            jnp.float32
        )
        turned = block.astype(jnp.float32).T
        var_start = min(member * var_part, var_count - var_part)
        for c in range(2):
            for own in range(2):
                at = (c * (ens_count + 1) + 2 * member + own) * ROW_PAD
                source = (2 * c + own) * var_count
                values[at : at + var_count, :] = turned[source : source + var_count]
            at = (c * (ens_count + 1) + ens_count) * ROW_PAD + var_start
            source = truth_at + c * var_part
            values[at : at + var_part, :] = turned[source : source + var_part]
    table = weights[...].astype(jnp.bfloat16)
    spectra[...] = jnp.dot(
        values[...].astype(jnp.bfloat16), table, preferred_element_type=jnp.float32
    )

    def tile(index, _):
        lane_tile = index % (weights.shape[1] // LANES)
        row_tile = index // (weights.shape[1] // LANES)
        lanes = pl.ds(pl.multiple_of(lane_tile * LANES, LANES), LANES)

        def load(c, e):
            at = (c * (ens_count + 1) + e) * ROW_PAD
            return spectra[pl.ds(pl.multiple_of(at + row_tile * 8, 8), 8), lanes]

        def pair(a, b):
            d0 = a[0] - b[0]
            d1 = a[1] - b[1]
            square = d0 * d0 + d1 * d1 + SOFTEN * SOFTEN
            inverse = lax.rsqrt(square)
            return square * inverse, d0 * inverse, d1 * inverse

        z = [(load(0, e), load(1, e)) for e in range(ens_count)]
        y = (load(0, ens_count), load(1, ens_count))
        zero = jnp.zeros((8, LANES), jnp.float32)
        pull = [[zero, zero] for _ in range(ens_count)]
        spread = zero
        for i in range(ens_count):
            for j in range(i + 1, ens_count):
                size, u0, u1 = pair(z[i], z[j])
                spread = spread + size
                pull[i][0] = pull[i][0] + u0
                pull[i][1] = pull[i][1] + u1
                pull[j][0] = pull[j][0] - u0
                pull[j][1] = pull[j][1] - u1
        error = zero
        for e in range(ens_count):
            size, u0, u1 = pair(z[e], y)
            error = error + size
            for c, u in enumerate((u0, u1)):
                at = ((e // 2) * 4 + 2 * c + e % 2) * ROW_PAD
                pulls[pl.ds(pl.multiple_of(at + row_tile * 8, 8), 8), lanes] = omega * (
                    u + pull_scale * pull[e][c]
                )
        pairs = ens_count * (ens_count - 1) // 2
        score = (error - SOFTEN * ens_count) * (1.0 / ens_count) + spread_scale * (
            spread - SOFTEN * pairs
        )
        scores[pl.ds(pl.multiple_of(row_tile * 8, 8), 8), lanes] = score
        return 0

    lax.fori_loop(0, (ROW_PAD // 8) * (weights.shape[1] // LANES), tile, 0)
    rounded = scores[:var_count, :deg_count].astype(jnp.bfloat16)
    for member in range(member_count):
        score_ref[member] = rounded
    for member in range(member_count):
        part = pulls[member * 4 * ROW_PAD : (member + 1) * 4 * ROW_PAD, :].astype(jnp.bfloat16)
        back = lax.dot_general(
            table, part, (((1,), (1,)), ((), ())), preferred_element_type=jnp.float32
        )
        halves = back.reshape(space_count, 2, BAND // 2, 4 * ROW_PAD)
        packed = jnp.concatenate(
            [
                halves[:, 0],
                halves[:, 1],
                jnp.zeros((space_count, BAND // 2, 3 * LANES - 8 * ROW_PAD), jnp.float32),
            ],
            axis=2,
        )
        grad_ref[:, member] = packed.astype(jnp.bfloat16)


def spectral(received, orders, fairness, member_count, var_count, deg_count):
    senders, band_rows, width = received.shape
    space_count = senders // member_count
    lat_count = space_count * band_rows
    deg_pad = -(-deg_count // LANES) * LANES
    ens_count = 2 * member_count
    grads, score = pl.pallas_call(
        functools.partial(spectral_kernel, fairness, member_count, var_count, deg_count),
        in_specs=[
            pl.BlockSpec(memory_space=pltpu.SMEM),
            pl.BlockSpec(memory_space=pltpu.VMEM),
        ],
        out_specs=[pl.BlockSpec(memory_space=pltpu.VMEM)] * 2,
        out_shape=[
            jax.ShapeDtypeStruct(
                (space_count, member_count, band_rows // 2, 3 * LANES), jnp.bfloat16
            ),
            jax.ShapeDtypeStruct((member_count, var_count, deg_count), jnp.bfloat16),
        ],
        scratch_shapes=[
            pltpu.VMEM((lat_count, deg_pad), jnp.float32),
            pltpu.VMEM((2 * (ens_count + 1) * ROW_PAD, lat_count), jnp.float32),
            pltpu.VMEM((2 * (ens_count + 1) * ROW_PAD, deg_pad), jnp.float32),
            pltpu.VMEM((2 * ens_count * ROW_PAD, deg_pad), jnp.float32),
            pltpu.VMEM((ROW_PAD, deg_pad), jnp.float32),
        ],
        compiler_params=pltpu.CompilerParams(vmem_limit_bytes=28 * MIB),
        cost_estimate=pl.CostEstimate(flops=COST, bytes_accessed=COST, transcendentals=0),
        name="spectral",
    )(orders, received.reshape(space_count, member_count, band_rows, width))
    return grads.reshape(senders, band_rows // 2, 3 * LANES), score


def backward_kernel(var_count, in_ref, table_ref, out_ref, staged, turned):
    step = pl.program_id(0)
    order_count = in_ref.shape[0]
    block = out_ref.shape[0]
    rows = 2 * var_count * BAND

    @pl.when(step == 0)
    def _():
        half = BAND // 2
        for part in range(3):
            staged[part] = (
                in_ref[:, :, part * LANES : (part + 1) * LANES]
                .astype(jnp.float32)
                .reshape(order_count * half, LANES)
            )
        for row in range(half):
            whole = jnp.concatenate(
                [staged[part, pl.ds(row, order_count, stride=half), :].T for part in range(3)],
                axis=0,
            )
            for high in range(2):
                for c in range(2):
                    for own in range(2):
                        source = (4 * high + 2 * c + own) * ROW_PAD
                        at = own * var_count * BAND + high * half + row
                        turned[c, pl.ds(at, var_count, stride=BAND), :] = whole[
                            source : source + var_count
                        ]

    at = pl.multiple_of(step * block, block)
    left = jnp.concatenate(
        [turned[0, pl.ds(at, block), :], turned[1, pl.ds(at, block), :]], axis=1
    ).astype(jnp.bfloat16)
    out_ref[...] = lax.dot_general(
        left, table_ref[...], (((1,), (1,)), ((), ())), preferred_element_type=jnp.float32
    ).astype(jnp.bfloat16)


def backward(received, table, own_count, var_count):
    order_count, half_rows, width = received.shape
    band_rows = 2 * half_rows
    lon_count = table.shape[0]
    rows = own_count * var_count * band_rows
    steps = 2
    return pl.pallas_call(
        functools.partial(backward_kernel, var_count),
        grid=(steps,),
        in_specs=[
            pl.BlockSpec((order_count, half_rows, width), lambda i: (0, 0, 0)),
            pl.BlockSpec((lon_count, 2 * order_count), lambda i: (0, 0)),
        ],
        out_specs=pl.BlockSpec((rows // steps, lon_count), lambda i: (i, 0)),
        out_shape=jax.ShapeDtypeStruct((rows, lon_count), jnp.bfloat16),
        scratch_shapes=[
            pltpu.VMEM((3, order_count * half_rows, LANES), jnp.float32),
            pltpu.VMEM((2, rows, order_count), jnp.float32),
        ],
        compiler_params=pltpu.CompilerParams(vmem_limit_bytes=16 * MIB),
        cost_estimate=pl.CostEstimate(flops=COST, bytes_accessed=COST, transcendentals=0),
        name="backward",
    )(received, table)


HOPS = ((0, 0), (0, 1), (0, 3), (1, 1), (1, 3), (1, 0), (0, 2), (1, 2))
RING = 4


def partner(member, hop, sign):
    half, spot = member // RING, member % RING
    return (half + hop[0]) % 2 * RING + (spot + sign * hop[1] + RING) % RING


def hop_pairs(hop, member_count):
    return [(i, partner(i, hop, 1)) for i in range(member_count)]


def regroup_kernel(var_count, sub_rows, ens_ref, truth_ref, *rest):
    outs, (target_ref, wide, paired) = rest[:-3], rest[-3:]
    member = lax.axis_index("member")

    def move(tile, goal, keep):
        for row in range(sub_rows):
            paired[tile, keep, pl.ds(row, var_count, stride=sub_rows), :] = wide[
                tile, pl.ds(goal * sub_rows + row, var_count, stride=BAND), :
            ]
        return paired[tile, keep].astype(jnp.bfloat16)

    for tile in range(wide.shape[0]):
        lanes = slice(tile * LANES, (tile + 1) * LANES)

        @pl.when(pl.program_id(1) == 0)
        def _(tile=tile, lanes=lanes):
            wide[tile] = truth_ref[:, lanes].astype(jnp.float32)
            target_ref[:, lanes] = move(tile, member, 0)

        wide[tile] = ens_ref[:, lanes].astype(jnp.float32)
        for place, hop in enumerate(HOPS):
            outs[place][0, :, lanes] = move(tile, partner(member, hop, 1), place)


def regroup(ens, truth, member_count):
    own_count, var_count, band_rows, lon_count = ens.shape
    sub_rows = band_rows // member_count
    width = 3 * LANES
    rows = var_count * sub_rows
    return pl.pallas_call(
        functools.partial(regroup_kernel, var_count, sub_rows),
        grid=(-(-lon_count // width), own_count),
        in_specs=[
            pl.BlockSpec((var_count * band_rows, width), lambda i, e: (e, i)),
            pl.BlockSpec((var_count * band_rows, width), lambda i, e: (0, i)),
        ],
        out_specs=[pl.BlockSpec((1, rows, width), lambda i, e: (e, 0, i))] * member_count
        + [pl.BlockSpec((rows, width), lambda i, e: (0, i))],
        out_shape=[
            jax.ShapeDtypeStruct((own_count, rows, lon_count), jnp.bfloat16)
            for _ in range(member_count)
        ]
        + [jax.ShapeDtypeStruct((rows, lon_count), jnp.bfloat16)],
        scratch_shapes=[
            pltpu.VMEM((width // LANES, var_count * band_rows, LANES), jnp.float32),
            pltpu.VMEM((width // LANES, member_count, rows, LANES), jnp.float32),
        ],
        compiler_params=pltpu.CompilerParams(vmem_limit_bytes=56 * MIB),
        cost_estimate=pl.CostEstimate(flops=COST, bytes_accessed=COST, transcendentals=0),
        name="regroup",
    )(ens.reshape(-1, lon_count), truth.reshape(-1, lon_count))


def sign(a, b):
    return jnp.minimum(jnp.maximum((a - b) * 2.0**70, -1.0), 1.0)


def count_kernel(*refs):
    parts, sum_ref = refs[:-1], refs[-1]
    per_part, row_count, width = parts[0].shape
    count = per_part * len(parts)

    def tile(at, rows, lane_at):
        lanes = slice(lane_at, lane_at + LANES)
        span = pl.ds(at, rows)
        wide = [
            parts[e // per_part][e % per_part, span, lanes].astype(jnp.float32) * 2.0**64
            for e in range(count)
        ]
        pieces = []
        for half in range(rows // 8):
            x = [value[8 * half : 8 * half + 8] for value in wide]
            sums = [jnp.zeros((8, LANES), jnp.float32)] * count
            for i in range(count):
                for j in range(i + 1, count):
                    s = sign(x[i], x[j])
                    sums[i] = sums[i] + s
                    sums[j] = sums[j] - s
            pieces.append(sums)
        for e in range(count):
            whole_sum = jnp.concatenate([sums[e] for sums in pieces], axis=0)
            sum_ref[e, span, lanes] = whole_sum.astype(jnp.bfloat16)

    over_tiles(tile, row_count, width)


def over_tiles(tile, row_count, width):
    whole = row_count // 16
    for lane_at in range(0, width, LANES):
        def body(index, _, lane_at=lane_at):
            tile(pl.multiple_of(index * 16, 16), 16, lane_at)
            return 0

        lax.fori_loop(0, whole, body, 0)
        if row_count % 16:
            tile(whole * 16, row_count % 16, lane_at)


def count_signs(parts):
    per_part, row_count, lon_count = parts[0].shape
    count = per_part * len(parts)
    width = GRID_WIDTH
    return pl.pallas_call(
        count_kernel,
        grid=(-(-lon_count // width),),
        in_specs=[pl.BlockSpec((per_part, row_count, width), lambda i: (0, 0, i))] * len(parts),
        out_specs=pl.BlockSpec((count, row_count, width), lambda i: (0, 0, i)),
        out_shape=jax.ShapeDtypeStruct((count, row_count, lon_count), jnp.bfloat16),
        compiler_params=pltpu.CompilerParams(vmem_limit_bytes=56 * MIB),
        cost_estimate=pl.CostEstimate(flops=COST, bytes_accessed=COST, transcendentals=0),
        name="count",
    )(*parts)


def grid_kernel(fairness, lon_count, first, part_count, known, weight_ref, truth_ref, *rest):
    parts, known_ref, carried = rest[:part_count], rest[part_count], rest[part_count + 1 : -3]
    grad_ref, score_ref, total = rest[-3:]
    step = pl.program_id(0)
    per_part, row_count, width = parts[0].shape
    ens_count = per_part * part_count
    sub_rows = grad_ref.shape[2]
    pull_scale = -fairness / (ens_count - 1)
    member = lax.axis_index("member")
    senders = [partner(member, hop, -1) for hop in HOPS]
    lat_start = (lax.axis_index("space") * part_count + member) * sub_rows
    which = lax.broadcasted_iota(jnp.int32, (8, LANES), 0) % sub_rows
    weight = jnp.full((8, LANES), weight_ref[lat_start], jnp.float32)
    for row in range(1, sub_rows):
        weight = jnp.where(which == row, weight_ref[lat_start + row], weight)

    @pl.when(step == 0)
    def _():
        total[...] = jnp.zeros_like(total)

    def tile(at, rows, lane_at):
        lanes = slice(lane_at, lane_at + LANES)
        span = pl.ds(at, rows)
        wide = [
            parts[e // per_part][e % per_part, span, lanes].astype(jnp.float32)
            for e in range(ens_count)
        ]
        goals = truth_ref[span, lanes].astype(jnp.float32)
        before = [known_ref[e, span, lanes].astype(jnp.float32) for e in range(known)]
        pieces = []
        for half in range(rows // 8):
            piece = slice(8 * half, 8 * half + 8)
            x = [value[piece] * 2.0**64 for value in wide]
            goal = goals[piece]
            y = goal * 2.0**64
            zero = jnp.zeros((8, LANES), jnp.float32)
            sums = [value[piece] for value in before] + [zero] * (ens_count - known)
            for i in range(ens_count):
                for j in range(max(i + 1, known), ens_count):
                    s = sign(x[i], x[j])
                    sums[i] = sums[i] + s
                    sums[j] = sums[j] - s
            score = zero
            toward_sum = zero
            grads = []
            for e in range(ens_count):
                toward = sign(x[e], y)
                toward_sum = toward_sum + toward
                pull = toward + pull_scale * sums[e]
                score = score + wide[e][piece] * pull
                grads.append(weight * pull)
            pieces.append(grads)
            score = (score - goal * toward_sum) * (1.0 / ens_count)
            lane = lax.broadcasted_iota(jnp.int32, (8, LANES), 1) + (
                (step + first) * width + lane_at
            )
            total[pl.ds(at + 8 * half, 8), :] += jnp.where(lane < lon_count, score, 0.0)
        for e in range(ens_count):
            whole_grad = jnp.concatenate([grads[e] for grads in pieces], axis=0)
            grad_ref[
                senders[e // per_part] * per_part + e % per_part,
                pl.ds(at // sub_rows, rows // sub_rows), :, lanes,
            ] = whole_grad.astype(jnp.bfloat16).reshape(rows // sub_rows, sub_rows, LANES)

    over_tiles(tile, row_count, width)

    @pl.when(step == pl.num_programs(0) - 1)
    def _():
        for row in range(sub_rows):
            rows = total[pl.ds(row, row_count // sub_rows, stride=sub_rows), :]
            result = jnp.sum(rows.T, axis=0, keepdims=True) * (1.0 / lon_count)
            score_ref[row : row + 1, :] = result + carried[1][row : row + 1, :] if carried else result


def grid_scores(parts, signs, target, weights, fairness, sub_rows, blocks, earlier=()):
    per_part, row_count, lon_count = parts[0].shape
    ens_count = per_part * len(parts)
    var_count = row_count // sub_rows
    width = GRID_WIDTH
    first, last = blocks
    return pl.pallas_call(
        functools.partial(grid_kernel, fairness, lon_count, first, len(parts), signs.shape[0]),
        grid=(last - first,),
        in_specs=[
            pl.BlockSpec(memory_space=pltpu.SMEM),
            pl.BlockSpec((row_count, width), lambda i: (0, i + first)),
        ]
        + [pl.BlockSpec((per_part, row_count, width), lambda i: (0, 0, i + first))] * len(parts)
        + [pl.BlockSpec((signs.shape[0], row_count, width), lambda i: (0, 0, i + first))]
        + [
            pl.BlockSpec(memory_space=pl.ANY),
            pl.BlockSpec((sub_rows, var_count), lambda i: (0, 0)),
        ][: len(earlier)],
        out_specs=[
            pl.BlockSpec((ens_count, var_count, sub_rows, width), lambda i: (0, 0, 0, i + first)),
            pl.BlockSpec((sub_rows, var_count), lambda i: (0, 0)),
        ],
        out_shape=[
            jax.ShapeDtypeStruct((ens_count, var_count, sub_rows, lon_count), jnp.bfloat16),
            jax.ShapeDtypeStruct((sub_rows, var_count), jnp.float32),
        ],
        scratch_shapes=[pltpu.VMEM((row_count, LANES), jnp.float32)],
        input_output_aliases={3 + len(parts): 0} if earlier else {},
        compiler_params=pltpu.CompilerParams(vmem_limit_bytes=56 * MIB),
        cost_estimate=pl.CostEstimate(flops=COST, bytes_accessed=COST, transcendentals=0),
        name="grid",
    )(weights, target, *parts, signs, *earlier)


def local(ens, truth, legendre, orders):
    own_count, var_count, band_rows, lon_count = ens.shape
    order_count = orders.shape[0]
    deg_count = legendre.shape[2]
    space_count = lax.axis_size("space")
    member_count = lax.axis_size("member")
    lat_count = band_rows * space_count
    ens_count = own_count * member_count
    sub_rows = band_rows // member_count
    fairness = 1.0 - FAIR_GAP / ens_count

    owners = ("space", "member")
    sent, table = forward(ens, truth, legendre, orders, member_count)
    received = lax.all_to_all(sent, owners, split_axis=0, concat_axis=0, tiled=True)

    *parts, target = regroup(ens, truth, member_count)
    for place, hop in enumerate(HOPS):
        if place:
            parts[place] = lax.ppermute(parts[place], "member", hop_pairs(hop, member_count))

    received, *parts[1:3] = lax.optimization_barrier((received, *parts[1:3]))
    grads, score = spectral(received, orders, fairness, member_count, var_count, deg_count)
    signs = count_signs(parts[:EARLY_PARTS])
    spec_score = lax.all_to_all(score, "member", split_axis=0, concat_axis=0, tiled=True)
    grads, spec_score, signs, *parts = lax.optimization_barrier(
        (grads, spec_score, signs, *parts)
    )
    returned = lax.all_to_all(grads, owners, split_axis=0, concat_axis=0, tiled=True)
    spec_score = spec_score.astype(jnp.float32)
    weights = jnp.asarray(latitude_weights(lat_count))
    grid_args = (parts, signs, target, weights, fairness, sub_rows)
    grid_grad, grid_rows = grid_scores(*grid_args, (0, -(-lon_count // GRID_WIDTH)))
    grid_grad = grid_grad.reshape(ens_count, var_count, 1, sub_rows, lon_count)
    grid_score = grid_rows.T.reshape(var_count, 1, sub_rows)
    spec_grad = backward(returned, table, own_count, var_count).reshape(ens.shape)
    return (grid_score, grid_grad, spec_score, spec_grad)


def solution(mesh):
    in_specs = (
        P("member", None, "space", None),
        P(None, "space", None),
        P("space", None, None),
        P(),
    )
    out_specs = (
        P(None, "space", "member"),
        P(None, None, "space", "member", None),
        P("space", None, None),
        P("member", None, "space", None),
    )
    return jax.shard_map(local, mesh=mesh, in_specs=in_specs, out_specs=out_specs, check_vma=False)
```

```python
import functools
import math

import jax
import jax.numpy as jnp
import numpy as np
from jax import lax
from jax.experimental import pallas as pl
from jax.experimental.pallas import tpu as pltpu
from jax.sharding import PartitionSpec as P

FAIR_GAP = 0.05
SOFTEN = 0.1
MIB = 1024 * 1024
COST = 1024
BAND = 16
LANES = 128
GRID_WIDTH = 2 * LANES
EARLY_PARTS = 6
FIELD_COPIES = 2
ROW_PAD = 40


def latitude_weights(lat_count):
    sine_values = np.sin((np.arange(lat_count) + 0.5) * (math.pi / lat_count))
    return (sine_values * (lat_count / sine_values.sum())).astype(np.float32)


def write_table(orders_ref, table_ref):
    lon_count = table_ref.shape[0]
    order_count = orders_ref.shape[1]
    chunk = 160
    norm = 1.0 / math.sqrt(lon_count)
    listed = orders_ref[...].astype(jnp.float32)

    def fill(step, _):
        start = pl.multiple_of(step * chunk, chunk)
        rows = lax.broadcasted_iota(jnp.int32, (chunk, order_count), 0) + start
        product = rows.astype(jnp.float32) * listed
        turns = jnp.floor(product * (1.0 / lon_count))
        phase = product - turns * lon_count
        quarter = jnp.floor(phase * (4.0 / lon_count) + 0.5)
        angle = (phase - quarter * (lon_count / 4.0)) * (2.0 * math.pi / lon_count)
        square = angle * angle
        sine = angle * (
            1.0 + square * (-1.0 / 6 + square * (1.0 / 120 + square * (-1.0 / 5040 + square / 362880)))
        )
        cosine = 1.0 + square * (
            -0.5 + square * (1.0 / 24 + square * (-1.0 / 720 + square * (1.0 / 40320)))
        )
        half = jnp.floor(quarter * 0.5)
        odd = quarter - 2.0 * half
        half_odd = half - 2.0 * jnp.floor(half * 0.5)
        flip = 1.0 - 2.0 * half_odd
        swap = odd > 0.5
        cos_value = jnp.where(swap, -sine, cosine) * flip
        sin_value = jnp.where(swap, cosine, sine) * flip
        table_ref[pl.ds(start, chunk), :order_count] = (cos_value * norm).astype(jnp.bfloat16)
        table_ref[pl.ds(start, chunk), order_count:] = (-sin_value * norm).astype(jnp.bfloat16)
        return 0

    lax.fori_loop(0, lon_count // chunk, fill, 0)


def forward_kernel(
    var_count, deg_count, orders_ref, ens_ref, truth_ref, leg_ref, out_ref, table_ref,
    staged, swapped, fields, truth_part, leg_part, sems,
):
    own_rows = 2 * var_count * BAND
    block = own_rows // FIELD_COPIES
    deg_part = leg_part.shape[0]
    var_part = truth_part.shape[0]
    leg_at = 2 * own_rows
    truth_at = leg_at + deg_part * BAND
    truth_rows = var_part * BAND
    used = truth_at + 2 * truth_rows
    order_count = orders_ref.shape[1]

    member = lax.axis_index("member")
    var_start = jnp.minimum(member * var_part, var_count - var_part)
    deg_start = jnp.minimum(member * deg_part, deg_count - deg_part)
    truth_copy = pltpu.make_async_copy(
        truth_ref.at[pl.ds(var_start, var_part)], truth_part, sems.at[0]
    )
    leg_copy = pltpu.make_async_copy(
        leg_ref.at[pl.ds(deg_start, deg_part)], leg_part, sems.at[1]
    )
    copies = [
        pltpu.make_async_copy(
            ens_ref.at[pl.ds(part * block, block)], fields.at[pl.ds(part * block, block)],
            sems.at[2 + part],
        )
        for part in range(FIELD_COPIES)
    ]
    truth_copy.start()
    for copy in copies:
        copy.start()
    leg_copy.start()
    write_table(orders_ref, table_ref)
    staged[used:, :] = jnp.zeros((staged.shape[0] - used, order_count), jnp.float32)
    truth_copy.wait()
    rows = jnp.dot(
        truth_part[...].reshape(truth_rows, -1), table_ref[...],
        preferred_element_type=jnp.float32,
    )
    staged[truth_at : truth_at + truth_rows, :] = rows[:, :order_count]
    staged[truth_at + truth_rows : used, :] = rows[:, order_count:]
    for part, copy in enumerate(copies):
        copy.wait()
        at = part * block
        rows = jnp.dot(
            fields[at : at + block, :], table_ref[...], preferred_element_type=jnp.float32
        )
        staged[at : at + block, :] = rows[:, :order_count]
        staged[own_rows + at : own_rows + at + block, :] = rows[:, order_count:]
    leg_copy.wait()
    staged[leg_at:truth_at, :] = (
        leg_part[...].reshape(deg_part * BAND, order_count).astype(jnp.float32)
    )

    width = staged.shape[0] // BAND
    for row in range(BAND):
        piece = staged[pl.ds(row, width, stride=BAND), :]
        swapped[0, pl.ds(row, order_count, stride=BAND), :] = piece[:LANES].T
        swapped[1, pl.ds(row, order_count, stride=BAND), :] = piece[LANES:].T
    for part in range(2):
        out_ref[:, :, part * LANES : (part + 1) * LANES] = (
            swapped[part].reshape(order_count, BAND, LANES).astype(jnp.bfloat16)
        )


def forward(ens, truth, legendre, orders, member_count):
    own_count, var_count, band_rows, lon_count = ens.shape
    order_count = orders.shape[0]
    deg_count = legendre.shape[2]
    deg_part = -(-deg_count // member_count)
    var_part = -(-var_count // member_count)
    rows = own_count * var_count * band_rows
    width = 2 * LANES
    return pl.pallas_call(
        functools.partial(forward_kernel, var_count, deg_count),
        in_specs=[pl.BlockSpec(memory_space=pltpu.VMEM)] + [pl.BlockSpec(memory_space=pl.ANY)] * 3,
        out_specs=[pl.BlockSpec(memory_space=pltpu.VMEM)] * 2,
        out_shape=[
            jax.ShapeDtypeStruct((order_count, band_rows, width), jnp.bfloat16),
            jax.ShapeDtypeStruct((lon_count, 2 * order_count), jnp.bfloat16),
        ],
        scratch_shapes=[
            pltpu.VMEM((width * band_rows, order_count), jnp.float32),
            pltpu.VMEM((2, order_count * band_rows, LANES), jnp.float32),
            pltpu.VMEM((rows, lon_count), jnp.bfloat16),
            pltpu.VMEM((var_part, band_rows, lon_count), jnp.bfloat16),
            pltpu.VMEM((deg_part, band_rows, order_count), jnp.bfloat16),
            pltpu.SemaphoreType.DMA((2 + FIELD_COPIES,)),
        ],
        compiler_params=pltpu.CompilerParams(vmem_limit_bytes=56 * MIB),
        cost_estimate=pl.CostEstimate(flops=COST, bytes_accessed=COST, transcendentals=0),
        name="forward",
    )(orders.reshape(1, -1), ens.reshape(rows, lon_count), truth,
      jnp.transpose(legendre, (2, 0, 1)))


def spectral_kernel(
    fairness, member_count, var_count, deg_count, orders_ref, in_ref, grad_ref, score_ref,
    weights, values, spectra, pulls, scores, split,
):
    ens_count = 2 * member_count
    deg_part = -(-deg_count // member_count)
    var_part = -(-var_count // member_count)
    lat_count = weights.shape[0]
    space_count = lat_count // BAND
    leg_at = 4 * var_count
    truth_at = leg_at + deg_part
    own_order = orders_ref[lax.axis_index("space") * member_count + lax.axis_index("member")]
    omega = jnp.where(own_order == 0, 1.0, 2.0).astype(jnp.float32)
    spread_scale = -fairness / (ens_count * (ens_count - 1))
    pull_scale = -fairness / (ens_count - 1)

    values[...] = jnp.zeros_like(values)
    weights[...] = jnp.zeros_like(weights)
    for member in range(member_count):
        block = in_ref[:, member].reshape(lat_count, 2 * LANES)
        deg_start = min(member * deg_part, deg_count - deg_part)
        weights[:, deg_start : deg_start + deg_part] = block[:, leg_at : leg_at + deg_part].astype(
            jnp.float32
        )
        turned = block.astype(jnp.float32).T
        var_start = min(member * var_part, var_count - var_part)
        for c in range(2):
            for own in range(2):
                at = (c * (ens_count + 1) + 2 * member + own) * ROW_PAD
                source = (2 * c + own) * var_count
                values[at : at + var_count, :] = turned[source : source + var_count]
            at = (c * (ens_count + 1) + ens_count) * ROW_PAD + var_start
            source = truth_at + c * var_part
            values[at : at + var_part, :] = turned[source : source + var_part]
    table = weights[...].astype(jnp.bfloat16)
    spectra[...] = jnp.dot(
        values[...].astype(jnp.bfloat16), table, preferred_element_type=jnp.float32
    )

    def tile(index, _):
        lane_tile = index % (weights.shape[1] // LANES)
        row_tile = index // (weights.shape[1] // LANES)
        lanes = pl.ds(pl.multiple_of(lane_tile * LANES, LANES), LANES)

        def load(c, e):
            at = (c * (ens_count + 1) + e) * ROW_PAD
            return spectra[pl.ds(pl.multiple_of(at + row_tile * 8, 8), 8), lanes]

        def pair(a, b):
            d0 = a[0] - b[0]
            d1 = a[1] - b[1]
            square = d0 * d0 + d1 * d1 + SOFTEN * SOFTEN
            inverse = lax.rsqrt(square)
            return square * inverse, d0 * inverse, d1 * inverse

        z = [(load(0, e), load(1, e)) for e in range(ens_count)]
        y = (load(0, ens_count), load(1, ens_count))
        zero = jnp.zeros((8, LANES), jnp.float32)
        pull = [[zero, zero] for _ in range(ens_count)]
        spread = zero
        for i in range(ens_count):
            for j in range(i + 1, ens_count):
                size, u0, u1 = pair(z[i], z[j])
                spread = spread + size
                pull[i][0] = pull[i][0] + u0
                pull[i][1] = pull[i][1] + u1
                pull[j][0] = pull[j][0] - u0
                pull[j][1] = pull[j][1] - u1
        error = zero
        for e in range(ens_count):
            size, u0, u1 = pair(z[e], y)
            error = error + size
            for c, u in enumerate((u0, u1)):
                at = ((e // 2) * 4 + 2 * c + e % 2) * ROW_PAD
                pulls[pl.ds(pl.multiple_of(at + row_tile * 8, 8), 8), lanes] = omega * (
                    u + pull_scale * pull[e][c]
                )
        pairs = ens_count * (ens_count - 1) // 2
        score = (error - SOFTEN * ens_count) * (1.0 / ens_count) + spread_scale * (
            spread - SOFTEN * pairs
        )
        scores[pl.ds(pl.multiple_of(row_tile * 8, 8), 8), lanes] = score
        return 0

    lax.fori_loop(0, (ROW_PAD // 8) * (weights.shape[1] // LANES), tile, 0)
    rounded = scores[:var_count, :deg_count].astype(jnp.bfloat16)
    for member in range(member_count):
        score_ref[member] = rounded
    half = BAND // 2
    for member in range(member_count):
        part = jnp.concatenate(
            [
                pulls[at : at + var_count, :]
                for at in range(4 * member * ROW_PAD, 4 * (member + 1) * ROW_PAD, ROW_PAD)
            ],
            axis=0,
        ).astype(jnp.bfloat16)
        back = lax.dot_general(
            table, part, (((1,), (1,)), ((), ())), preferred_element_type=jnp.float32
        )
        split[0] = back[:, :LANES]
        split[1, :, : 4 * var_count - LANES] = back[:, LANES:]
        pieces = []
        for row in range(half):
            rows = pl.ds(row, lat_count // half, stride=half)
            pieces += [split[0, rows, :], split[1, rows, :][:, : 4 * var_count - LANES]]
        packed = jnp.concatenate(pieces, axis=1).astype(jnp.bfloat16)
        grad_ref[:, member] = packed.reshape(space_count, 2, half * 4 * var_count)


def spectral(received, orders, fairness, member_count, var_count, deg_count):
    senders, band_rows, width = received.shape
    space_count = senders // member_count
    lat_count = space_count * band_rows
    deg_pad = -(-deg_count // LANES) * LANES
    ens_count = 2 * member_count
    grads, score = pl.pallas_call(
        functools.partial(spectral_kernel, fairness, member_count, var_count, deg_count),
        in_specs=[
            pl.BlockSpec(memory_space=pltpu.SMEM),
            pl.BlockSpec(memory_space=pltpu.VMEM),
        ],
        out_specs=[pl.BlockSpec(memory_space=pltpu.VMEM)] * 2,
        out_shape=[
            jax.ShapeDtypeStruct(
                (space_count, member_count, 2, band_rows // 2 * 4 * var_count), jnp.bfloat16
            ),
            jax.ShapeDtypeStruct((member_count, var_count, deg_count), jnp.bfloat16),
        ],
        scratch_shapes=[
            pltpu.VMEM((lat_count, deg_pad), jnp.float32),
            pltpu.VMEM((2 * (ens_count + 1) * ROW_PAD, lat_count), jnp.float32),
            pltpu.VMEM((2 * (ens_count + 1) * ROW_PAD, deg_pad), jnp.float32),
            pltpu.VMEM((2 * ens_count * ROW_PAD, deg_pad), jnp.float32),
            pltpu.VMEM((ROW_PAD, deg_pad), jnp.float32),
            pltpu.VMEM((2, lat_count, LANES), jnp.float32),
        ],
        compiler_params=pltpu.CompilerParams(vmem_limit_bytes=28 * MIB),
        cost_estimate=pl.CostEstimate(flops=COST, bytes_accessed=COST, transcendentals=0),
        name="spectral",
    )(orders, received.reshape(space_count, member_count, band_rows, width))
    return grads.reshape(senders, 2, band_rows // 2 * 4 * var_count), score


def backward_kernel(var_count, in_ref, table_ref, out_ref, staged, turned):
    step = pl.program_id(0)
    order_count = in_ref.shape[0]
    block = out_ref.shape[0]
    rows = 2 * var_count * BAND

    @pl.when(step == 0)
    def _():
        half = BAND // 2
        tiles = staged.shape[0]
        for part in range(tiles):
            staged[part] = (
                in_ref[:, :, part * LANES : (part + 1) * LANES]
                .reshape(2 * order_count, LANES)
                .astype(jnp.float32)
            )
        for high in range(2):
            whole = jnp.concatenate(
                [staged[part, pl.ds(high, order_count, stride=2), :].T for part in range(tiles)],
                axis=0,
            )
            for low in range(half):
                for c in range(2):
                    for own in range(2):
                        source = (4 * low + 2 * c + own) * var_count
                        at = own * var_count * BAND + high * half + low
                        turned[c, pl.ds(at, var_count, stride=BAND), :] = whole[
                            source : source + var_count
                        ]

    at = pl.multiple_of(step * block, block)
    left = jnp.concatenate(
        [turned[0, pl.ds(at, block), :], turned[1, pl.ds(at, block), :]], axis=1
    ).astype(jnp.bfloat16)
    out_ref[...] = lax.dot_general(
        left, table_ref[...], (((1,), (1,)), ((), ())), preferred_element_type=jnp.float32
    ).astype(jnp.bfloat16)


def backward(received, table, own_count, var_count):
    order_count, _, width = received.shape
    band_rows = 2 * width // (2 * own_count * var_count)
    lon_count = table.shape[0]
    rows = own_count * var_count * band_rows
    steps = 2
    return pl.pallas_call(
        functools.partial(backward_kernel, var_count),
        grid=(steps,),
        in_specs=[
            pl.BlockSpec((order_count, 2, width), lambda i: (0, 0, 0)),
            pl.BlockSpec((lon_count, 2 * order_count), lambda i: (0, 0)),
        ],
        out_specs=pl.BlockSpec((rows // steps, lon_count), lambda i: (i, 0)),
        out_shape=jax.ShapeDtypeStruct((rows, lon_count), jnp.bfloat16),
        scratch_shapes=[
            pltpu.VMEM((width // LANES, 2 * order_count, LANES), jnp.float32),
            pltpu.VMEM((2, rows, order_count), jnp.float32),
        ],
        compiler_params=pltpu.CompilerParams(vmem_limit_bytes=16 * MIB),
        cost_estimate=pl.CostEstimate(flops=COST, bytes_accessed=COST, transcendentals=0),
        name="backward",
    )(received, table)


HOPS = ((0, 0), (0, 1), (0, 3), (1, 1), (1, 3), (1, 0), (0, 2), (1, 2))
RING = 4


def partner(member, hop, sign):
    half, spot = member // RING, member % RING
    return (half + hop[0]) % 2 * RING + (spot + sign * hop[1] + RING) % RING


def hop_pairs(hop, member_count):
    return [(i, partner(i, hop, 1)) for i in range(member_count)]


def regroup_kernel(var_count, sub_rows, ens_ref, truth_ref, *rest):
    outs, (target_ref, wide, paired) = rest[:-3], rest[-3:]
    member = lax.axis_index("member")

    def move(tile, goal, keep):
        for row in range(sub_rows):
            paired[tile, keep, pl.ds(row, var_count, stride=sub_rows), :] = wide[
                tile, pl.ds(goal * sub_rows + row, var_count, stride=BAND), :
            ]
        return paired[tile, keep].astype(jnp.bfloat16)

    for tile in range(wide.shape[0]):
        lanes = slice(tile * LANES, (tile + 1) * LANES)

        @pl.when(pl.program_id(1) == 0)
        def _(tile=tile, lanes=lanes):
            wide[tile] = truth_ref[:, lanes].astype(jnp.float32)
            target_ref[:, lanes] = move(tile, member, 0)

        wide[tile] = ens_ref[:, lanes].astype(jnp.float32)
        for place, hop in enumerate(HOPS):
            outs[place][0, :, lanes] = move(tile, partner(member, hop, 1), place)


def regroup(ens, truth, member_count):
    own_count, var_count, band_rows, lon_count = ens.shape
    sub_rows = band_rows // member_count
    width = 3 * LANES
    rows = var_count * sub_rows
    return pl.pallas_call(
        functools.partial(regroup_kernel, var_count, sub_rows),
        grid=(-(-lon_count // width), own_count),
        in_specs=[
            pl.BlockSpec((var_count * band_rows, width), lambda i, e: (e, i)),
            pl.BlockSpec((var_count * band_rows, width), lambda i, e: (0, i)),
        ],
        out_specs=[pl.BlockSpec((1, rows, width), lambda i, e: (e, 0, i))] * member_count
        + [pl.BlockSpec((rows, width), lambda i, e: (0, i))],
        out_shape=[
            jax.ShapeDtypeStruct((own_count, rows, lon_count), jnp.bfloat16)
            for _ in range(member_count)
        ]
        + [jax.ShapeDtypeStruct((rows, lon_count), jnp.bfloat16)],
        scratch_shapes=[
            pltpu.VMEM((width // LANES, var_count * band_rows, LANES), jnp.float32),
            pltpu.VMEM((width // LANES, member_count, rows, LANES), jnp.float32),
        ],
        compiler_params=pltpu.CompilerParams(vmem_limit_bytes=56 * MIB),
        cost_estimate=pl.CostEstimate(flops=COST, bytes_accessed=COST, transcendentals=0),
        name="regroup",
    )(ens.reshape(-1, lon_count), truth.reshape(-1, lon_count))


def stretch(x):
    scaled = x * 2.0**124
    return scaled + jnp.minimum(jnp.maximum(scaled * 2.0**10, -(2.0**24)), 2.0**24)


def sign(a, b):
    return jnp.minimum(jnp.maximum(a - b, -1.0), 1.0)


def count_kernel(*refs):
    parts, sum_ref = refs[:-1], refs[-1]
    per_part, row_count, width = parts[0].shape
    count = per_part * len(parts)

    def tile(at, rows, lane_at):
        lanes = slice(lane_at, lane_at + LANES)
        span = pl.ds(at, rows)
        wide = [
            stretch(parts[e // per_part][e % per_part, span, lanes].astype(jnp.float32))
            for e in range(count)
        ]
        pieces = []
        for half in range(rows // 8):
            x = [value[8 * half : 8 * half + 8] for value in wide]
            sums = [jnp.zeros((8, LANES), jnp.float32)] * count
            for i in range(count):
                for j in range(i + 1, count):
                    s = sign(x[i], x[j])
                    sums[i] = sums[i] + s
                    sums[j] = sums[j] - s
            pieces.append(sums)
        for e in range(count):
            whole_sum = jnp.concatenate([sums[e] for sums in pieces], axis=0)
            sum_ref[e, span, lanes] = whole_sum.astype(jnp.bfloat16)

    over_tiles(tile, row_count, width)


def over_tiles(tile, row_count, width):
    whole = row_count // 16
    for lane_at in range(0, width, LANES):
        def body(index, _, lane_at=lane_at):
            tile(pl.multiple_of(index * 16, 16), 16, lane_at)
            return 0

        lax.fori_loop(0, whole, body, 0)
        if row_count % 16:
            tile(whole * 16, row_count % 16, lane_at)


def count_signs(parts):
    per_part, row_count, lon_count = parts[0].shape
    count = per_part * len(parts)
    width = GRID_WIDTH
    return pl.pallas_call(
        count_kernel,
        grid=(-(-lon_count // width),),
        in_specs=[pl.BlockSpec((per_part, row_count, width), lambda i: (0, 0, i))] * len(parts),
        out_specs=pl.BlockSpec((count, row_count, width), lambda i: (0, 0, i)),
        out_shape=jax.ShapeDtypeStruct((count, row_count, lon_count), jnp.bfloat16),
        compiler_params=pltpu.CompilerParams(vmem_limit_bytes=56 * MIB),
        cost_estimate=pl.CostEstimate(flops=COST, bytes_accessed=COST, transcendentals=0),
        name="count",
    )(*parts)


def grid_kernel(fairness, lon_count, known, weight_ref, truth_ref, spec_ref, *rest):
    part_count = spec_ref.shape[0]
    parts, known_ref = rest[:part_count], rest[part_count]
    grad_ref, score_ref, wide_ref, total, mixed = rest[part_count + 1 :]
    step = pl.program_id(0)
    per_part, row_count, width = parts[0].shape
    ens_count = per_part * part_count
    sub_rows = grad_ref.shape[2]
    pull_scale = -fairness / (ens_count - 1)
    member = lax.axis_index("member")
    senders = [partner(member, hop, -1) for hop in HOPS]
    lat_start = (lax.axis_index("space") * part_count + member) * sub_rows
    which = lax.broadcasted_iota(jnp.int32, (8, LANES), 0) % sub_rows
    weight = jnp.full((8, LANES), weight_ref[lat_start], jnp.float32)
    for row in range(1, sub_rows):
        weight = jnp.where(which == row, weight_ref[lat_start + row], weight)

    @pl.when(step == 0)
    def _():
        total[...] = jnp.zeros_like(total)
        spec_count, spec_vars, degrees = spec_ref.shape
        for lane_at in range(0, degrees, LANES):
            size = min(LANES, degrees - lane_at)
            lanes = slice(lane_at, lane_at + size)
            for order in range(spec_count):
                mixed[pl.ds(order, spec_vars, stride=spec_count), :size] = spec_ref[
                    order, :, lanes
                ].astype(jnp.float32)
            wide_ref[:, :, lanes] = mixed[:, :size].reshape(spec_vars, spec_count, size)

    def tile(at, rows, lane_at):
        lanes = slice(lane_at, lane_at + LANES)
        span = pl.ds(at, rows)
        wide = [
            parts[e // per_part][e % per_part, span, lanes].astype(jnp.float32)
            for e in range(ens_count)
        ]
        goals = truth_ref[span, lanes].astype(jnp.float32)
        before = [known_ref[e, span, lanes].astype(jnp.float32) for e in range(known)]
        pieces = []
        for half in range(rows // 8):
            piece = slice(8 * half, 8 * half + 8)
            x = [stretch(value[piece]) for value in wide]
            goal = goals[piece]
            y = stretch(goal)
            zero = jnp.zeros((8, LANES), jnp.float32)
            sums = [value[piece] for value in before] + [zero] * (ens_count - known)
            for i in range(ens_count):
                for j in range(max(i + 1, known), ens_count):
                    s = sign(x[i], x[j])
                    sums[i] = sums[i] + s
                    sums[j] = sums[j] - s
            score = zero
            toward_sum = zero
            grads = []
            for e in range(ens_count):
                toward = sign(x[e], y)
                toward_sum = toward_sum + toward
                pull = toward + pull_scale * sums[e]
                score = score + wide[e][piece] * pull
                grads.append(weight * pull)
            pieces.append(grads)
            score = (score - goal * toward_sum) * (1.0 / ens_count)
            lane = lax.broadcasted_iota(jnp.int32, (8, LANES), 1) + (
                step * width + lane_at
            )
            total[pl.ds(at + 8 * half, 8), :] += jnp.where(lane < lon_count, score, 0.0)
        for e in range(ens_count):
            whole_grad = jnp.concatenate([grads[e] for grads in pieces], axis=0)
            grad_ref[
                senders[e // per_part] * per_part + e % per_part,
                pl.ds(at // sub_rows, rows // sub_rows), :, lanes,
            ] = whole_grad.astype(jnp.bfloat16).reshape(rows // sub_rows, sub_rows, LANES)

    over_tiles(tile, row_count, width)

    @pl.when(step == pl.num_programs(0) - 1)
    def _():
        for row in range(sub_rows):
            rows = total[pl.ds(row, row_count // sub_rows, stride=sub_rows), :]
            result = jnp.sum(rows.T, axis=0, keepdims=True) * (1.0 / lon_count)
            score_ref[row : row + 1, :] = result


def grid_scores(parts, signs, target, weights, spec_score, fairness, sub_rows):
    per_part, row_count, lon_count = parts[0].shape
    ens_count = per_part * len(parts)
    var_count = row_count // sub_rows
    order_count, _, deg_count = spec_score.shape
    width = GRID_WIDTH
    return pl.pallas_call(
        functools.partial(grid_kernel, fairness, lon_count, signs.shape[0]),
        grid=(-(-lon_count // width),),
        in_specs=[
            pl.BlockSpec(memory_space=pltpu.SMEM),
            pl.BlockSpec((row_count, width), lambda i: (0, i)),
            pl.BlockSpec((order_count, var_count, deg_count), lambda i: (0, 0, 0)),
        ]
        + [pl.BlockSpec((per_part, row_count, width), lambda i: (0, 0, i))] * len(parts)
        + [pl.BlockSpec((signs.shape[0], row_count, width), lambda i: (0, 0, i))],
        out_specs=[
            pl.BlockSpec((ens_count, var_count, sub_rows, width), lambda i: (0, 0, 0, i)),
            pl.BlockSpec((sub_rows, var_count), lambda i: (0, 0)),
            pl.BlockSpec((var_count, order_count, deg_count), lambda i: (0, 0, 0)),
        ],
        out_shape=[
            jax.ShapeDtypeStruct((ens_count, var_count, sub_rows, lon_count), jnp.bfloat16),
            jax.ShapeDtypeStruct((sub_rows, var_count), jnp.float32),
            jax.ShapeDtypeStruct((var_count, order_count, deg_count), jnp.float32),
        ],
        scratch_shapes=[
            pltpu.VMEM((row_count, LANES), jnp.float32),
            pltpu.VMEM((var_count * order_count, LANES), jnp.float32),
        ],
        compiler_params=pltpu.CompilerParams(vmem_limit_bytes=56 * MIB),
        cost_estimate=pl.CostEstimate(flops=COST, bytes_accessed=COST, transcendentals=0),
        name="grid",
    )(weights, target, spec_score, *parts, signs)


def local(ens, truth, legendre, orders):
    own_count, var_count, band_rows, lon_count = ens.shape
    order_count = orders.shape[0]
    deg_count = legendre.shape[2]
    space_count = lax.axis_size("space")
    member_count = lax.axis_size("member")
    lat_count = band_rows * space_count
    ens_count = own_count * member_count
    sub_rows = band_rows // member_count
    fairness = 1.0 - FAIR_GAP / ens_count

    owners = ("space", "member")
    sent, table = forward(ens, truth, legendre, orders, member_count)
    received = lax.all_to_all(sent, owners, split_axis=0, concat_axis=0, tiled=True)

    *parts, target = regroup(ens, truth, member_count)
    for place, hop in enumerate(HOPS):
        if place:
            parts[place] = lax.ppermute(parts[place], "member", hop_pairs(hop, member_count))

    received, *parts[1:3] = lax.optimization_barrier((received, *parts[1:3]))
    grads, score = spectral(received, orders, fairness, member_count, var_count, deg_count)
    signs = count_signs(parts[:EARLY_PARTS])
    spec_score = lax.all_to_all(score, "member", split_axis=0, concat_axis=0, tiled=True)
    grads, spec_score, signs, *parts = lax.optimization_barrier(
        (grads, spec_score, signs, *parts)
    )
    returned = lax.all_to_all(grads, owners, split_axis=0, concat_axis=0, tiled=True)
    weights = jnp.asarray(latitude_weights(lat_count))
    grid_grad, grid_rows, spec_score = grid_scores(
        parts, signs, target, weights, spec_score, fairness, sub_rows
    )
    spec_score = spec_score.swapaxes(0, 1)
    grid_grad = grid_grad.reshape(ens_count, var_count, 1, sub_rows, lon_count)
    grid_score = grid_rows.T.reshape(var_count, 1, sub_rows)
    spec_grad = backward(returned, table, own_count, var_count).reshape(ens.shape)
    return (grid_score, grid_grad, spec_score, spec_grad)


def solution(mesh):
    in_specs = (
        P("member", None, "space", None),
        P(None, "space", None),
        P("space", None, None),
        P(),
    )
    out_specs = (
        P(None, "space", "member"),
        P(None, None, "space", "member", None),
        P("space", None, None),
        P("member", None, "space", None),
    )
    return jax.shard_map(local, mesh=mesh, in_specs=in_specs, out_specs=out_specs, check_vma=False)
```

```python
import functools
import math

import jax
import jax.numpy as jnp
import numpy as np
from jax import lax
from jax.experimental import pallas as pl
from jax.experimental.pallas import tpu as pltpu
from jax.sharding import PartitionSpec as P

FAIR_GAP = 0.05
SOFTEN = 0.1
MIB = 1024 * 1024
COST = 1024
BAND = 16
LANES = 128
GRID_WIDTH = 2 * LANES
EARLY_PARTS = 6
FIELD_COPIES = 2
ROW_PAD = 40


def latitude_weights(lat_count):
    sine_values = np.sin((np.arange(lat_count) + 0.5) * (math.pi / lat_count))
    return (sine_values * (lat_count / sine_values.sum())).astype(np.float32)


def write_table(orders_ref, table_ref):
    lon_count = table_ref.shape[0]
    order_count = orders_ref.shape[1]
    chunk = 160
    norm = 1.0 / math.sqrt(lon_count)
    listed = orders_ref[...].astype(jnp.float32)

    def fill(step, _):
        start = pl.multiple_of(step * chunk, chunk)
        rows = lax.broadcasted_iota(jnp.int32, (chunk, order_count), 0) + start
        product = rows.astype(jnp.float32) * listed
        turns = jnp.floor(product * (1.0 / lon_count))
        phase = product - turns * lon_count
        quarter = jnp.floor(phase * (4.0 / lon_count) + 0.5)
        angle = (phase - quarter * (lon_count / 4.0)) * (2.0 * math.pi / lon_count)
        square = angle * angle
        sine = angle * (
            1.0 + square * (-1.0 / 6 + square * (1.0 / 120 + square * (-1.0 / 5040 + square / 362880)))
        )
        cosine = 1.0 + square * (
            -0.5 + square * (1.0 / 24 + square * (-1.0 / 720 + square * (1.0 / 40320)))
        )
        half = jnp.floor(quarter * 0.5)
        odd = quarter - 2.0 * half
        half_odd = half - 2.0 * jnp.floor(half * 0.5)
        flip = 1.0 - 2.0 * half_odd
        swap = odd > 0.5
        cos_value = jnp.where(swap, -sine, cosine) * flip
        sin_value = jnp.where(swap, cosine, sine) * flip
        table_ref[pl.ds(start, chunk), :order_count] = (cos_value * norm).astype(jnp.bfloat16)
        table_ref[pl.ds(start, chunk), order_count:] = (-sin_value * norm).astype(jnp.bfloat16)
        return 0

    lax.fori_loop(0, lon_count // chunk, fill, 0)


def forward_kernel(
    var_count, deg_count, orders_ref, ens_ref, truth_ref, leg_ref, out_ref, table_ref,
    staged, swapped, fields, truth_part, leg_part, sems,
):
    own_rows = 2 * var_count * BAND
    block = own_rows // FIELD_COPIES
    deg_part = leg_part.shape[0]
    var_part = truth_part.shape[0]
    leg_at = 2 * own_rows
    truth_at = leg_at + deg_part * BAND
    truth_rows = var_part * BAND
    used = truth_at + 2 * truth_rows
    order_count = orders_ref.shape[1]

    member = lax.axis_index("member")
    var_start = jnp.minimum(member * var_part, var_count - var_part)
    deg_start = jnp.minimum(member * deg_part, deg_count - deg_part)
    truth_copy = pltpu.make_async_copy(
        truth_ref.at[pl.ds(var_start, var_part)], truth_part, sems.at[0]
    )
    leg_copy = pltpu.make_async_copy(
        leg_ref.at[pl.ds(deg_start, deg_part)], leg_part, sems.at[1]
    )
    copies = [
        pltpu.make_async_copy(
            ens_ref.at[pl.ds(part * block, block)], fields.at[pl.ds(part * block, block)],
            sems.at[2 + part],
        )
        for part in range(FIELD_COPIES)
    ]
    truth_copy.start()
    for copy in copies:
        copy.start()
    leg_copy.start()
    write_table(orders_ref, table_ref)
    staged[used:, :] = jnp.zeros((staged.shape[0] - used, order_count), jnp.float32)
    truth_copy.wait()
    rows = jnp.dot(
        truth_part[...].reshape(truth_rows, -1), table_ref[...],
        preferred_element_type=jnp.float32,
    )
    staged[truth_at : truth_at + truth_rows, :] = rows[:, :order_count]
    staged[truth_at + truth_rows : used, :] = rows[:, order_count:]
    for part, copy in enumerate(copies):
        copy.wait()
        at = part * block
        rows = jnp.dot(
            fields[at : at + block, :], table_ref[...], preferred_element_type=jnp.float32
        )
        staged[at : at + block, :] = rows[:, :order_count]
        staged[own_rows + at : own_rows + at + block, :] = rows[:, order_count:]
    leg_copy.wait()
    staged[leg_at:truth_at, :] = (
        leg_part[...].reshape(deg_part * BAND, order_count).astype(jnp.float32)
    )

    width = staged.shape[0] // BAND
    for row in range(BAND):
        piece = staged[pl.ds(row, width, stride=BAND), :]
        swapped[0, pl.ds(row, order_count, stride=BAND), :] = piece[:LANES].T
        swapped[1, pl.ds(row, order_count, stride=BAND), :] = piece[LANES:].T
    for part in range(2):
        out_ref[:, :, part * LANES : (part + 1) * LANES] = (
            swapped[part].reshape(order_count, BAND, LANES).astype(jnp.bfloat16)
        )


def forward(ens, truth, legendre, orders, member_count):
    own_count, var_count, band_rows, lon_count = ens.shape
    order_count = orders.shape[0]
    deg_count = legendre.shape[2]
    deg_part = -(-deg_count // member_count)
    var_part = -(-var_count // member_count)
    rows = own_count * var_count * band_rows
    width = 2 * LANES
    return pl.pallas_call(
        functools.partial(forward_kernel, var_count, deg_count),
        in_specs=[pl.BlockSpec(memory_space=pltpu.VMEM)] + [pl.BlockSpec(memory_space=pl.ANY)] * 3,
        out_specs=[pl.BlockSpec(memory_space=pltpu.VMEM)] * 2,
        out_shape=[
            jax.ShapeDtypeStruct((order_count, band_rows, width), jnp.bfloat16),
            jax.ShapeDtypeStruct((lon_count, 2 * order_count), jnp.bfloat16),
        ],
        scratch_shapes=[
            pltpu.VMEM((width * band_rows, order_count), jnp.float32),
            pltpu.VMEM((2, order_count * band_rows, LANES), jnp.float32),
            pltpu.VMEM((rows, lon_count), jnp.bfloat16),
            pltpu.VMEM((var_part, band_rows, lon_count), jnp.bfloat16),
            pltpu.VMEM((deg_part, band_rows, order_count), jnp.bfloat16),
            pltpu.SemaphoreType.DMA((2 + FIELD_COPIES,)),
        ],
        compiler_params=pltpu.CompilerParams(vmem_limit_bytes=56 * MIB),
        cost_estimate=pl.CostEstimate(flops=COST, bytes_accessed=COST, transcendentals=0),
        name="forward",
    )(orders.reshape(1, -1), ens.reshape(rows, lon_count), truth,
      jnp.transpose(legendre, (2, 0, 1)))


def spectral_kernel(
    fairness, member_count, var_count, deg_count, orders_ref, in_ref, grad_ref, score_ref,
    weights, values, spectra, pulls, scores, split,
):
    ens_count = 2 * member_count
    deg_part = -(-deg_count // member_count)
    var_part = -(-var_count // member_count)
    lat_count = weights.shape[0]
    space_count = lat_count // BAND
    leg_at = 4 * var_count
    truth_at = leg_at + deg_part
    own_order = orders_ref[lax.axis_index("space") * member_count + lax.axis_index("member")]
    omega = jnp.where(own_order == 0, 1.0, 2.0).astype(jnp.float32)
    spread_scale = -fairness / (ens_count * (ens_count - 1))
    pull_scale = -fairness / (ens_count - 1)

    values[...] = jnp.zeros_like(values)
    weights[...] = jnp.zeros_like(weights)
    for member in range(member_count):
        block = in_ref[:, member].reshape(lat_count, 2 * LANES)
        deg_start = min(member * deg_part, deg_count - deg_part)
        weights[:, deg_start : deg_start + deg_part] = block[:, leg_at : leg_at + deg_part].astype(
            jnp.float32
        )
        turned = block.astype(jnp.float32).T
        var_start = min(member * var_part, var_count - var_part)
        for c in range(2):
            for own in range(2):
                at = (c * (ens_count + 1) + 2 * member + own) * ROW_PAD
                source = (2 * c + own) * var_count
                values[at : at + var_count, :] = turned[source : source + var_count]
            at = (c * (ens_count + 1) + ens_count) * ROW_PAD + var_start
            source = truth_at + c * var_part
            values[at : at + var_part, :] = turned[source : source + var_part]
    table = weights[...].astype(jnp.bfloat16)
    spectra[...] = jnp.dot(
        values[...].astype(jnp.bfloat16), table, preferred_element_type=jnp.float32
    )

    def tile(index, _):
        lane_tile = index % (weights.shape[1] // LANES)
        row_tile = index // (weights.shape[1] // LANES)
        lanes = pl.ds(pl.multiple_of(lane_tile * LANES, LANES), LANES)

        def load(c, e):
            at = (c * (ens_count + 1) + e) * ROW_PAD
            return spectra[pl.ds(pl.multiple_of(at + row_tile * 8, 8), 8), lanes]

        def pair(a, b):
            d0 = a[0] - b[0]
            d1 = a[1] - b[1]
            square = d0 * d0 + d1 * d1 + SOFTEN * SOFTEN
            inverse = lax.rsqrt(square)
            return square * inverse, d0 * inverse, d1 * inverse

        z = [(load(0, e), load(1, e)) for e in range(ens_count)]
        y = (load(0, ens_count), load(1, ens_count))
        zero = jnp.zeros((8, LANES), jnp.float32)
        pull = [[zero, zero] for _ in range(ens_count)]
        spread = zero
        for i in range(ens_count):
            for j in range(i + 1, ens_count):
                size, u0, u1 = pair(z[i], z[j])
                spread = spread + size
                pull[i][0] = pull[i][0] + u0
                pull[i][1] = pull[i][1] + u1
                pull[j][0] = pull[j][0] - u0
                pull[j][1] = pull[j][1] - u1
        error = zero
        for e in range(ens_count):
            size, u0, u1 = pair(z[e], y)
            error = error + size
            for c, u in enumerate((u0, u1)):
                at = ((e // 2) * 4 + 2 * c + e % 2) * ROW_PAD
                pulls[pl.ds(pl.multiple_of(at + row_tile * 8, 8), 8), lanes] = omega * (
                    u + pull_scale * pull[e][c]
                )
        pairs = ens_count * (ens_count - 1) // 2
        score = (error - SOFTEN * ens_count) * (1.0 / ens_count) + spread_scale * (
            spread - SOFTEN * pairs
        )
        scores[pl.ds(pl.multiple_of(row_tile * 8, 8), 8), lanes] = score
        return 0

    lax.fori_loop(0, (ROW_PAD // 8) * (weights.shape[1] // LANES), tile, 0)
    rounded = scores[:var_count, :deg_count].astype(jnp.bfloat16)
    for member in range(member_count):
        score_ref[member] = rounded
    half = BAND // 2
    for member in range(member_count):
        part = jnp.concatenate(
            [
                pulls[at : at + var_count, :]
                for at in range(4 * member * ROW_PAD, 4 * (member + 1) * ROW_PAD, ROW_PAD)
            ],
            axis=0,
        ).astype(jnp.bfloat16)
        back = lax.dot_general(
            table, part, (((1,), (1,)), ((), ())), preferred_element_type=jnp.float32
        )
        split[0] = back[:, :LANES]
        split[1, :, : 4 * var_count - LANES] = back[:, LANES:]
        pieces = []
        for row in range(half):
            rows = pl.ds(row, lat_count // half, stride=half)
            pieces += [split[0, rows, :], split[1, rows, :][:, : 4 * var_count - LANES]]
        packed = jnp.concatenate(pieces, axis=1).astype(jnp.bfloat16)
        grad_ref[:, member] = packed.reshape(space_count, 2, half * 4 * var_count)


def spectral(received, orders, fairness, member_count, var_count, deg_count):
    senders, band_rows, width = received.shape
    space_count = senders // member_count
    lat_count = space_count * band_rows
    deg_pad = -(-deg_count // LANES) * LANES
    ens_count = 2 * member_count
    grads, score = pl.pallas_call(
        functools.partial(spectral_kernel, fairness, member_count, var_count, deg_count),
        in_specs=[
            pl.BlockSpec(memory_space=pltpu.SMEM),
            pl.BlockSpec(memory_space=pltpu.VMEM),
        ],
        out_specs=[pl.BlockSpec(memory_space=pltpu.VMEM)] * 2,
        out_shape=[
            jax.ShapeDtypeStruct(
                (space_count, member_count, 2, band_rows // 2 * 4 * var_count), jnp.bfloat16
            ),
            jax.ShapeDtypeStruct((member_count, var_count, deg_count), jnp.bfloat16),
        ],
        scratch_shapes=[
            pltpu.VMEM((lat_count, deg_pad), jnp.float32),
            pltpu.VMEM((2 * (ens_count + 1) * ROW_PAD, lat_count), jnp.float32),
            pltpu.VMEM((2 * (ens_count + 1) * ROW_PAD, deg_pad), jnp.float32),
            pltpu.VMEM((2 * ens_count * ROW_PAD, deg_pad), jnp.float32),
            pltpu.VMEM((ROW_PAD, deg_pad), jnp.float32),
            pltpu.VMEM((2, lat_count, LANES), jnp.float32),
        ],
        compiler_params=pltpu.CompilerParams(vmem_limit_bytes=28 * MIB),
        cost_estimate=pl.CostEstimate(flops=COST, bytes_accessed=COST, transcendentals=0),
        name="spectral",
    )(orders, received.reshape(space_count, member_count, band_rows, width))
    return grads.reshape(senders, 2, band_rows // 2 * 4 * var_count), score


def backward_kernel(var_count, in_ref, table_ref, out_ref, staged, turned):
    step = pl.program_id(0)
    order_count = in_ref.shape[0]
    block = out_ref.shape[0]
    rows = 2 * var_count * BAND

    @pl.when(step == 0)
    def _():
        half = BAND // 2
        tiles = staged.shape[0]
        for part in range(tiles):
            staged[part] = (
                in_ref[:, :, part * LANES : (part + 1) * LANES]
                .reshape(2 * order_count, LANES)
                .astype(jnp.float32)
            )
        for high in range(2):
            whole = jnp.concatenate(
                [staged[part, pl.ds(high, order_count, stride=2), :].T for part in range(tiles)],
                axis=0,
            )
            for low in range(half):
                for c in range(2):
                    for own in range(2):
                        source = (4 * low + 2 * c + own) * var_count
                        at = own * var_count * BAND + high * half + low
                        turned[c, pl.ds(at, var_count, stride=BAND), :] = whole[
                            source : source + var_count
                        ]

    at = pl.multiple_of(step * block, block)
    left = jnp.concatenate(
        [turned[0, pl.ds(at, block), :], turned[1, pl.ds(at, block), :]], axis=1
    ).astype(jnp.bfloat16)
    out_ref[...] = lax.dot_general(
        left, table_ref[...], (((1,), (1,)), ((), ())), preferred_element_type=jnp.float32
    ).astype(jnp.bfloat16)


def backward(received, table, own_count, var_count):
    order_count, _, width = received.shape
    band_rows = 2 * width // (2 * own_count * var_count)
    lon_count = table.shape[0]
    rows = own_count * var_count * band_rows
    steps = 2
    return pl.pallas_call(
        functools.partial(backward_kernel, var_count),
        grid=(steps,),
        in_specs=[
            pl.BlockSpec((order_count, 2, width), lambda i: (0, 0, 0)),
            pl.BlockSpec((lon_count, 2 * order_count), lambda i: (0, 0)),
        ],
        out_specs=pl.BlockSpec((rows // steps, lon_count), lambda i: (i, 0)),
        out_shape=jax.ShapeDtypeStruct((rows, lon_count), jnp.bfloat16),
        scratch_shapes=[
            pltpu.VMEM((width // LANES, 2 * order_count, LANES), jnp.float32),
            pltpu.VMEM((2, rows, order_count), jnp.float32),
        ],
        compiler_params=pltpu.CompilerParams(vmem_limit_bytes=16 * MIB),
        cost_estimate=pl.CostEstimate(flops=COST, bytes_accessed=COST, transcendentals=0),
        name="backward",
    )(received, table)


HOPS = ((0, 0), (0, 1), (0, 3), (1, 3), (1, 1), (1, 2), (1, 0), (0, 2))
RING = 4


def partner(member, hop, sign):
    half, spot = member // RING, member % RING
    return (half + hop[0]) % 2 * RING + (spot + sign * hop[1] + RING) % RING


def hop_pairs(hop, member_count):
    return [(i, partner(i, hop, 1)) for i in range(member_count)]


def regroup_kernel(var_count, sub_rows, ens_ref, truth_ref, *rest):
    outs, (target_ref, wide, paired) = rest[:-3], rest[-3:]
    member = lax.axis_index("member")

    def move(tile, goal, keep):
        for row in range(sub_rows):
            paired[tile, keep, pl.ds(row, var_count, stride=sub_rows), :] = wide[
                tile, pl.ds(goal * sub_rows + row, var_count, stride=BAND), :
            ]
        return paired[tile, keep].astype(jnp.bfloat16)

    for tile in range(wide.shape[0]):
        lanes = slice(tile * LANES, (tile + 1) * LANES)

        @pl.when(pl.program_id(1) == 0)
        def _(tile=tile, lanes=lanes):
            wide[tile] = truth_ref[:, lanes].astype(jnp.float32)
            target_ref[:, lanes] = move(tile, member, 0)

        wide[tile] = ens_ref[:, lanes].astype(jnp.float32)
        for place, hop in enumerate(HOPS):
            outs[place][0, :, lanes] = move(tile, partner(member, hop, 1), place)


def regroup(ens, truth, member_count):
    own_count, var_count, band_rows, lon_count = ens.shape
    sub_rows = band_rows // member_count
    width = 3 * LANES
    rows = var_count * sub_rows
    return pl.pallas_call(
        functools.partial(regroup_kernel, var_count, sub_rows),
        grid=(-(-lon_count // width), own_count),
        in_specs=[
            pl.BlockSpec((var_count * band_rows, width), lambda i, e: (e, i)),
            pl.BlockSpec((var_count * band_rows, width), lambda i, e: (0, i)),
        ],
        out_specs=[pl.BlockSpec((1, rows, width), lambda i, e: (e, 0, i))] * member_count
        + [pl.BlockSpec((rows, width), lambda i, e: (0, i))],
        out_shape=[
            jax.ShapeDtypeStruct((own_count, rows, lon_count), jnp.bfloat16)
            for _ in range(member_count)
        ]
        + [jax.ShapeDtypeStruct((rows, lon_count), jnp.bfloat16)],
        scratch_shapes=[
            pltpu.VMEM((width // LANES, var_count * band_rows, LANES), jnp.float32),
            pltpu.VMEM((width // LANES, member_count, rows, LANES), jnp.float32),
        ],
        compiler_params=pltpu.CompilerParams(vmem_limit_bytes=56 * MIB),
        cost_estimate=pl.CostEstimate(flops=COST, bytes_accessed=COST, transcendentals=0),
        name="regroup",
    )(ens.reshape(-1, lon_count), truth.reshape(-1, lon_count))


def stretch(x):
    scaled = x * 2.0**124
    return scaled + jnp.minimum(jnp.maximum(scaled * 2.0**10, -(2.0**24)), 2.0**24)


def sign(a, b):
    return jnp.minimum(jnp.maximum(a - b, -1.0), 1.0)


def count_kernel(*refs):
    parts, sum_ref = refs[:-1], refs[-1]
    per_part, row_count, width = parts[0].shape
    count = per_part * len(parts)

    def tile(at, rows, lane_at):
        lanes = slice(lane_at, lane_at + LANES)
        span = pl.ds(at, rows)
        wide = [
            stretch(parts[e // per_part][e % per_part, span, lanes].astype(jnp.float32))
            for e in range(count)
        ]
        pieces = []
        for half in range(rows // 8):
            x = [value[8 * half : 8 * half + 8] for value in wide]
            sums = [jnp.zeros((8, LANES), jnp.float32)] * count
            for i in range(count):
                for j in range(i + 1, count):
                    s = sign(x[i], x[j])
                    sums[i] = sums[i] + s
                    sums[j] = sums[j] - s
            pieces.append(sums)
        for e in range(count):
            whole_sum = jnp.concatenate([sums[e] for sums in pieces], axis=0)
            sum_ref[e, span, lanes] = whole_sum.astype(jnp.bfloat16)

    over_tiles(tile, row_count, width)


def over_tiles(tile, row_count, width):
    whole = row_count // 16
    for lane_at in range(0, width, LANES):
        def body(index, _, lane_at=lane_at):
            tile(pl.multiple_of(index * 16, 16), 16, lane_at)
            return 0

        lax.fori_loop(0, whole, body, 0)
        if row_count % 16:
            tile(whole * 16, row_count % 16, lane_at)


def count_signs(parts):
    per_part, row_count, lon_count = parts[0].shape
    count = per_part * len(parts)
    width = GRID_WIDTH
    return pl.pallas_call(
        count_kernel,
        grid=(-(-lon_count // width),),
        in_specs=[pl.BlockSpec((per_part, row_count, width), lambda i: (0, 0, i))] * len(parts),
        out_specs=pl.BlockSpec((count, row_count, width), lambda i: (0, 0, i)),
        out_shape=jax.ShapeDtypeStruct((count, row_count, lon_count), jnp.bfloat16),
        compiler_params=pltpu.CompilerParams(vmem_limit_bytes=56 * MIB),
        cost_estimate=pl.CostEstimate(flops=COST, bytes_accessed=COST, transcendentals=0),
        name="count",
    )(*parts)


def grid_kernel(fairness, lon_count, known, weight_ref, truth_ref, spec_ref, *rest):
    part_count = spec_ref.shape[0]
    parts, known_ref = rest[:part_count], rest[part_count]
    grad_ref, score_ref, wide_ref, total, mixed = rest[part_count + 1 :]
    step = pl.program_id(0)
    per_part, row_count, width = parts[0].shape
    ens_count = per_part * part_count
    sub_rows = grad_ref.shape[2]
    pull_scale = -fairness / (ens_count - 1)
    member = lax.axis_index("member")
    senders = [partner(member, hop, -1) for hop in HOPS]
    lat_start = (lax.axis_index("space") * part_count + member) * sub_rows
    which = lax.broadcasted_iota(jnp.int32, (8, LANES), 0) % sub_rows
    weight = jnp.full((8, LANES), weight_ref[lat_start], jnp.float32)
    for row in range(1, sub_rows):
        weight = jnp.where(which == row, weight_ref[lat_start + row], weight)

    @pl.when(step == 0)
    def _():
        total[...] = jnp.zeros_like(total)
        spec_count, spec_vars, degrees = spec_ref.shape
        for lane_at in range(0, degrees, LANES):
            size = min(LANES, degrees - lane_at)
            lanes = slice(lane_at, lane_at + size)
            for order in range(spec_count):
                mixed[pl.ds(order, spec_vars, stride=spec_count), :size] = spec_ref[
                    order, :, lanes
                ].astype(jnp.float32)
            wide_ref[:, :, lanes] = mixed[:, :size].reshape(spec_vars, spec_count, size)

    def tile(at, rows, lane_at):
        lanes = slice(lane_at, lane_at + LANES)
        span = pl.ds(at, rows)
        wide = [
            parts[e // per_part][e % per_part, span, lanes].astype(jnp.float32)
            for e in range(ens_count)
        ]
        goals = truth_ref[span, lanes].astype(jnp.float32)
        before = [known_ref[e, span, lanes].astype(jnp.float32) for e in range(known)]
        pieces = []
        for half in range(rows // 8):
            piece = slice(8 * half, 8 * half + 8)
            x = [stretch(value[piece]) for value in wide]
            goal = goals[piece]
            y = stretch(goal)
            zero = jnp.zeros((8, LANES), jnp.float32)
            sums = [value[piece] for value in before] + [zero] * (ens_count - known)
            for i in range(ens_count):
                for j in range(max(i + 1, known), ens_count):
                    s = sign(x[i], x[j])
                    sums[i] = sums[i] + s
                    sums[j] = sums[j] - s
            score = zero
            toward_sum = zero
            grads = []
            for e in range(ens_count):
                toward = sign(x[e], y)
                toward_sum = toward_sum + toward
                pull = toward + pull_scale * sums[e]
                score = score + wide[e][piece] * pull
                grads.append(weight * pull)
            pieces.append(grads)
            score = (score - goal * toward_sum) * (1.0 / ens_count)
            lane = lax.broadcasted_iota(jnp.int32, (8, LANES), 1) + (
                step * width + lane_at
            )
            total[pl.ds(at + 8 * half, 8), :] += jnp.where(lane < lon_count, score, 0.0)
        for e in range(ens_count):
            whole_grad = jnp.concatenate([grads[e] for grads in pieces], axis=0)
            grad_ref[
                senders[e // per_part] * per_part + e % per_part,
                pl.ds(at // sub_rows, rows // sub_rows), :, lanes,
            ] = whole_grad.astype(jnp.bfloat16).reshape(rows // sub_rows, sub_rows, LANES)

    over_tiles(tile, row_count, width)

    @pl.when(step == pl.num_programs(0) - 1)
    def _():
        for row in range(sub_rows):
            rows = total[pl.ds(row, row_count // sub_rows, stride=sub_rows), :]
            result = jnp.sum(rows.T, axis=0, keepdims=True) * (1.0 / lon_count)
            score_ref[row : row + 1, :] = result


def grid_scores(parts, signs, target, weights, spec_score, fairness, sub_rows):
    per_part, row_count, lon_count = parts[0].shape
    ens_count = per_part * len(parts)
    var_count = row_count // sub_rows
    order_count, _, deg_count = spec_score.shape
    width = GRID_WIDTH
    return pl.pallas_call(
        functools.partial(grid_kernel, fairness, lon_count, signs.shape[0]),
        grid=(-(-lon_count // width),),
        in_specs=[
            pl.BlockSpec(memory_space=pltpu.SMEM),
            pl.BlockSpec((row_count, width), lambda i: (0, i)),
            pl.BlockSpec((order_count, var_count, deg_count), lambda i: (0, 0, 0)),
        ]
        + [pl.BlockSpec((per_part, row_count, width), lambda i: (0, 0, i))] * len(parts)
        + [pl.BlockSpec((signs.shape[0], row_count, width), lambda i: (0, 0, i))],
        out_specs=[
            pl.BlockSpec((ens_count, var_count, sub_rows, width), lambda i: (0, 0, 0, i)),
            pl.BlockSpec((sub_rows, var_count), lambda i: (0, 0)),
            pl.BlockSpec((var_count, order_count, deg_count), lambda i: (0, 0, 0)),
        ],
        out_shape=[
            jax.ShapeDtypeStruct((ens_count, var_count, sub_rows, lon_count), jnp.bfloat16),
            jax.ShapeDtypeStruct((sub_rows, var_count), jnp.float32),
            jax.ShapeDtypeStruct((var_count, order_count, deg_count), jnp.float32),
        ],
        scratch_shapes=[
            pltpu.VMEM((row_count, LANES), jnp.float32),
            pltpu.VMEM((var_count * order_count, LANES), jnp.float32),
        ],
        compiler_params=pltpu.CompilerParams(vmem_limit_bytes=56 * MIB),
        cost_estimate=pl.CostEstimate(flops=COST, bytes_accessed=COST, transcendentals=0),
        name="grid",
    )(weights, target, spec_score, *parts, signs)


def local(ens, truth, legendre, orders):
    own_count, var_count, band_rows, lon_count = ens.shape
    order_count = orders.shape[0]
    deg_count = legendre.shape[2]
    space_count = lax.axis_size("space")
    member_count = lax.axis_size("member")
    lat_count = band_rows * space_count
    ens_count = own_count * member_count
    sub_rows = band_rows // member_count
    fairness = 1.0 - FAIR_GAP / ens_count

    owners = ("space", "member")
    sent, table = forward(ens, truth, legendre, orders, member_count)
    received = lax.all_to_all(sent, owners, split_axis=0, concat_axis=0, tiled=True)

    *parts, target = regroup(ens, truth, member_count)
    for place, hop in enumerate(HOPS):
        if place:
            parts[place] = lax.ppermute(parts[place], "member", hop_pairs(hop, member_count))

    received, *parts[1:3] = lax.optimization_barrier((received, *parts[1:3]))
    grads, score = spectral(received, orders, fairness, member_count, var_count, deg_count)
    signs = count_signs(parts[:EARLY_PARTS])
    spec_score = lax.all_to_all(score, "member", split_axis=0, concat_axis=0, tiled=True)
    grads, spec_score, signs, *parts = lax.optimization_barrier(
        (grads, spec_score, signs, *parts)
    )
    returned = lax.all_to_all(grads, owners, split_axis=0, concat_axis=0, tiled=True)
    weights = jnp.asarray(latitude_weights(lat_count))
    grid_grad, grid_rows, spec_score = grid_scores(
        parts, signs, target, weights, spec_score, fairness, sub_rows
    )
    spec_score = spec_score.swapaxes(0, 1)
    grid_grad = grid_grad.reshape(ens_count, var_count, 1, sub_rows, lon_count)
    grid_score = grid_rows.T.reshape(var_count, 1, sub_rows)
    spec_grad = backward(returned, table, own_count, var_count).reshape(ens.shape)
    return (grid_score, grid_grad, spec_score, spec_grad)


def solution(mesh):
    in_specs = (
        P("member", None, "space", None),
        P(None, "space", None),
        P("space", None, None),
        P(),
    )
    out_specs = (
        P(None, "space", "member"),
        P(None, None, "space", "member", None),
        P("space", None, None),
        P("member", None, "space", None),
    )
    return jax.shard_map(local, mesh=mesh, in_specs=in_specs, out_specs=out_specs, check_vma=False)
```

```python
import functools
import math

import jax
import jax.numpy as jnp
import numpy as np
from jax import lax
from jax.experimental import pallas as pl
from jax.experimental.pallas import tpu as pltpu
from jax.sharding import PartitionSpec as P

FAIR_GAP = 0.05
SOFTEN = 0.1
MIB = 1024 * 1024
COST = 1024
BAND = 16
LANES = 128
GRID_WIDTH = 2 * LANES
EARLY_PARTS = 6
FIELD_COPIES = 2
ROW_PAD = 40


def latitude_weights(lat_count):
    sine_values = np.sin((np.arange(lat_count) + 0.5) * (math.pi / lat_count))
    return (sine_values * (lat_count / sine_values.sum())).astype(np.float32)


def write_table(orders_ref, table_ref):
    lon_count = table_ref.shape[0]
    order_count = orders_ref.shape[1]
    chunk = 160
    norm = 1.0 / math.sqrt(lon_count)
    listed = orders_ref[...].astype(jnp.float32)

    def fill(step, _):
        start = pl.multiple_of(step * chunk, chunk)
        rows = lax.broadcasted_iota(jnp.int32, (chunk, order_count), 0) + start
        product = rows.astype(jnp.float32) * listed
        turns = jnp.floor(product * (1.0 / lon_count))
        phase = product - turns * lon_count
        quarter = jnp.floor(phase * (4.0 / lon_count) + 0.5)
        angle = (phase - quarter * (lon_count / 4.0)) * (2.0 * math.pi / lon_count)
        square = angle * angle
        sine = angle * (
            1.0 + square * (-1.0 / 6 + square * (1.0 / 120 + square * (-1.0 / 5040 + square / 362880)))
        )
        cosine = 1.0 + square * (
            -0.5 + square * (1.0 / 24 + square * (-1.0 / 720 + square * (1.0 / 40320)))
        )
        half = jnp.floor(quarter * 0.5)
        odd = quarter - 2.0 * half
        half_odd = half - 2.0 * jnp.floor(half * 0.5)
        flip = 1.0 - 2.0 * half_odd
        swap = odd > 0.5
        cos_value = jnp.where(swap, -sine, cosine) * flip
        sin_value = jnp.where(swap, cosine, sine) * flip
        table_ref[pl.ds(start, chunk), :order_count] = (cos_value * norm).astype(jnp.bfloat16)
        table_ref[pl.ds(start, chunk), order_count:] = (-sin_value * norm).astype(jnp.bfloat16)
        return 0

    lax.fori_loop(0, lon_count // chunk, fill, 0)


def forward_kernel(
    var_count, deg_count, orders_ref, ens_ref, truth_ref, leg_ref, out_ref, table_ref,
    staged, swapped, fields, truth_part, leg_part, sems,
):
    own_rows = 2 * var_count * BAND
    block = own_rows // FIELD_COPIES
    deg_part = leg_part.shape[0]
    var_part = truth_part.shape[0]
    leg_at = 2 * own_rows
    truth_at = leg_at + deg_part * BAND
    truth_rows = var_part * BAND
    used = truth_at + 2 * truth_rows
    order_count = orders_ref.shape[1]

    member = lax.axis_index("member")
    var_start = jnp.minimum(member * var_part, var_count - var_part)
    deg_start = jnp.minimum(member * deg_part, deg_count - deg_part)
    truth_copy = pltpu.make_async_copy(
        truth_ref.at[pl.ds(var_start, var_part)], truth_part, sems.at[0]
    )
    leg_copy = pltpu.make_async_copy(
        leg_ref.at[pl.ds(deg_start, deg_part)], leg_part, sems.at[1]
    )
    copies = [
        pltpu.make_async_copy(
            ens_ref.at[pl.ds(part * block, block)], fields.at[pl.ds(part * block, block)],
            sems.at[2 + part],
        )
        for part in range(FIELD_COPIES)
    ]
    truth_copy.start()
    for copy in copies:
        copy.start()
    leg_copy.start()
    write_table(orders_ref, table_ref)
    staged[used:, :] = jnp.zeros((staged.shape[0] - used, order_count), jnp.float32)
    truth_copy.wait()
    rows = jnp.dot(
        truth_part[...].reshape(truth_rows, -1), table_ref[...],
        preferred_element_type=jnp.float32,
    )
    staged[truth_at : truth_at + truth_rows, :] = rows[:, :order_count]
    staged[truth_at + truth_rows : used, :] = rows[:, order_count:]
    for part, copy in enumerate(copies):
        copy.wait()
        at = part * block
        rows = jnp.dot(
            fields[at : at + block, :], table_ref[...], preferred_element_type=jnp.float32
        )
        staged[at : at + block, :] = rows[:, :order_count]
        staged[own_rows + at : own_rows + at + block, :] = rows[:, order_count:]
    leg_copy.wait()
    staged[leg_at:truth_at, :] = (
        leg_part[...].reshape(deg_part * BAND, order_count).astype(jnp.float32)
    )

    width = staged.shape[0] // BAND
    for row in range(BAND):
        piece = staged[pl.ds(row, width, stride=BAND), :]
        swapped[0, pl.ds(row, order_count, stride=BAND), :] = piece[:LANES].T
        swapped[1, pl.ds(row, order_count, stride=BAND), :] = piece[LANES:].T
    for part in range(2):
        out_ref[:, :, part * LANES : (part + 1) * LANES] = (
            swapped[part].reshape(order_count, BAND, LANES).astype(jnp.bfloat16)
        )


def forward(ens, truth, legendre, orders, member_count):
    own_count, var_count, band_rows, lon_count = ens.shape
    order_count = orders.shape[0]
    deg_count = legendre.shape[2]
    deg_part = -(-deg_count // member_count)
    var_part = -(-var_count // member_count)
    rows = own_count * var_count * band_rows
    width = 2 * LANES
    return pl.pallas_call(
        functools.partial(forward_kernel, var_count, deg_count),
        in_specs=[pl.BlockSpec(memory_space=pltpu.VMEM)] + [pl.BlockSpec(memory_space=pl.ANY)] * 3,
        out_specs=[pl.BlockSpec(memory_space=pltpu.VMEM)] * 2,
        out_shape=[
            jax.ShapeDtypeStruct((order_count, band_rows, width), jnp.bfloat16),
            jax.ShapeDtypeStruct((lon_count, 2 * order_count), jnp.bfloat16),
        ],
        scratch_shapes=[
            pltpu.VMEM((width * band_rows, order_count), jnp.float32),
            pltpu.VMEM((2, order_count * band_rows, LANES), jnp.float32),
            pltpu.VMEM((rows, lon_count), jnp.bfloat16),
            pltpu.VMEM((var_part, band_rows, lon_count), jnp.bfloat16),
            pltpu.VMEM((deg_part, band_rows, order_count), jnp.bfloat16),
            pltpu.SemaphoreType.DMA((2 + FIELD_COPIES,)),
        ],
        compiler_params=pltpu.CompilerParams(vmem_limit_bytes=56 * MIB),
        cost_estimate=pl.CostEstimate(flops=COST, bytes_accessed=COST, transcendentals=0),
        name="forward",
    )(orders.reshape(1, -1), ens.reshape(rows, lon_count), truth,
      jnp.transpose(legendre, (2, 0, 1)))


def spectral_kernel(
    fairness, member_count, var_count, deg_count, orders_ref, in_ref, grad_ref, score_ref,
    weights, values, spectra, pulls, scores, split,
):
    ens_count = 2 * member_count
    deg_part = -(-deg_count // member_count)
    var_part = -(-var_count // member_count)
    lat_count = weights.shape[0]
    space_count = lat_count // BAND
    leg_at = 4 * var_count
    truth_at = leg_at + deg_part
    own_order = orders_ref[lax.axis_index("space") * member_count + lax.axis_index("member")]
    omega = jnp.where(own_order == 0, 1.0, 2.0).astype(jnp.float32)
    spread_scale = -fairness / (ens_count * (ens_count - 1))
    pull_scale = -fairness / (ens_count - 1)

    values[...] = jnp.zeros_like(values)
    weights[...] = jnp.zeros_like(weights)
    for member in range(member_count):
        block = in_ref[:, member].reshape(lat_count, 2 * LANES)
        deg_start = min(member * deg_part, deg_count - deg_part)
        weights[:, deg_start : deg_start + deg_part] = block[:, leg_at : leg_at + deg_part].astype(
            jnp.float32
        )
        turned = block.astype(jnp.float32).T
        var_start = min(member * var_part, var_count - var_part)
        for c in range(2):
            for own in range(2):
                at = (c * (ens_count + 1) + 2 * member + own) * ROW_PAD
                source = (2 * c + own) * var_count
                values[at : at + var_count, :] = turned[source : source + var_count]
            at = (c * (ens_count + 1) + ens_count) * ROW_PAD + var_start
            source = truth_at + c * var_part
            values[at : at + var_part, :] = turned[source : source + var_part]
    table = weights[...].astype(jnp.bfloat16)
    spectra[...] = jnp.dot(
        values[...].astype(jnp.bfloat16), table, preferred_element_type=jnp.float32
    )

    def tile(index, _):
        lane_tile = index % (weights.shape[1] // LANES)
        row_tile = index // (weights.shape[1] // LANES)
        lanes = pl.ds(pl.multiple_of(lane_tile * LANES, LANES), LANES)

        def load(c, e):
            at = (c * (ens_count + 1) + e) * ROW_PAD
            return spectra[pl.ds(pl.multiple_of(at + row_tile * 8, 8), 8), lanes]

        def pair(a, b):
            d0 = a[0] - b[0]
            d1 = a[1] - b[1]
            square = d0 * d0 + d1 * d1 + SOFTEN * SOFTEN
            inverse = lax.rsqrt(square)
            return square * inverse, d0 * inverse, d1 * inverse

        z = [(load(0, e), load(1, e)) for e in range(ens_count)]
        y = (load(0, ens_count), load(1, ens_count))
        zero = jnp.zeros((8, LANES), jnp.float32)
        pull = [[zero, zero] for _ in range(ens_count)]
        spread = zero
        for i in range(ens_count):
            for j in range(i + 1, ens_count):
                size, u0, u1 = pair(z[i], z[j])
                spread = spread + size
                pull[i][0] = pull[i][0] + u0
                pull[i][1] = pull[i][1] + u1
                pull[j][0] = pull[j][0] - u0
                pull[j][1] = pull[j][1] - u1
        error = zero
        for e in range(ens_count):
            size, u0, u1 = pair(z[e], y)
            error = error + size
            for c, u in enumerate((u0, u1)):
                at = ((e // 2) * 4 + 2 * c + e % 2) * ROW_PAD
                pulls[pl.ds(pl.multiple_of(at + row_tile * 8, 8), 8), lanes] = omega * (
                    u + pull_scale * pull[e][c]
                )
        pairs = ens_count * (ens_count - 1) // 2
        score = (error - SOFTEN * ens_count) * (1.0 / ens_count) + spread_scale * (
            spread - SOFTEN * pairs
        )
        scores[pl.ds(pl.multiple_of(row_tile * 8, 8), 8), lanes] = score
        return 0

    lax.fori_loop(0, (ROW_PAD // 8) * (weights.shape[1] // LANES), tile, 0)
    rounded = scores[:var_count, :deg_count].astype(jnp.bfloat16)
    for member in range(member_count):
        score_ref[member] = rounded
    half = BAND // 2
    for member in range(member_count):
        part = jnp.concatenate(
            [
                pulls[at : at + var_count, :]
                for at in range(4 * member * ROW_PAD, 4 * (member + 1) * ROW_PAD, ROW_PAD)
            ],
            axis=0,
        ).astype(jnp.bfloat16)
        back = lax.dot_general(
            table, part, (((1,), (1,)), ((), ())), preferred_element_type=jnp.float32
        )
        split[0] = back[:, :LANES]
        split[1, :, : 4 * var_count - LANES] = back[:, LANES:]
        pieces = []
        for row in range(half):
            rows = pl.ds(row, lat_count // half, stride=half)
            pieces += [split[0, rows, :], split[1, rows, :][:, : 4 * var_count - LANES]]
        packed = jnp.concatenate(pieces, axis=1).astype(jnp.bfloat16)
        grad_ref[:, member] = packed.reshape(space_count, 2, half * 4 * var_count)


def spectral(received, orders, fairness, member_count, var_count, deg_count):
    senders, band_rows, width = received.shape
    space_count = senders // member_count
    lat_count = space_count * band_rows
    deg_pad = -(-deg_count // LANES) * LANES
    ens_count = 2 * member_count
    grads, score = pl.pallas_call(
        functools.partial(spectral_kernel, fairness, member_count, var_count, deg_count),
        in_specs=[
            pl.BlockSpec(memory_space=pltpu.SMEM),
            pl.BlockSpec(memory_space=pltpu.VMEM),
        ],
        out_specs=[pl.BlockSpec(memory_space=pltpu.VMEM)] * 2,
        out_shape=[
            jax.ShapeDtypeStruct(
                (space_count, member_count, 2, band_rows // 2 * 4 * var_count), jnp.bfloat16
            ),
            jax.ShapeDtypeStruct((member_count, var_count, deg_count), jnp.bfloat16),
        ],
        scratch_shapes=[
            pltpu.VMEM((lat_count, deg_pad), jnp.float32),
            pltpu.VMEM((2 * (ens_count + 1) * ROW_PAD, lat_count), jnp.float32),
            pltpu.VMEM((2 * (ens_count + 1) * ROW_PAD, deg_pad), jnp.float32),
            pltpu.VMEM((2 * ens_count * ROW_PAD, deg_pad), jnp.float32),
            pltpu.VMEM((ROW_PAD, deg_pad), jnp.float32),
            pltpu.VMEM((2, lat_count, LANES), jnp.float32),
        ],
        compiler_params=pltpu.CompilerParams(vmem_limit_bytes=28 * MIB),
        cost_estimate=pl.CostEstimate(flops=COST, bytes_accessed=COST, transcendentals=0),
        name="spectral",
    )(orders, received.reshape(space_count, member_count, band_rows, width))
    return grads.reshape(senders, 2, band_rows // 2 * 4 * var_count), score


def backward_kernel(var_count, in_ref, table_ref, out_ref, staged, turned):
    step = pl.program_id(0)
    order_count = in_ref.shape[0]
    block = out_ref.shape[0]
    rows = 2 * var_count * BAND

    @pl.when(step == 0)
    def _():
        half = BAND // 2
        tiles = staged.shape[0]
        for part in range(tiles):
            staged[part] = (
                in_ref[:, :, part * LANES : (part + 1) * LANES]
                .reshape(2 * order_count, LANES)
                .astype(jnp.float32)
            )
        for high in range(2):
            whole = jnp.concatenate(
                [staged[part, pl.ds(high, order_count, stride=2), :].T for part in range(tiles)],
                axis=0,
            )
            for low in range(half):
                for c in range(2):
                    for own in range(2):
                        source = (4 * low + 2 * c + own) * var_count
                        at = own * var_count * BAND + high * half + low
                        turned[c, pl.ds(at, var_count, stride=BAND), :] = whole[
                            source : source + var_count
                        ]

    at = pl.multiple_of(step * block, block)
    left = jnp.concatenate(
        [turned[0, pl.ds(at, block), :], turned[1, pl.ds(at, block), :]], axis=1
    ).astype(jnp.bfloat16)
    out_ref[...] = lax.dot_general(
        left, table_ref[...], (((1,), (1,)), ((), ())), preferred_element_type=jnp.float32
    ).astype(jnp.bfloat16)


def backward(received, table, own_count, var_count):
    order_count, _, width = received.shape
    band_rows = 2 * width // (2 * own_count * var_count)
    lon_count = table.shape[0]
    rows = own_count * var_count * band_rows
    steps = 2
    return pl.pallas_call(
        functools.partial(backward_kernel, var_count),
        grid=(steps,),
        in_specs=[
            pl.BlockSpec((order_count, 2, width), lambda i: (0, 0, 0)),
            pl.BlockSpec((lon_count, 2 * order_count), lambda i: (0, 0)),
        ],
        out_specs=pl.BlockSpec((rows // steps, lon_count), lambda i: (i, 0)),
        out_shape=jax.ShapeDtypeStruct((rows, lon_count), jnp.bfloat16),
        scratch_shapes=[
            pltpu.VMEM((width // LANES, 2 * order_count, LANES), jnp.float32),
            pltpu.VMEM((2, rows, order_count), jnp.float32),
        ],
        compiler_params=pltpu.CompilerParams(vmem_limit_bytes=16 * MIB),
        cost_estimate=pl.CostEstimate(flops=COST, bytes_accessed=COST, transcendentals=0),
        name="backward",
    )(received, table)


HOPS = ((0, 0), (0, 1), (0, 3), (1, 3), (1, 1), (1, 2), (1, 0), (0, 2))
RING = 4


def partner(member, hop, sign):
    half, spot = member // RING, member % RING
    return (half + hop[0]) % 2 * RING + (spot + sign * hop[1] + RING) % RING


def hop_pairs(hop, member_count):
    return [(i, partner(i, hop, 1)) for i in range(member_count)]


def regroup_kernel(var_count, sub_rows, ens_ref, truth_ref, *rest):
    outs, (target_ref, wide, paired) = rest[:-3], rest[-3:]
    member = lax.axis_index("member")

    def move(tile, goal, keep):
        for row in range(sub_rows):
            paired[tile, keep, pl.ds(row, var_count, stride=sub_rows), :] = wide[
                tile, pl.ds(goal * sub_rows + row, var_count, stride=BAND), :
            ]
        return paired[tile, keep].astype(jnp.bfloat16)

    for tile in range(wide.shape[0]):
        lanes = slice(tile * LANES, (tile + 1) * LANES)

        @pl.when(pl.program_id(1) == 0)
        def _(tile=tile, lanes=lanes):
            wide[tile] = truth_ref[:, lanes].astype(jnp.float32)
            target_ref[:, lanes] = move(tile, member, 0)

        wide[tile] = ens_ref[:, lanes].astype(jnp.float32)
        for place, hop in enumerate(HOPS):
            outs[place][0, :, lanes] = move(tile, partner(member, hop, 1), place)


def regroup(ens, truth, member_count):
    own_count, var_count, band_rows, lon_count = ens.shape
    sub_rows = band_rows // member_count
    width = 6 * LANES
    rows = var_count * sub_rows
    return pl.pallas_call(
        functools.partial(regroup_kernel, var_count, sub_rows),
        grid=(-(-lon_count // width), own_count),
        in_specs=[
            pl.BlockSpec((var_count * band_rows, width), lambda i, e: (e, i)),
            pl.BlockSpec((var_count * band_rows, width), lambda i, e: (0, i)),
        ],
        out_specs=[pl.BlockSpec((1, rows, width), lambda i, e: (e, 0, i))] * member_count
        + [pl.BlockSpec((rows, width), lambda i, e: (0, i))],
        out_shape=[
            jax.ShapeDtypeStruct((own_count, rows, lon_count), jnp.bfloat16)
            for _ in range(member_count)
        ]
        + [jax.ShapeDtypeStruct((rows, lon_count), jnp.bfloat16)],
        scratch_shapes=[
            pltpu.VMEM((width // LANES, var_count * band_rows, LANES), jnp.float32),
            pltpu.VMEM((width // LANES, member_count, rows, LANES), jnp.float32),
        ],
        compiler_params=pltpu.CompilerParams(vmem_limit_bytes=56 * MIB),
        cost_estimate=pl.CostEstimate(flops=COST, bytes_accessed=COST, transcendentals=0),
        name="regroup",
    )(ens.reshape(-1, lon_count), truth.reshape(-1, lon_count))


def stretch(x):
    scaled = x * 2.0**124
    return scaled + jnp.minimum(jnp.maximum(scaled * 2.0**10, -(2.0**24)), 2.0**24)


def sign(a, b):
    return jnp.minimum(jnp.maximum(a - b, -1.0), 1.0)


def count_kernel(*refs):
    parts, sum_ref = refs[:-1], refs[-1]
    per_part, row_count, width = parts[0].shape
    count = per_part * len(parts)

    def tile(at, rows, lane_at):
        lanes = slice(lane_at, lane_at + LANES)
        span = pl.ds(at, rows)
        wide = [
            stretch(parts[e // per_part][e % per_part, span, lanes].astype(jnp.float32))
            for e in range(count)
        ]
        pieces = []
        for half in range(rows // 8):
            x = [value[8 * half : 8 * half + 8] for value in wide]
            sums = [jnp.zeros((8, LANES), jnp.float32)] * count
            for i in range(count):
                for j in range(i + 1, count):
                    s = sign(x[i], x[j])
                    sums[i] = sums[i] + s
                    sums[j] = sums[j] - s
            pieces.append(sums)
        for e in range(count):
            whole_sum = jnp.concatenate([sums[e] for sums in pieces], axis=0)
            sum_ref[e, span, lanes] = whole_sum.astype(jnp.bfloat16)

    over_tiles(tile, row_count, width)


def over_tiles(tile, row_count, width):
    whole = row_count // 16
    for lane_at in range(0, width, LANES):
        def body(index, _, lane_at=lane_at):
            tile(pl.multiple_of(index * 16, 16), 16, lane_at)
            return 0

        lax.fori_loop(0, whole, body, 0)
        if row_count % 16:
            tile(whole * 16, row_count % 16, lane_at)


def count_signs(parts):
    per_part, row_count, lon_count = parts[0].shape
    count = per_part * len(parts)
    width = GRID_WIDTH
    return pl.pallas_call(
        count_kernel,
        grid=(-(-lon_count // width),),
        in_specs=[pl.BlockSpec((per_part, row_count, width), lambda i: (0, 0, i))] * len(parts),
        out_specs=pl.BlockSpec((count, row_count, width), lambda i: (0, 0, i)),
        out_shape=jax.ShapeDtypeStruct((count, row_count, lon_count), jnp.bfloat16),
        compiler_params=pltpu.CompilerParams(vmem_limit_bytes=56 * MIB),
        cost_estimate=pl.CostEstimate(flops=COST, bytes_accessed=COST, transcendentals=0),
        name="count",
    )(*parts)


def grid_kernel(fairness, lon_count, known, weight_ref, truth_ref, spec_ref, *rest):
    part_count = spec_ref.shape[0]
    parts, known_ref = rest[:part_count], rest[part_count]
    grad_ref, score_ref, wide_ref, total, mixed = rest[part_count + 1 :]
    step = pl.program_id(0)
    per_part, row_count, width = parts[0].shape
    ens_count = per_part * part_count
    sub_rows = grad_ref.shape[2]
    pull_scale = -fairness / (ens_count - 1)
    member = lax.axis_index("member")
    senders = [partner(member, hop, -1) for hop in HOPS]
    lat_start = (lax.axis_index("space") * part_count + member) * sub_rows
    which = lax.broadcasted_iota(jnp.int32, (8, LANES), 0) % sub_rows
    weight = jnp.full((8, LANES), weight_ref[lat_start], jnp.float32)
    for row in range(1, sub_rows):
        weight = jnp.where(which == row, weight_ref[lat_start + row], weight)

    @pl.when(step == 0)
    def _():
        total[...] = jnp.zeros_like(total)
        spec_count, spec_vars, degrees = spec_ref.shape
        for lane_at in range(0, degrees, LANES):
            size = min(LANES, degrees - lane_at)
            lanes = slice(lane_at, lane_at + size)
            for order in range(spec_count):
                mixed[pl.ds(order, spec_vars, stride=spec_count), :size] = spec_ref[
                    order, :, lanes
                ].astype(jnp.float32)
            wide_ref[:, :, lanes] = mixed[:, :size].reshape(spec_vars, spec_count, size)

    def tile(at, rows, lane_at):
        lanes = slice(lane_at, lane_at + LANES)
        span = pl.ds(at, rows)
        wide = [
            parts[e // per_part][e % per_part, span, lanes].astype(jnp.float32)
            for e in range(ens_count)
        ]
        goals = truth_ref[span, lanes].astype(jnp.float32)
        before = [known_ref[e, span, lanes].astype(jnp.float32) for e in range(known)]
        pieces = []
        for half in range(rows // 8):
            piece = slice(8 * half, 8 * half + 8)
            x = [stretch(value[piece]) for value in wide]
            goal = goals[piece]
            y = stretch(goal)
            zero = jnp.zeros((8, LANES), jnp.float32)
            sums = [value[piece] for value in before] + [zero] * (ens_count - known)
            for i in range(ens_count):
                for j in range(max(i + 1, known), ens_count):
                    s = sign(x[i], x[j])
                    sums[i] = sums[i] + s
                    sums[j] = sums[j] - s
            score = zero
            toward_sum = zero
            grads = []
            for e in range(ens_count):
                toward = sign(x[e], y)
                toward_sum = toward_sum + toward
                pull = toward + pull_scale * sums[e]
                score = score + wide[e][piece] * pull
                grads.append(weight * pull)
            pieces.append(grads)
            score = (score - goal * toward_sum) * (1.0 / ens_count)
            lane = lax.broadcasted_iota(jnp.int32, (8, LANES), 1) + (
                step * width + lane_at
            )
            total[pl.ds(at + 8 * half, 8), :] += jnp.where(lane < lon_count, score, 0.0)
        for e in range(ens_count):
            whole_grad = jnp.concatenate([grads[e] for grads in pieces], axis=0)
            grad_ref[
                senders[e // per_part] * per_part + e % per_part,
                pl.ds(at // sub_rows, rows // sub_rows), :, lanes,
            ] = whole_grad.astype(jnp.bfloat16).reshape(rows // sub_rows, sub_rows, LANES)

    over_tiles(tile, row_count, width)

    @pl.when(step == pl.num_programs(0) - 1)
    def _():
        for row in range(sub_rows):
            rows = total[pl.ds(row, row_count // sub_rows, stride=sub_rows), :]
            result = jnp.sum(rows.T, axis=0, keepdims=True) * (1.0 / lon_count)
            score_ref[row : row + 1, :] = result


def grid_scores(parts, signs, target, weights, spec_score, fairness, sub_rows):
    per_part, row_count, lon_count = parts[0].shape
    ens_count = per_part * len(parts)
    var_count = row_count // sub_rows
    order_count, _, deg_count = spec_score.shape
    width = GRID_WIDTH
    return pl.pallas_call(
        functools.partial(grid_kernel, fairness, lon_count, signs.shape[0]),
        grid=(-(-lon_count // width),),
        in_specs=[
            pl.BlockSpec(memory_space=pltpu.SMEM),
            pl.BlockSpec((row_count, width), lambda i: (0, i)),
            pl.BlockSpec((order_count, var_count, deg_count), lambda i: (0, 0, 0)),
        ]
        + [pl.BlockSpec((per_part, row_count, width), lambda i: (0, 0, i))] * len(parts)
        + [pl.BlockSpec((signs.shape[0], row_count, width), lambda i: (0, 0, i))],
        out_specs=[
            pl.BlockSpec((ens_count, var_count, sub_rows, width), lambda i: (0, 0, 0, i)),
            pl.BlockSpec((sub_rows, var_count), lambda i: (0, 0)),
            pl.BlockSpec((var_count, order_count, deg_count), lambda i: (0, 0, 0)),
        ],
        out_shape=[
            jax.ShapeDtypeStruct((ens_count, var_count, sub_rows, lon_count), jnp.bfloat16),
            jax.ShapeDtypeStruct((sub_rows, var_count), jnp.float32),
            jax.ShapeDtypeStruct((var_count, order_count, deg_count), jnp.float32),
        ],
        scratch_shapes=[
            pltpu.VMEM((row_count, LANES), jnp.float32),
            pltpu.VMEM((var_count * order_count, LANES), jnp.float32),
        ],
        compiler_params=pltpu.CompilerParams(vmem_limit_bytes=56 * MIB),
        cost_estimate=pl.CostEstimate(flops=COST, bytes_accessed=COST, transcendentals=0),
        name="grid",
    )(weights, target, spec_score, *parts, signs)


def local(ens, truth, legendre, orders):
    own_count, var_count, band_rows, lon_count = ens.shape
    order_count = orders.shape[0]
    deg_count = legendre.shape[2]
    space_count = lax.axis_size("space")
    member_count = lax.axis_size("member")
    lat_count = band_rows * space_count
    ens_count = own_count * member_count
    sub_rows = band_rows // member_count
    fairness = 1.0 - FAIR_GAP / ens_count

    owners = ("space", "member")
    sent, table = forward(ens, truth, legendre, orders, member_count)
    received = lax.all_to_all(sent, owners, split_axis=0, concat_axis=0, tiled=True)

    *parts, target = regroup(ens, truth, member_count)
    for place, hop in enumerate(HOPS):
        if place:
            parts[place] = lax.ppermute(parts[place], "member", hop_pairs(hop, member_count))

    received, parts[1] = lax.optimization_barrier((received, parts[1]))
    grads, score = spectral(received, orders, fairness, member_count, var_count, deg_count)
    signs = count_signs(parts[:EARLY_PARTS])
    spec_score = lax.all_to_all(score, "member", split_axis=0, concat_axis=0, tiled=True)
    grads, spec_score, signs, *parts = lax.optimization_barrier(
        (grads, spec_score, signs, *parts)
    )
    returned = lax.all_to_all(grads, owners, split_axis=0, concat_axis=0, tiled=True)
    weights = jnp.asarray(latitude_weights(lat_count))
    grid_grad, grid_rows, spec_score = grid_scores(
        parts, signs, target, weights, spec_score, fairness, sub_rows
    )
    spec_score = spec_score.swapaxes(0, 1)
    grid_grad = grid_grad.reshape(ens_count, var_count, 1, sub_rows, lon_count)
    grid_score = grid_rows.T.reshape(var_count, 1, sub_rows)
    spec_grad = backward(returned, table, own_count, var_count).reshape(ens.shape)
    return (grid_score, grid_grad, spec_score, spec_grad)


def solution(mesh):
    in_specs = (
        P("member", None, "space", None),
        P(None, "space", None),
        P("space", None, None),
        P(),
    )
    out_specs = (
        P(None, "space", "member"),
        P(None, None, "space", "member", None),
        P("space", None, None),
        P("member", None, "space", None),
    )
    return jax.shard_map(local, mesh=mesh, in_specs=in_specs, out_specs=out_specs, check_vma=False)
```
